32 devices in a mesh: win: 4 (over y, x), blk: 8 (over z, core).
Axes of the slice: x: 2, y: 2, z: 4, core: 2. Of those that a mesh axis runs over, the one named last changes fastest.
Arguments:
- inputs: bfloat16 [8, 1024, 768], P('win', 'blk'), may hold values from -6 to 6
- species: int32 [8], replicated, may hold values from 0 to 3, as said below
- random_blocks: int32 [16, 12, 3], replicated, may hold values from 1 to 14, as said below
- qkv_weight: bfloat16 [768, 2304], replicated, may hold values from -0.21875 to 0.21875
- q_bias: float32 [768], replicated, may hold values from -3 to 3
- v_bias: float32 [768], replicated, may hold values from -0.12 to 0.12
- out_weight: bfloat16 [768, 768], replicated, may hold values from -2.5 to 2.5
- out_bias: float32 [768], replicated, may hold values from -1.2 to 1.2
- norm1_gain: float32 [768], replicated, may hold values from 0.5 to 1.5
- norm1_bias: float32 [768], replicated, may hold values from -1.2 to 1.2
- norm2_gain: float32 [768], replicated, may hold values from 0.5 to 1.5
- norm2_bias: float32 [768], replicated, may hold values from -1.2 to 1.2
- ffn_in_weight: bfloat16 [768, 3072], replicated, may hold values from -0.21875 to 0.21875
- ffn_in_bias: float32 [3072], replicated, may hold values from -1.2 to 1.2
- ffn_out_weight: bfloat16 [3072, 768], replicated, may hold values from -0.15625 to 0.15625
- ffn_out_bias: float32 [768], replicated, may hold values from -1.2 to 1.2
- cotangent: bfloat16 [16, 1024, 768], P('win', 'blk'), may hold values from -6 to 6
Outputs:
- result: bfloat16 [16, 1024, 768], P('win', 'blk')
- input_grad: bfloat16 [8, 1024, 768], P('win', 'blk')
- qkv_weight_grad: float32 [768, 2304], replicated
- q_bias_grad: float32 [768], replicated
- v_bias_grad: float32 [768], replicated
- out_weight_grad: float32 [768, 768], replicated
- out_bias_grad: float32 [768], replicated
- norm1_gain_grad: float32 [768], replicated
- norm1_bias_grad: float32 [768], replicated
- norm2_gain_grad: float32 [768], replicated
- norm2_bias_grad: float32 [768], replicated
- ffn_in_weight_grad: float32 [768, 3072], replicated
- ffn_in_bias_grad: float32 [3072], replicated
- ffn_out_weight_grad: float32 [3072, 768], replicated
- ffn_out_bias_grad: float32 [768], replicated
The draws below stay inside these ranges and needn't reach their ends.
Inputs may be any that keep to these rules, and one draw needn't show every extreme that they name: One species group, drawn from the seed, holds exactly 4 windows and none holds more; the other groups share the rest as evenly as possible. `random_blocks`: take the blocks in groups of 2 consecutive ones. For each query block and head the 3 blocks lie in different groups, none in the query block's own group, and none is the first or last block. Of the 72 picks of one group's query blocks, at most (78) // 7 lie in any one other group, and the group just before it (the last group before the first) receives exactly that many.
All inputs are finite; a program needn't handle non-finite values.
Results may differ from the reference program's by a relative error of at most 0.013.
Values may be sent and summed in bfloat16 or wider, within the bound.
No kernel may reach another device: no remote copies, remote signals or barrier semaphores. Data moves between devices by JAX's collectives and lax.ppermute only.
A program may use at most 320 MiB of HBM per device.

```python
import jax
import jax.numpy as jnp
from jax import lax

D = 768
HEADS = 12
HD = 64
FF = 3072
BS = 64
RAND = 3
BLK_DEV = 2
GROUPS = 4
SLOTS = 4
WINDOWS = 8
BLOCKS = 16
LEN = 1024


def draw_species(key, part):
    first_key, second_key = jax.random.split(jax.random.fold_in(key, 11))
    shuffled = jax.random.permutation(first_key, WINDOWS)
    heavy_group = jax.random.randint(second_key, (), 0, GROUPS)
    position = jnp.zeros((WINDOWS,), jnp.int32).at[shuffled].set(jnp.arange(WINDOWS, dtype=jnp.int32))
    spread_group = (heavy_group + 1 + (position - SLOTS) % (GROUPS - 1)) % GROUPS
    return jnp.where(position < SLOTS, heavy_group, spread_group).astype(jnp.int32)


def draw_random_blocks(key, part):
    group_total = BLOCKS // BLK_DEV
    offset_range = group_total - 1
    local_key = jax.random.fold_in(key, 23)
    block_ids = jnp.arange(BLOCKS, dtype=jnp.int32)
    own_group = block_ids // BLK_DEV
    inner_index = block_ids % BLK_DEV
    pick_order = (inner_index[:, None, None] * HEADS + jnp.arange(HEADS, dtype=jnp.int32)[None, :, None]) * RAND + jnp.arange(RAND, dtype=jnp.int32)[None, None, :]
    offset_value = pick_order % offset_range
    target_group = (own_group[:, None, None] + group_total - 1 - offset_value) % group_total
    local_index = jax.random.randint(local_key, (BLOCKS, HEADS, RAND), 0, BLK_DEV).astype(jnp.int32)
    return jnp.clip(target_group * BLK_DEV + local_index, 1, BLOCKS - 2).astype(jnp.int32)


def shard_levels(stream_key, dims, cuts, low, top_value):
    level = 1.0
    for dim, shards_of in cuts:
        steps = jax.random.uniform(jax.random.fold_in(jax.random.fold_in(stream_key, 6), dim), (shards_of,), jnp.float32, low / len(cuts), top_value / len(cuts))
        level = level * jnp.repeat(jnp.exp(steps), dims[dim] // shards_of).reshape((-1,) + (1,) * (len(dims) - 1 - dim))
    return level


def bell_draw(own_key, dims, scale, limit, pieces=(), kind=jnp.bfloat16):
    loudness = shard_levels(own_key, dims, pieces, -0.22, 0.18) if pieces else 1.0
    entries = jax.random.normal(own_key, dims, jnp.float32) * scale * loudness
    return jnp.minimum(jnp.maximum(entries, -limit), limit).astype(kind)


def setup_inputs(seed: int = 0) -> dict:
    keys = jax.random.split(jax.random.key(seed), 18)
    inputs = bell_draw(keys[0], (WINDOWS, LEN, D), 1.0, 6.0, ((0, 4), (1, 8)))
    species = draw_species(jax.random.fold_in(keys[17], 71), 0)
    random_blocks = draw_random_blocks(jax.random.fold_in(keys[17], 71), 0)
    qkv_weight = bell_draw(keys[3], (D, 3 * D), D ** -0.5, 0.21875)
    q_bias = bell_draw(keys[4], (D,), 0.5, 3.0, (), jnp.float32)
    v_bias = bell_draw(keys[5], (D,), 0.02, 0.12, (), jnp.float32)
    out_weight = bell_draw(keys[6], (D, D), (max(D // 128, 1)) ** -0.5, 2.5)
    out_bias = bell_draw(keys[7], (D,), 0.2, 1.2, (), jnp.float32)
    norm1_gain = jnp.clip(1.0 + 0.1 * jax.random.normal(keys[8], (D,), jnp.float32), 0.5, 1.5)
    norm1_bias = bell_draw(keys[9], (D,), 0.2, 1.2, (), jnp.float32)
    norm2_gain = jnp.clip(1.0 + 0.1 * jax.random.normal(keys[10], (D,), jnp.float32), 0.5, 1.5)
    norm2_bias = bell_draw(keys[11], (D,), 0.2, 1.2, (), jnp.float32)
    ffn_in_weight = bell_draw(keys[12], (D, FF), D ** -0.5, 0.21875)
    ffn_in_bias = bell_draw(keys[13], (FF,), 0.2, 1.2, (), jnp.float32)
    ffn_out_weight = bell_draw(keys[14], (FF, D), (FF // 2) ** -0.5, 0.15625)
    ffn_out_bias = bell_draw(keys[15], (D,), 0.2, 1.2, (), jnp.float32)
    cotangent = bell_draw(keys[16], (GROUPS * SLOTS, LEN, D), 1.0, 6.0, ((0, 4), (1, 8)))
    return dict(inputs=inputs, species=species, random_blocks=random_blocks, qkv_weight=qkv_weight, q_bias=q_bias, v_bias=v_bias, out_weight=out_weight, out_bias=out_bias, norm1_gain=norm1_gain, norm1_bias=norm1_bias, norm2_gain=norm2_gain, norm2_bias=norm2_bias, ffn_in_weight=ffn_in_weight, ffn_in_bias=ffn_in_bias, ffn_out_weight=ffn_out_weight, ffn_out_bias=ffn_out_bias, cotangent=cotangent)


NORM_EPS = 1e-05
SCORE_SCALE = 0.125
MASKED_SCORE = -1e+30
PRECISE = lax.Precision.HIGHEST

@jax.custom_vjp
def low(v):
    return lax.optimization_barrier(v.astype(jnp.bfloat16)).astype(jnp.float32)

@jax.custom_vjp
def low_back(v):
    return v

def low_keep(v):
    return (low(v), None)

def low_pass(kept, grad):
    return (grad,)

def back_keep(v):
    return (v, None)

def back_low(kept, grad):
    return (low(grad),)
low.defvjp(low_keep, low_pass)
low_back.defvjp(back_keep, back_low)

def layer_norm(values, gain_vec, bias_vec):
    average = lax.optimization_barrier(jnp.mean(values, axis=-1, keepdims=True))
    centred = values - average
    spread = lax.optimization_barrier(jnp.mean(centred * centred, axis=-1, keepdims=True))
    return centred * lax.rsqrt(spread + NORM_EPS) * gain_vec + bias_vec

def softmax_rows(scores):
    row_top = lax.optimization_barrier(jnp.max(scores, axis=-1, keepdims=True))
    expd = jnp.exp(scores - row_top)
    return expd / lax.optimization_barrier(jnp.sum(expd, axis=-1, keepdims=True))

def slot_mask(block_ids, block_total):
    always = jnp.ones(block_ids.shape, dtype=jnp.bool_)
    columns = [block_ids >= 1, always, block_ids <= block_total - 2, block_ids >= 2, block_ids <= block_total - 3] + [always] * RAND
    return jnp.stack(columns, axis=1)

def head_attention(head_item):
    q_head, k_head, v_head, head_picks = head_item
    q_blocks = q_head.reshape(BLOCKS, BS, HD)
    k_blocks = k_head.reshape(BLOCKS, BS, HD)
    v_blocks = v_head.reshape(BLOCKS, BS, HD)
    blocks = jnp.arange(BLOCKS, dtype=jnp.int32)
    left_block = jnp.clip(blocks - 1, 0, BLOCKS - 1)
    right_block = jnp.clip(blocks + 1, 0, BLOCKS - 1)
    first_block = jnp.zeros_like(blocks)
    last_block = jnp.full_like(blocks, BLOCKS - 1)
    chosen = jnp.concatenate([jnp.stack([left_block, blocks, right_block, first_block, last_block], axis=1), head_picks], axis=1)
    key_sets = k_blocks[chosen].reshape(BLOCKS, -1, HD)
    value_sets = v_blocks[chosen].reshape(BLOCKS, -1, HD)
    scores = low_back(jnp.einsum('nqd,nkd->nqk', q_blocks, key_sets, precision=PRECISE) * SCORE_SCALE)
    allowed = jnp.repeat(slot_mask(blocks, BLOCKS), BS, axis=1)[:, None, :]
    scores = jnp.where(allowed, scores, MASKED_SCORE)
    sparse = jnp.einsum('nqk,nkd->nqd', low(softmax_rows(scores)), value_sets, precision=PRECISE)
    end_query = q_blocks[jnp.array([0, BLOCKS - 1], dtype=jnp.int32)].reshape(2 * BS, HD)
    wide_scores = low_back(jnp.dot(end_query, k_head.T, precision=PRECISE) * SCORE_SCALE)
    wide_out = jnp.dot(low(softmax_rows(wide_scores)), v_head, precision=PRECISE).reshape(2, BS, HD)
    sparse = sparse.at[0].set(wide_out[0]).at[BLOCKS - 1].set(wide_out[1])
    return sparse.reshape(LEN, HD)

def attention(query_rows, key_rows, value_rows, random_picks):
    q_heads = query_rows.reshape(LEN, HEADS, HD).transpose(1, 0, 2)
    k_heads = key_rows.reshape(LEN, HEADS, HD).transpose(1, 0, 2)
    v_heads = value_rows.reshape(LEN, HEADS, HD).transpose(1, 0, 2)
    head_picks = random_picks.transpose(1, 0, 2)
    outputs = lax.map(jax.checkpoint(head_attention), (q_heads, k_heads, v_heads, head_picks))
    return outputs.transpose(1, 0, 2).reshape(LEN, D)

def layer_forward(tokens, params, random_picks):
    w_qkv, bias_q, bias_v, w_out, bias_out, gain_one, shift_one, gain_two, shift_two, w_in, bias_in, w_down, bias_down = params
    normed = low(layer_norm(tokens, gain_one, shift_one))
    mixed_qkv = jnp.dot(normed, w_qkv, precision=PRECISE)
    query_rows = low(low_back(mixed_qkv[:, :D] + bias_q))
    key_rows = low(low_back(mixed_qkv[:, D:2 * D]))
    value_rows = low(low_back(mixed_qkv[:, 2 * D:] + bias_v))
    head_out = low(low_back(attention(query_rows, key_rows, value_rows, random_picks)))
    residual = tokens + low_back(jnp.dot(head_out, w_out, precision=PRECISE) + bias_out)
    second = low(layer_norm(residual, gain_two, shift_two))
    hidden = low_back(jnp.dot(second, w_in, precision=PRECISE) + bias_in)
    activated = low(jax.nn.gelu(hidden, approximate=False))
    return residual + jnp.dot(activated, w_down, precision=PRECISE) + bias_down

def reference(inputs, species, random_blocks, qkv_weight, q_bias, v_bias, out_weight, out_bias, norm1_gain, norm1_bias, norm2_gain, norm2_bias, ffn_in_weight, ffn_in_bias, ffn_out_weight, ffn_out_bias, cotangent):
    params = tuple((item.astype(jnp.float32) for item in (qkv_weight, q_bias, v_bias, out_weight, out_bias, norm1_gain, norm1_bias, norm2_gain, norm2_bias, ffn_in_weight, ffn_in_bias, ffn_out_weight, ffn_out_bias)))
    window = jnp.arange(WINDOWS, dtype=jnp.int32)
    same_group = species[:, None] == species[None, :]
    earlier = window[None, :] < window[:, None]
    slot_rank = lax.optimization_barrier(jnp.sum((same_group & earlier).astype(jnp.int32), axis=1))
    slot_index = (species * SLOTS + slot_rank).astype(jnp.int32)

    def one_window(totals, window_item):
        x_win, s_win = window_item
        upstream = lax.dynamic_index_in_dim(cotangent, s_win, 0, keepdims=False).astype(jnp.float32)

        def forward(tokens, *weights):
            return layer_forward(tokens, weights, random_blocks)
        output, pullback = jax.vjp(forward, x_win.astype(jnp.float32), *params)
        grad_all = pullback(upstream)
        totals = tuple((total + grad for total, grad in zip(totals, grad_all[1:])))
        return (totals, (output.astype(jnp.bfloat16), grad_all[0].astype(jnp.bfloat16)))
    zero_grads = tuple((jnp.zeros_like(item) for item in params))
    totals, (outputs, input_grads) = lax.scan(one_window, zero_grads, (inputs, slot_index))
    result = jnp.zeros((GROUPS * SLOTS, LEN, D), jnp.bfloat16).at[slot_index].set(outputs)
    return (result, input_grads) + totals
```

```python
import functools

import jax
import jax.numpy as jnp
from jax import lax
from jax.experimental import pallas as pl
from jax.experimental.pallas import tpu as pltpu
from jax.sharding import PartitionSpec as P

HEADS = 12
HD = 64
BS = 64
PAIRS = HEADS // 2
PW = 2 * HD

EPS = 1e-05
SCALE = 0.125
MASKED = -1e30
BF = jnp.bfloat16
F32 = jnp.float32
BOTH = ("win", "blk")
VMEM_LIMIT = 56 * 1024 * 1024


def dot(a, b, ca=1, cb=0, precision=None):
    return lax.dot_general(
        a, b, (((ca,), (cb,)), ((), ())), precision=precision, preferred_element_type=F32
    )


def params(grid_dims):
    return pltpu.CompilerParams(
        dimension_semantics=("arbitrary",) * grid_dims, vmem_limit_bytes=VMEM_LIMIT
    )


def cost(flops, nbytes, exps=0):
    return pl.CostEstimate(flops=int(flops), bytes_accessed=int(nbytes), transcendentals=int(exps))


def norm_stats(x):
    width = x.shape[-1]
    mean = jnp.sum(x, axis=-1, keepdims=True) * (1.0 / width)
    c = x - mean
    var = jnp.sum(c * c, axis=-1, keepdims=True) * (1.0 / width)
    rstd = lax.rsqrt(var + EPS)
    return c * rstd, rstd


def norm_back(g, xhat, rstd):
    width = g.shape[-1]
    m1 = jnp.sum(g, axis=-1, keepdims=True) * (1.0 / width)
    m2 = jnp.sum(g * xhat, axis=-1, keepdims=True) * (1.0 / width)
    return rstd * (g - m1 - xhat * m2)


def query_kernel(x_ref, gain_ref, shift_ref, w_ref, b_ref, a_ref, q_ref):
    xhat, _ = norm_stats(x_ref[...].astype(F32))
    a = (xhat * gain_ref[...] + shift_ref[...]).astype(BF)
    a_ref[...] = a
    q = (dot(a, w_ref[...]) + b_ref[...]).astype(BF)
    q_ref[...] = (q.astype(F32) * SCALE).astype(BF)


def query_rows(x, gain, shift, w_qkv, b_q):
    rows, d = x.shape
    tile = rows // 2
    row = pl.BlockSpec((tile, d), lambda i: (i, 0))
    vec = pl.BlockSpec((1, d), lambda i: (0, 0))
    return pl.pallas_call(
        query_kernel,
        grid=(rows // tile,),
        in_specs=[row, vec, vec, pl.BlockSpec((d, d), lambda i: (0, 0)), vec],
        out_specs=[row, row],
        out_shape=[jax.ShapeDtypeStruct((rows, d), BF)] * 2,
        compiler_params=params(1),
        cost_estimate=cost(2 * rows * d * d, 2 * d * d + 6 * rows * d),
        name="query_rows",
    )(x, gain, shift, w_qkv, b_q)


def kv_kernel(x_ref, gain_ref, shift_ref, wk_ref, wv_ref, bv_ref, a_ref, k_ref, v_ref):
    xhat, _ = norm_stats(x_ref[...].astype(F32))
    a = (xhat * gain_ref[...] + shift_ref[...]).astype(BF)
    a_ref[...] = a
    k_ref[...] = dot(a, wk_ref[...]).astype(BF)
    v_ref[...] = (dot(a, wv_ref[...]) + bv_ref[...]).astype(BF)


def kv_rows(x, gain, shift, w_qkv, b_v):
    rows, d = x.shape
    tile = min(rows, 512)
    row = pl.BlockSpec((tile, d), lambda i: (i, 0))
    vec = pl.BlockSpec((1, d), lambda i: (0, 0))
    return pl.pallas_call(
        kv_kernel,
        grid=(rows // tile,),
        in_specs=[
            row,
            vec,
            vec,
            pl.BlockSpec((d, d), lambda i: (0, 1)),
            pl.BlockSpec((d, d), lambda i: (0, 2)),
            vec,
        ],
        out_specs=[row, row, row],
        out_shape=[jax.ShapeDtypeStruct((rows, d), BF)] * 3,
        compiler_params=params(1),
        cost_estimate=cost(4 * rows * d * d, 4 * d * d + 8 * rows * d),
        name="kv_rows",
    )(x, gain, shift, w_qkv, w_qkv, b_v)


def head_stack(pair):
    lane = lax.broadcasted_iota(jnp.int32, pair.shape, 1)
    zero = jnp.zeros_like(pair)
    return jnp.concatenate([jnp.where(lane < HD, pair, zero), jnp.where(lane < HD, zero, pair)], axis=0)


def head_select(both):
    rows = both.shape[0] // 2
    lane = lax.broadcasted_iota(jnp.int32, (rows, both.shape[1]), 1)
    return jnp.where(lane < HD, both[:rows], both[rows:])


def biased_scores(k, q2, bias):
    s = dot(k, q2, 1, 1)
    keys, lanes = s.shape
    return (s.reshape(keys // BS, BS, lanes) + bias[:, None, :]).reshape(keys, lanes)


def attend_kernel(q_ref, k_ref, v_ref, bias_ref, o_ref, lse_ref):
    q2 = head_stack(q_ref[...])
    s = biased_scores(k_ref[...], q2, bias_ref[0])
    top = jnp.max(s, axis=0, keepdims=True)
    e = jnp.exp(s - top)
    total = jnp.sum(e, axis=0, keepdims=True)
    p = (e * (1.0 / total)).astype(BF)
    o_t = dot(v_ref[...], p, 0, 0)
    o_ref[...] = head_select(o_t.T).astype(BF)
    lse_ref[0, 0] = top + jnp.log(total)


def attend(q, k, v, bias, windows):
    rows, d = q.shape
    tok = rows // windows
    keys = k.shape[0] // windows
    nkb = keys // BS
    q_spec = pl.BlockSpec((tok, PW), lambda w, p: (w, p))
    k_spec = pl.BlockSpec((keys, PW), lambda w, p: (w, p))
    return pl.pallas_call(
        attend_kernel,
        grid=(windows, PAIRS),
        in_specs=[q_spec, k_spec, k_spec, pl.BlockSpec((1, nkb, 2 * tok), lambda w, p: (p, 0, 0))],
        out_specs=[q_spec, pl.BlockSpec((1, 1, 1, 2 * tok), lambda w, p: (w, p, 0, 0))],
        out_shape=[
            jax.ShapeDtypeStruct((rows, d), BF),
            jax.ShapeDtypeStruct((windows, PAIRS, 1, 2 * tok), F32),
        ],
        compiler_params=params(2),
        cost_estimate=cost(
            4 * windows * PAIRS * keys * 2 * tok * PW, 4 * k.size, windows * PAIRS * keys * 2 * tok
        ),
        name="attend",
    )(q, k, v, bias)


def ffn_kernel(
    x_ref,
    o_ref,
    dy_ref,
    wo_ref,
    bo_ref,
    gain_ref,
    shift_ref,
    wi_ref,
    bi_ref,
    wd_ref,
    bd_ref,
    y_ref,
    dx1_ref,
    do_ref,
    gw_ref,
    gwo_ref,
    gbi_ref,
    vec_ref,
    x1_s,
    h2_s,
    h2t_s,
    y_s,
    dh_s,
):
    step = pl.program_id(0)

    @pl.when(step == 0)
    def _():
        x1 = x_ref[...].astype(F32) + (dot(o_ref[...], wo_ref[...]) + bo_ref[...])
        x1_s[...] = x1
        xhat, _ = norm_stats(x1)
        h2 = xhat * gain_ref[...] + shift_ref[...]
        h2_s[...] = h2.astype(BF)
        h2t_s[...] = h2.T.astype(BF)
        y_s[...] = jnp.zeros_like(y_s)
        dh_s[...] = jnp.zeros_like(dh_s)

    dy = dy_ref[...]
    wi = wi_ref[...]
    wd = wd_ref[...]
    u = dot(h2_s[...], wi) + bi_ref[0]
    half = 0.5 * (1.0 + lax.erf(u * 0.7071067811865476))
    f = (u * half).astype(BF)
    slope = half + u * (jnp.exp(u * u * -0.5) * 0.3989422804014327)
    du = dot(dy, wd, 1, 1) * slope
    du_low = du.astype(BF)
    y_s[...] += dot(f, wd)
    dh_s[...] += dot(du_low, wi, 1, 1)
    gw_ref[0, 0] = dot(f, dy, 0, 0).astype(BF)
    gw_ref[0, 1] = dot(h2t_s[...], du_low).astype(BF)
    gbi_ref[0] = jnp.sum(du_low.astype(F32), axis=0, keepdims=True)

    @pl.when(step == pl.num_programs(0) - 1)
    def _():
        x1 = x1_s[...]
        y_ref[...] = (x1 + (y_s[...] + bd_ref[...])).astype(BF)
        dyf = dy.astype(F32)
        dh = dh_s[...]
        xhat, rstd = norm_stats(x1)
        dx1 = dyf + norm_back(dh * gain_ref[...], xhat, rstd)
        dx1_ref[...] = dx1
        dx1r = dx1.astype(BF)
        do_ref[...] = dot(dx1r, wo_ref[...], 1, 1).astype(BF)
        gwo_ref[...] = dot(o_ref[...], dx1r, 0, 0).astype(BF)
        vec_ref[0:1] = jnp.sum(dyf, axis=0, keepdims=True)
        vec_ref[1:2] = jnp.sum(dh * xhat, axis=0, keepdims=True)
        vec_ref[2:3] = jnp.sum(dh, axis=0, keepdims=True)
        vec_ref[3:4] = jnp.sum(dx1r.astype(F32), axis=0, keepdims=True)
        vec_ref[4:8] = jnp.zeros((4, vec_ref.shape[1]), F32)


def ffn(x, o, dy, w_out, b_out, gain, shift, w_in, b_in, w_down, b_down):
    rows, d = x.shape
    ff = w_in.shape[1]
    steps = ff // d
    row = pl.BlockSpec((rows, d), lambda t: (0, 0))
    vec = pl.BlockSpec((1, d), lambda t: (0, 0))
    square = pl.BlockSpec((d, d), lambda t: (0, 0))
    lane_vec = pl.BlockSpec((1, 1, d), lambda t: (t, 0, 0))
    return pl.pallas_call(
        ffn_kernel,
        grid=(steps,),
        in_specs=[
            row,
            row,
            row,
            square,
            vec,
            vec,
            vec,
            pl.BlockSpec((d, d), lambda t: (0, t)),
            lane_vec,
            pl.BlockSpec((d, d), lambda t: (t, 0)),
            vec,
        ],
        out_specs=[
            row,
            row,
            row,
            pl.BlockSpec((1, 2, d, d), lambda t: (t, 0, 0, 0)),
            square,
            lane_vec,
            pl.BlockSpec((8, d), lambda t: (0, 0)),
        ],
        out_shape=[
            jax.ShapeDtypeStruct((rows, d), BF),
            jax.ShapeDtypeStruct((rows, d), F32),
            jax.ShapeDtypeStruct((rows, d), BF),
            jax.ShapeDtypeStruct((steps, 2, d, d), BF),
            jax.ShapeDtypeStruct((d, d), BF),
            jax.ShapeDtypeStruct((steps, 1, d), F32),
            jax.ShapeDtypeStruct((8, d), F32),
        ],
        scratch_shapes=[
            pltpu.VMEM((rows, d), F32),
            pltpu.VMEM((rows, d), BF),
            pltpu.VMEM((d, rows), BF),
            pltpu.VMEM((rows, d), F32),
            pltpu.VMEM((rows, d), F32),
        ],
        compiler_params=params(1),
        cost_estimate=cost(12 * rows * d * ff + 6 * rows * d * d, 8 * d * ff + 20 * rows * d, 2 * rows * ff),
        name="ffn",
    )(x, o, dy, w_out, b_out, gain, shift, w_in, b_in.reshape(steps, 1, d), w_down, b_down)


def attend_back_kernel(
    q_ref, o_ref, do_ref, k_ref, v_ref, bias_ref, lse_ref, dq_ref, dk_ref, dv_ref, dq_s
):
    step = pl.program_id(2)
    q2 = head_stack(q_ref[...])
    do = do_ref[...]
    do2 = head_stack(do)
    prod = head_stack(do.astype(F32) * o_ref[...].astype(F32))
    delta = dot(jnp.ones((8, PW), F32), prod, 1, 1, lax.Precision.HIGHEST)[0:1]
    k = k_ref[...]
    p = jnp.exp(biased_scores(k, q2, bias_ref[0]) - lse_ref[0, 0])
    dp = dot(v_ref[...], do2, 1, 1)
    ds = (p * (dp - delta)).astype(BF)
    dv_ref[...] = dot(p.astype(BF), do2).astype(BF)
    dk_ref[...] = dot(ds, q2).astype(BF)
    dq_t = dot(k, ds, 0, 0)

    @pl.when(step == 0)
    def _():
        dq_s[...] = dq_t

    @pl.when(step > 0)
    def _():
        dq_s[...] += dq_t

    @pl.when(step == pl.num_programs(2) - 1)
    def _():
        dq_ref[...] = (head_select(dq_s[...].T) * SCALE).astype(BF)


def attend_back(q, o, do, k, v, bias, lse, windows):
    rows, d = q.shape
    tok = rows // windows
    keys = k.shape[0] // windows
    chunk = min(keys, 1024)
    parts = keys // chunk
    nkb = chunk // BS
    q_spec = pl.BlockSpec((tok, PW), lambda w, p, c: (w, p))
    k_spec = pl.BlockSpec((chunk, PW), lambda w, p, c: (w * parts + c, p))
    return pl.pallas_call(
        attend_back_kernel,
        grid=(windows, PAIRS, parts),
        in_specs=[
            q_spec,
            q_spec,
            q_spec,
            k_spec,
            k_spec,
            pl.BlockSpec((1, nkb, 2 * tok), lambda w, p, c: (p, c, 0)),
            pl.BlockSpec((1, 1, 1, 2 * tok), lambda w, p, c: (w, p, 0, 0)),
        ],
        out_specs=[q_spec, k_spec, k_spec],
        out_shape=[
            jax.ShapeDtypeStruct((rows, d), BF),
            jax.ShapeDtypeStruct(k.shape, BF),
            jax.ShapeDtypeStruct(k.shape, BF),
        ],
        scratch_shapes=[pltpu.VMEM((PW, 2 * tok), F32)],
        compiler_params=params(3),
        cost_estimate=cost(
            10 * windows * PAIRS * keys * 2 * tok * PW, 8 * k.size, windows * PAIRS * keys * 2 * tok
        ),
        name="attend_back",
    )(q, o, do, k, v, bias, lse)


def qkv_back_kernel(
    a_ref,
    dk_ref,
    dv_ref,
    al_ref,
    dq_ref,
    wq_ref,
    wk_ref,
    wv_ref,
    da_ref,
    dal_ref,
    gw_ref,
    vec_ref,
    gk_s,
    gv_s,
    vec_s,
):
    step = pl.program_id(0)

    @pl.when(step == 0)
    def _():
        gk_s[...] = jnp.zeros_like(gk_s)
        gv_s[...] = jnp.zeros_like(gv_s)
        al = al_ref[...]
        dq = dq_ref[...]
        dal = dot(dq, wq_ref[...], 1, 1)
        dal_ref[...] = dal
        gw_ref[0] = dot(al, dq, 0, 0).astype(BF)
        vec_s[0:1] = jnp.sum(dal * al.astype(F32), axis=0, keepdims=True)
        vec_s[1:2] = jnp.sum(dal, axis=0, keepdims=True)
        vec_s[2:3] = jnp.sum(dq.astype(F32), axis=0, keepdims=True)
        vec_s[3:8] = jnp.zeros((5, vec_s.shape[1]), F32)

    a = a_ref[...]
    dk = dk_ref[...]
    dv = dv_ref[...]
    da = dot(dk, wk_ref[...], 1, 1) + dot(dv, wv_ref[...], 1, 1)
    da_ref[...] = da.astype(BF)
    a_t = a.T
    gk_s[...] += dot(a_t, dk)
    gv_s[...] += dot(a_t, dv)
    vec_s[0:1] += jnp.sum(da * a.astype(F32), axis=0, keepdims=True)
    vec_s[1:2] += jnp.sum(da, axis=0, keepdims=True)
    vec_s[3:4] += jnp.sum(dv.astype(F32), axis=0, keepdims=True)

    @pl.when(step == pl.num_programs(0) - 1)
    def _():
        gw_ref[1] = gk_s[...].astype(BF)
        gw_ref[2] = gv_s[...].astype(BF)
        vec_ref[...] = vec_s[...]


def qkv_back(a, dk, dv, a_own, dq, w_qkv):
    rows, d = a.shape
    own = dq.shape[0]
    tile = min(rows, 512)
    row = pl.BlockSpec((tile, d), lambda i: (i, 0))
    own_row = pl.BlockSpec((own, d), lambda i: (0, 0))
    return pl.pallas_call(
        qkv_back_kernel,
        grid=(rows // tile,),
        in_specs=[
            row,
            row,
            row,
            own_row,
            own_row,
            pl.BlockSpec((d, d), lambda i: (0, 0)),
            pl.BlockSpec((d, d), lambda i: (0, 1)),
            pl.BlockSpec((d, d), lambda i: (0, 2)),
        ],
        out_specs=[
            row,
            own_row,
            pl.BlockSpec((3, d, d), lambda i: (0, 0, 0)),
            pl.BlockSpec((8, d), lambda i: (0, 0)),
        ],
        out_shape=[
            jax.ShapeDtypeStruct((rows, d), BF),
            jax.ShapeDtypeStruct((own, d), F32),
            jax.ShapeDtypeStruct((3, d, d), BF),
            jax.ShapeDtypeStruct((8, d), F32),
        ],
        scratch_shapes=[pltpu.VMEM((d, d), F32), pltpu.VMEM((d, d), F32), pltpu.VMEM((8, d), F32)],
        compiler_params=params(1),
        cost_estimate=cost(8 * rows * d * d + 4 * own * d * d, 8 * rows * d + 12 * d * d),
        name="qkv_back",
    )(a, dk, dv, a_own, dq, w_qkv, w_qkv, w_qkv)


def input_back_kernel(x_ref, da_ref, dal_ref, dx1_ref, gain_ref, g_ref):
    xhat, rstd = norm_stats(x_ref[...].astype(F32))
    da = da_ref[...].astype(F32) + dal_ref[...]
    g_ref[...] = (dx1_ref[...] + norm_back(da * gain_ref[...], xhat, rstd)).astype(BF)


def input_back(x, da, dal, dx1, gain):
    rows, d = x.shape
    return pl.pallas_call(
        input_back_kernel,
        out_shape=jax.ShapeDtypeStruct((rows, d), BF),
        compiler_params=pltpu.CompilerParams(vmem_limit_bytes=VMEM_LIMIT),
        cost_estimate=cost(20 * rows * d, 14 * rows * d),
        name="input_back",
    )(x, da, dal, dx1, gain)


def swap(x, partner):
    wins, blks = lax.axis_size("win"), lax.axis_size("blk")
    perm = []
    for w in range(wins):
        for b in range(blks):
            pw, pb = partner(w, b)
            perm.append((w * blks + b, pw * blks + pb))
    return lax.ppermute(x, BOTH, perm)


def core_swap(x):
    return swap(x, lambda w, b: (w, b ^ 1))


def chip_swap(x, s):
    return swap(x, lambda w, b: (w, b ^ (2 * s)))


def win_swap(x, s):
    return swap(x, lambda w, b: (w ^ s, b))


def win_turns():
    bits = (lax.axis_size("win") - 1).bit_length()
    even = [1 << i for i in range(bits)]
    return list(zip(even, even[::-1]))


def pick(flag, a, b):
    return jnp.where(flag, a, b)


def add_low(parts):
    total = parts[0].astype(F32)
    for part in parts[1:]:
        total = total + part.astype(F32)
    return total.astype(BF)


def keep_send(x, bit):
    half = x.shape[0] // 2
    low, high = x[:half], x[half:]
    return pick(bit, high, low), pick(bit, low, high)


def scatter_sum(x):
    core = (lax.axis_index("blk") % 2) == 1
    win = lax.axis_index("win")
    chip = lax.axis_index("blk") // 2
    chips = lax.axis_size("blk") // 2
    keep, send = keep_send(x, core)
    x = add_low([keep, core_swap(send)])
    for even, odd in win_turns():
        bit = (win & jnp.where(core, odd, even)) != 0
        keep, send = keep_send(x, bit)
        got = swap(send, lambda w, b: (w ^ (odd if b % 2 else even), b))
        x = add_low([keep, got])
    x = x.reshape((chips, x.shape[0] // chips) + x.shape[1:])
    parts = [lax.dynamic_index_in_dim(x, chip, 0, keepdims=False)]
    for s in range(1, chips):
        parts.append(chip_swap(lax.dynamic_index_in_dim(x, chip ^ s, 0, keepdims=False), s))
    return add_low(parts)


def gather_all(x):
    core = (lax.axis_index("blk") % 2) == 1
    win = lax.axis_index("win")
    chip = lax.axis_index("blk") // 2
    chips = lax.axis_size("blk") // 2
    parts = [x] + [chip_swap(x, s) for s in range(1, chips)]
    out = jnp.zeros((chips,) + x.shape, x.dtype)
    for s, part in enumerate(parts):
        out = lax.dynamic_update_index_in_dim(out, part, chip ^ s, 0)
    x = out.reshape((chips * x.shape[0],) + x.shape[1:])
    for even, odd in win_turns()[::-1]:
        bit = (win & jnp.where(core, odd, even)) != 0
        got = swap(x, lambda w, b: (w ^ (odd if b % 2 else even), b))
        x = jnp.concatenate([pick(bit, got, x), pick(bit, x, got)])
    got = core_swap(x)
    return jnp.concatenate([pick(core, got, x), pick(core, x, got)])


def sum_all(x):
    for s in range((lax.axis_size("blk") - 1).bit_length()):
        x = x + swap(x, lambda w, b: (w, b ^ (1 << s)))
    for s in range((lax.axis_size("win") - 1).bit_length()):
        x = x + win_swap(x, 1 << s)
    return x


def gather_tokens(x):
    blk = lax.axis_index("blk")
    chips = lax.axis_size("blk") // 2
    core, chip = blk % 2, blk // 2
    mine = [x] + [chip_swap(x, s) for s in range(1, chips)]
    theirs = core_swap(jnp.stack(mine, axis=0))
    out = jnp.zeros((x.shape[0], 2 * chips) + x.shape[1:], x.dtype)
    for s in range(chips):
        place = 2 * (chip ^ s)
        out = lax.dynamic_update_index_in_dim(out, mine[s], place + core, 1)
        out = lax.dynamic_update_index_in_dim(out, theirs[s], place + 1 - core, 1)
    return out


def scatter_tokens(x):
    blk = lax.axis_index("blk")
    chips = lax.axis_size("blk") // 2
    core, chip = blk % 2, blk // 2
    x = x.reshape((x.shape[0], chips, 2) + x.shape[2:])
    send = lax.dynamic_index_in_dim(x, 1 - core, 2, keepdims=False)
    keep = lax.dynamic_index_in_dim(x, core, 2, keepdims=False)
    x = add_low([keep, core_swap(send)])
    parts = [lax.dynamic_index_in_dim(x, chip, 1, keepdims=False)]
    for s in range(1, chips):
        parts.append(chip_swap(lax.dynamic_index_in_dim(x, chip ^ s, 1, keepdims=False), s))
    return add_low(parts)


def rank_within(species):
    window = jnp.arange(species.shape[0], dtype=jnp.int32)
    same = species[:, None] == species[None, :]
    earlier = window[None, :] < window[:, None]
    return jnp.sum((same & earlier).astype(jnp.int32), axis=1)


def fetch_cotangent(cot, species, rank, count):
    me = lax.axis_index("win")
    total = None
    for s in range(lax.axis_size("win")):
        rows = []
        for j in range(count):
            w = (me ^ s) * count + j
            row = lax.dynamic_index_in_dim(cot, jnp.minimum(rank[w], cot.shape[0] - 1), 0, keepdims=False)
            rows.append(jnp.where(species[w] == me, row, jnp.zeros((), cot.dtype)))
        part = jnp.stack(rows)
        if s:
            part = win_swap(part, s)
        total = part if total is None else total + part
    return total


def place_result(y, species, rank, slots):
    me = lax.axis_index("win")
    count = y.shape[0]
    wins = lax.axis_size("win")
    parts = jnp.concatenate([y] + [win_swap(y, s) for s in range(1, wins)])
    order = jnp.concatenate([(me ^ s) * count + jnp.arange(count, dtype=jnp.int32) for s in range(wins)])
    here = jnp.where(species[order] == me, rank[order], -1)
    out = []
    for k in range(slots):
        hit = here == k
        row = lax.dynamic_index_in_dim(parts, jnp.argmax(hit), 0, keepdims=False)
        out.append(jnp.where(jnp.any(hit), row, jnp.zeros((), y.dtype)))
    return jnp.stack(out)


def key_bias(random_blocks, tok):
    per = tok // BS
    blk = lax.axis_index("blk")
    total = lax.axis_size("blk") * per
    picks = lax.dynamic_slice_in_dim(random_blocks, blk * per, per, 0)
    i = (blk * per + jnp.arange(per, dtype=jnp.int32))[:, None, None]
    kb = jnp.arange(total, dtype=jnp.int32)[None, None, :]

    def hits(flag):
        return flag.astype(F32)

    m = hits(kb == i - 1) + hits(kb == i) + hits(kb == i + 1)
    m = m + hits((kb == 0) & (i >= 2)) + hits((kb == total - 1) & (i <= total - 3))
    for r in range(picks.shape[2]):
        m = m + hits(picks[:, :, r : r + 1] == kb)
    m = jnp.where((i == 0) | (i == total - 1), 1.0, m)
    bias = jnp.where(m > 0, jnp.log(jnp.maximum(m, 1.0)), MASKED)
    bias = bias.reshape(per, PAIRS, 2, total).transpose(1, 3, 2, 0)
    return jnp.broadcast_to(bias[..., None], bias.shape + (BS,)).reshape(PAIRS, total, 2 * tok)


def per_device(
    inputs,
    species,
    random_blocks,
    qkv_weight,
    q_bias,
    v_bias,
    out_weight,
    out_bias,
    norm1_gain,
    norm1_bias,
    norm2_gain,
    norm2_bias,
    ffn_in_weight,
    ffn_in_bias,
    ffn_out_weight,
    ffn_out_bias,
    cotangent,
):
    count, tok, d = inputs.shape
    rows = count * tok
    blks = lax.axis_size("blk")
    row_vec = lambda v: v.reshape(1, d)
    rank = rank_within(species)

    everything = gather_tokens(inputs).reshape(count * blks * tok, d)
    dy = fetch_cotangent(cotangent, species, rank, count).reshape(rows, d)
    bias = key_bias(random_blocks, tok)
    x = inputs.reshape(rows, d)
    gain1, shift1 = row_vec(norm1_gain), row_vec(norm1_bias)
    a_own, q = query_rows(x, gain1, shift1, qkv_weight, row_vec(q_bias))
    a, k, v = kv_rows(everything, gain1, shift1, qkv_weight, row_vec(v_bias))
    o, lse = attend(q, k, v, bias, count)
    y, dx1, do, g_ffn, g_out, g_bi, vec2 = ffn(
        x,
        o,
        dy,
        out_weight,
        row_vec(out_bias),
        row_vec(norm2_gain),
        row_vec(norm2_bias),
        ffn_in_weight,
        ffn_in_bias,
        ffn_out_weight,
        row_vec(ffn_out_bias),
    )
    result = place_result(y.reshape(count, tok, d), species, rank, cotangent.shape[0])
    steps = g_ffn.shape[0]
    ffn_chunk = scatter_sum(g_ffn.reshape(steps * 2 * d, d))
    dq, dk, dv = attend_back(q, o, do, k, v, bias, lse, count)
    da, da_own, g_qkv, vec1 = qkv_back(a, dk, dv, a_own, dq, qkv_weight)
    da_sum = scatter_tokens(da.reshape(count, blks, tok, d)).reshape(rows, d)
    input_grad = input_back(x, da_sum, da_own, dx1, gain1).reshape(count, tok, d)

    qkvo_chunk = scatter_sum(jnp.concatenate([g_qkv, g_out[None]]).reshape(4 * d, d))
    vecs = sum_all(jnp.concatenate([vec1[:4], vec2[:4], g_bi.reshape(steps, d)]))
    ffn_all = gather_all(ffn_chunk).reshape(steps, 2, d, d)
    qkvo_all = gather_all(qkvo_chunk).reshape(4, d, d)

    ffn_out_grad = ffn_all[:, 0].reshape(steps * d, d).astype(F32)
    ffn_in_grad = ffn_all[:, 1].transpose(1, 0, 2).reshape(d, steps * d).astype(F32)
    qkv_grad = qkvo_all[:3].transpose(1, 0, 2).reshape(d, 3 * d).astype(F32)
    out_grad = qkvo_all[3].astype(F32)
    gain1_grad = (vecs[0] - norm1_bias * vecs[1]) / norm1_gain
    return (
        result,
        input_grad,
        qkv_grad,
        vecs[2],
        vecs[3],
        out_grad,
        vecs[7],
        gain1_grad,
        vecs[1],
        vecs[5],
        vecs[6],
        ffn_in_grad,
        vecs[8:].reshape(steps * d),
        ffn_out_grad,
        vecs[4],
    )


def solution(mesh):
    split = P("win", "blk", None)
    return jax.shard_map(
        per_device,
        mesh=mesh,
        in_specs=(split,) + (P(),) * 15 + (split,),
        out_specs=(split, split) + (P(),) * 13,
        check_vma=False,
    )
```

```python
import functools

import jax
import jax.numpy as jnp
import numpy as np
from jax import lax
from jax.experimental import pallas as pl
from jax.experimental.pallas import tpu as pltpu
from jax.sharding import PartitionSpec as P

HEADS = 12
HD = 64
BS = 64
PAIRS = HEADS // 2
PW = 2 * HD

EPS = 1e-05
SCALE = 0.125
MASKED = -1e30
BF = jnp.bfloat16
F32 = jnp.float32
BOTH = ("win", "blk")
MIB = 1024 * 1024


def dot(a, b, ca=1, cb=0, precision=None):
    return lax.dot_general(
        a, b, (((ca,), (cb,)), ((), ())), precision=precision, preferred_element_type=F32
    )


def flip(i, size):
    bits = (size - 1).bit_length()
    out = 0
    for k in range(bits):
        out = out | (((i >> k) & 1) << (bits - 1 - k))
    return out


def params(grid_dims, mib):
    return pltpu.CompilerParams(
        dimension_semantics=("arbitrary",) * grid_dims, vmem_limit_bytes=mib * MIB
    )


def cost(us):
    return pl.CostEstimate(flops=1, bytes_accessed=int(us * 0.1 * 3.6e6), transcendentals=0)


def norm_stats(x):
    width = x.shape[-1]
    mean = jnp.sum(x, axis=-1, keepdims=True) * (1.0 / width)
    c = x - mean
    var = jnp.sum(c * c, axis=-1, keepdims=True) * (1.0 / width)
    rstd = lax.rsqrt(var + EPS)
    return c * rstd, rstd


def norm_back(g, xhat, rstd):
    width = g.shape[-1]
    m1 = jnp.sum(g, axis=-1, keepdims=True) * (1.0 / width)
    m2 = jnp.sum(g * xhat, axis=-1, keepdims=True) * (1.0 / width)
    return rstd * (g - m1 - xhat * m2)


class Order:
    def __init__(self):
        self.last = None
        self.touched = []

    def touch(self, *arrays):
        self.touched += arrays

    def call(
        self, kernel, grid, in_specs, out_specs, out_shape, scratch, estimate, name, args, ids=None, alias=None, mib=8, mark=False
    ):
        scalars = [] if ids is None else list(ids) if isinstance(ids, tuple) else [ids]
        after = [] if self.last is None or any(self.last is arg for arg in args) else [self.last]
        after += self.touched
        count, outs = len(scalars) + len(in_specs), len(out_specs)
        if mark:
            out_specs = list(out_specs) + [pl.BlockSpec((8, 128), lambda *_: (0, 0))]
            out_shape = list(out_shape) + [jax.ShapeDtypeStruct((8, 128), F32)]

        def body(*refs):
            at = count + len(after)
            if mark:
                refs[at + outs][...] = jnp.zeros((8, 128), F32)
            kernel(*refs[:count], *refs[at : at + outs], *refs[at + len(out_specs) :])

        out = pl.pallas_call(
            body,
            grid_spec=pltpu.PrefetchScalarGridSpec(
                num_scalar_prefetch=len(scalars),
                grid=grid,
                in_specs=list(in_specs) + [pl.BlockSpec(memory_space=pl.ANY)] * len(after),
                out_specs=out_specs,
                scratch_shapes=scratch,
            ),
            out_shape=out_shape,
            input_output_aliases={len(scalars) + i: o for i, o in (alias or {}).items()},
            compiler_params=params(len(grid), mib),
            cost_estimate=estimate,
            name=name,
        )(*scalars, *args, *after)
        self.last = min(out, key=lambda part: part.size * part.dtype.itemsize)
        self.touched = []
        return out[:outs]


def slot_of(species_ref, w):
    group = species_ref[w]
    rank = jnp.int32(0)
    for other in range(species_ref.shape[0]):
        rank = rank + ((species_ref[other] == group) & (other < w)).astype(jnp.int32)
    return group, rank


def query_kernel(
    ids_ref, species_ref, picks_ref, x_ref, vec_ref, w_ref, cot_ref, a_ref, q_ref, bias_ref, *part_refs, wins, blks
):
    count, tok, _ = part_refs[0].shape
    me, blk = ids_ref[2 * wins + 2], ids_ref[2 * wins + 3]
    for s, ref in enumerate(part_refs):
        for j in range(count):
            group, rank = slot_of(species_ref, (me ^ s) * count + j)
            here = group == me
            row = cot_ref[jnp.minimum(rank, cot_ref.shape[0] - 1)]
            ref[j] = jnp.where(here, row, jnp.zeros_like(row))

    xhat, _ = norm_stats(x_ref[...].astype(F32))
    a = (xhat * vec_ref[0:1] + vec_ref[1:2]).astype(BF)
    a_ref[...] = a
    q = (dot(a, w_ref[...]) + vec_ref[2:3]).astype(BF)
    q_ref[...] = (q.astype(F32) * SCALE).astype(BF)

    per, chips = tok // BS, blks // 2
    total = blks * per
    shape = bias_ref.shape[1:]
    place = lax.broadcasted_iota(jnp.int32, shape, 0)
    lane = lax.broadcasted_iota(jnp.int32, shape, 1)
    j = (lane % tok) // BS
    group = place // per
    owner = blk ^ (2 * flip(group % chips, chips) + group // chips)
    kb = owner * per + place % per
    i = blk * per + j
    one, zero = jnp.float32(1), jnp.float32(0)

    def hits(flag):
        return jnp.where(flag, one, zero)

    near = hits(kb == i - 1) + hits(kb == i) + hits(kb == i + 1)
    near = near + hits((kb == 0) & (i >= 2)) + hits((kb == total - 1) & (i <= total - 3))
    rand = picks_ref.shape[0]
    for pair in range(PAIRS):
        m = near
        for r in range(rand):
            picked = jnp.zeros(shape, jnp.int32)
            for h in range(2):
                for b in range(per):
                    value = picks_ref[r, blk * per + b, 2 * pair + h]
                    picked = jnp.where(lane // BS == h * per + b, value, picked)
            m = m + hits(picked == kb)
        m = jnp.where((i == 0) | (i == total - 1), one, m)
        bias_ref[pair] = jnp.where(m > 0, jnp.log(jnp.maximum(m, one)), MASKED)


def query_rows(run, ids, species, picks, x, vecs, w_qkv, cot, count, wins, blks):
    rows, d = x.shape
    slots, tok, _ = cot.shape
    row = pl.BlockSpec((rows, d), lambda i, *_: (0, 0))
    part = pl.BlockSpec((count, tok, d), lambda i, *_: (0, 0, 0))
    keys = (PAIRS, blks * (tok // BS), 2 * tok)
    return run.call(
        functools.partial(query_kernel, wins=wins, blks=blks),
        (1,),
        [
            row,
            pl.BlockSpec(vecs.shape, lambda i, *_: (0, 0)),
            pl.BlockSpec((d, d), lambda i, *_: (0, 0)),
            pl.BlockSpec((slots, tok, d), lambda i, *_: (0, 0, 0)),
        ],
        [row, row, pl.BlockSpec(keys, lambda i, *_: (0, 0, 0))] + [part] * wins,
        [jax.ShapeDtypeStruct((rows, d), BF)] * 2
        + [jax.ShapeDtypeStruct(keys, F32)]
        + [jax.ShapeDtypeStruct((count, tok, d), BF)] * wins,
        [],
        cost(1.7),
        "query_rows",
        (x, vecs, w_qkv, cot),
        ids=(ids, species, picks),
        mib=16,
    )


def kv_kernel(x0_ref, x1_ref, vec_ref, wk_ref, wv_ref, *refs):
    a_ref, k_ref, v_ref = refs[-3:]
    step, half = pl.program_id(0), pl.num_programs(0) // 2
    groups, tok, d = x0_ref.shape
    x = jnp.where(step < half, x0_ref[...], x1_ref[...]).reshape(groups * tok, d)
    xhat, _ = norm_stats(x.astype(F32))
    a = (xhat * vec_ref[0:1] + vec_ref[1:2]).astype(BF)
    a_ref[0] = a
    k_ref[...] = dot(a, wk_ref[...]).astype(BF)
    v_ref[...] = (dot(a, wv_ref[...]) + vec_ref[3:4]).astype(BF)


def kv_rows(run, mine, theirs, vecs, w_qkv, window, windows, before):
    chips, tok, d = mine.shape
    size = min(chips, 4)
    half = chips // size
    rows = 2 * chips * tok
    tile = size * tok
    row = pl.BlockSpec((tile, d), lambda i: (i, 0))
    return run.call(
        kv_kernel,
        (2 * half,),
        [
            pl.BlockSpec((size, tok, d), lambda i: (jnp.minimum(i, half - 1), 0, 0)),
            pl.BlockSpec((size, tok, d), lambda i: (jnp.maximum(i - half, 0), 0, 0)),
            pl.BlockSpec(vecs.shape, lambda i: (0, 0)),
            pl.BlockSpec((d, d), lambda i: (0, 1)),
            pl.BlockSpec((d, d), lambda i: (0, 2)),
        ]
        + [pl.BlockSpec(memory_space=pl.ANY)] * len(before),
        [pl.BlockSpec((1, tile, d), lambda i: (window, i, 0)), row, row],
        [jax.ShapeDtypeStruct((windows, rows, d), BF)] + [jax.ShapeDtypeStruct((rows, d), BF)] * 2,
        [],
        cost(3.7),
        "kv_rows",
        (mine, theirs, vecs, w_qkv, w_qkv, *before),
        alias={5: 0} if before else None,
        mib=14,
    )


def head_stack(pair):
    lane = lax.broadcasted_iota(jnp.int32, pair.shape, 1)
    zero = jnp.zeros_like(pair)
    return jnp.concatenate([jnp.where(lane < HD, pair, zero), jnp.where(lane < HD, zero, pair)], axis=0)


def head_select(both):
    rows = both.shape[0] // 2
    lane = lax.broadcasted_iota(jnp.int32, (rows, both.shape[1]), 1)
    return jnp.where(lane < HD, both[:rows], both[rows:])


def biased_scores(k, q2, bias):
    s = dot(k, q2, 1, 1)
    keys, lanes = s.shape
    return (s.reshape(keys // BS, BS, lanes) + bias[:, None, :]).reshape(keys, lanes)


def attend_kernel(q_ref, k_ref, v_ref, bias_ref, *refs):
    o_ref, lse_ref = refs[-2:]
    q2 = head_stack(q_ref[...])
    s = biased_scores(k_ref[...], q2, bias_ref[0])
    top = jnp.max(s, axis=0, keepdims=True)
    e = jnp.exp(s - top)
    total = jnp.sum(e, axis=0, keepdims=True)
    p = (e * (1.0 / total)).astype(BF)
    o_t = dot(v_ref[...], p, 0, 0)
    o_ref[...] = head_select(o_t.T).astype(BF)
    lse_ref[0, 0] = top + jnp.log(total)


def attend(run, q, k, v, bias, window, windows, before):
    rows, d = q.shape
    tok = rows // windows
    keys = k.shape[0]
    nkb = keys // BS
    q_spec = pl.BlockSpec((tok, PW), lambda p: (window, p))
    k_spec = pl.BlockSpec((keys, PW), lambda p: (0, p))
    return run.call(
        attend_kernel,
        (PAIRS,),
        [q_spec, k_spec, k_spec, pl.BlockSpec((1, nkb, 2 * tok), lambda p: (p, 0, 0))]
        + [pl.BlockSpec(memory_space=pl.ANY)] * len(before),
        [q_spec, pl.BlockSpec((1, 1, 1, 2 * tok), lambda p: (window, p, 0, 0))],
        [
            jax.ShapeDtypeStruct((rows, d), BF),
            jax.ShapeDtypeStruct((windows, PAIRS, 1, 2 * tok), F32),
        ],
        [],
        cost(6.6),
        "attend",
        (q, k, v, bias, *before),
        alias={4: 0, 5: 1} if before else None,
        mib=6 + keys // 256,
    )


def ffn_kernel(
    ids_ref,
    x_ref,
    o_ref,
    *refs,
    wins,
):
    ends = (wins, wins + 9, 3 * wins + 9)
    cots, head, sends, tail = (refs[a:b] for a, b in zip((0,) + ends, ends + (None,)))
    ffn_body(ids_ref, x_ref, o_ref, cots, *head, sends, *tail, wins=wins)


def ffn_body(
    ids_ref,
    x_ref,
    o_ref,
    cot_refs,
    wo_ref,
    vec_ref,
    wi_ref,
    wd_ref,
    y_ref,
    dx1_ref,
    do_ref,
    keep0_ref,
    keep1_ref,
    send_refs,
    gwo_ref,
    sum_ref,
    x1_s,
    h2_s,
    h2t_s,
    y_s,
    dh_s,
    dy_s,
    *,
    wins,
):
    step = pl.program_id(0)
    core = ids_ref[2 * wins]
    chip = ids_ref[2 * wins + 1]
    gain = vec_ref[5:6]

    @pl.when(step == 0)
    def _():
        x1 = x_ref[...].astype(F32) + (dot(o_ref[...], wo_ref[...]) + vec_ref[4:5])
        x1_s[...] = x1
        xhat, _ = norm_stats(x1)
        h2 = xhat * gain + vec_ref[6:7]
        h2_s[...] = h2.astype(BF)
        h2t_s[...] = h2.T.astype(BF)
        y_s[...] = jnp.zeros_like(y_s)
        dh_s[...] = jnp.zeros_like(dh_s)
        sum_ref[...] = jnp.zeros_like(sum_ref)
        total = cot_refs[0][...].astype(F32)
        for ref in cot_refs[1:]:
            total = total + ref[...].astype(F32)
        dy_s[...] = total.reshape(dy_s.shape).astype(BF)

    dy = dy_s[...]
    wi = wi_ref[...]
    wd = wd_ref[...]
    u = dot(h2_s[...], wi) + vec_ref[pl.ds(8 + ids_ref[step], 1)]
    half = 0.5 * (1.0 + lax.erf(u * 0.7071067811865476))
    f = (u * half).astype(BF)
    slope = half + u * (jnp.exp(u * u * -0.5) * 0.3989422804014327)
    du = dot(dy, wd, 1, 1) * slope
    du_low = du.astype(BF)
    y_s[...] += dot(f, wd)
    dh_s[...] += dot(du_low, wi, 1, 1)
    gd = dot(f, dy, 0, 0)
    gi = dot(h2t_s[...], du_low)
    keep = jnp.where(core == 0, gd, gi).astype(BF)
    send = jnp.where(core == 0, gi, gd).astype(BF)
    _, chips, sub, cols = keep0_ref.shape
    for q in range(chips):
        rows = slice(q * sub, (q + 1) * sub)
        for part, ref in enumerate((keep0_ref, keep1_ref)):
            ref[0, flip(q ^ chip, chips)] = keep[rows, part * cols : (part + 1) * cols]
    for slot in range(wins):

        @pl.when(step == flip(slot, wins))
        def _():
            for q in range(chips):
                for part in range(2):
                    value = send[q * sub : (q + 1) * sub, part * cols : (part + 1) * cols]
                    send_refs[part * wins + slot][flip(q ^ chip, chips)] = value

    sum_ref[pl.ds(8 + ids_ref[step], 1)] = jnp.sum(du_low.astype(F32), axis=0, keepdims=True)

    @pl.when(step == pl.num_programs(0) - 1)
    def _():
        x1 = x1_s[...]
        y_ref[...] = (x1 + (y_s[...] + vec_ref[7:8])).astype(BF)
        dyf = dy.astype(F32)
        dh = dh_s[...]
        xhat, rstd = norm_stats(x1)
        dx1 = dyf + norm_back(dh * gain, xhat, rstd)
        dx1_ref[...] = dx1
        dx1r = dx1.astype(BF)
        do_ref[...] = dot(dx1r, wo_ref[...], 1, 1).astype(BF)
        gwo_ref[...] = dot(o_ref[...], dx1r, 0, 0).astype(BF)
        sum_ref[4:5] = jnp.sum(dyf, axis=0, keepdims=True)
        sum_ref[5:6] = jnp.sum(dh * xhat, axis=0, keepdims=True)
        sum_ref[6:7] = jnp.sum(dh, axis=0, keepdims=True)
        sum_ref[7:8] = jnp.sum(dx1r.astype(F32), axis=0, keepdims=True)


def ffn(run, ids, x, o, cots, w_out, vecs, w_in, w_down, wins, chips):
    rows, d = x.shape
    ff = w_in.shape[1]
    tile = ff // wins
    sub = tile // chips
    cols = d // 2
    row = pl.BlockSpec((rows, d), lambda t, ids: (0, 0))
    square = pl.BlockSpec((d, d), lambda t, ids: (0, 0))
    keep = pl.BlockSpec((1, chips, sub, cols), lambda t, ids: (t, 0, 0, 0))
    send = pl.BlockSpec((chips, sub, cols), lambda t, ids: (0, 0, 0))
    part = jax.ShapeDtypeStruct((wins, chips, sub, cols), BF)
    return run.call(
        functools.partial(ffn_kernel, wins=wins),
        (wins,),
        [row, row]
        + [pl.BlockSpec(cots[0].shape, lambda t, ids: (0, 0, 0))] * wins
        + [
            square,
            pl.BlockSpec(vecs.shape, lambda t, ids: (0, 0)),
            pl.BlockSpec((d, tile), lambda t, ids: (0, ids[t])),
            pl.BlockSpec((tile, d), lambda t, ids: (ids[t], 0)),
        ],
        [row, row, row, keep, keep] + [send] * (2 * wins) + [square, pl.BlockSpec((16, d), lambda t, ids: (0, 0))],
        [
            jax.ShapeDtypeStruct((rows, d), BF),
            jax.ShapeDtypeStruct((rows, d), F32),
            jax.ShapeDtypeStruct((rows, d), BF),
            part,
            part,
        ]
        + [jax.ShapeDtypeStruct((chips, sub, cols), BF)] * (2 * wins)
        + [
            jax.ShapeDtypeStruct((d, d), BF),
            jax.ShapeDtypeStruct((16, d), F32),
        ],
        [
            pltpu.VMEM((rows, d), F32),
            pltpu.VMEM((rows, d), BF),
            pltpu.VMEM((d, rows), BF),
            pltpu.VMEM((rows, d), F32),
            pltpu.VMEM((rows, d), F32),
            pltpu.VMEM((rows, d), BF),
        ],
        cost(14),
        "ffn",
        (x, o, *cots, w_out, vecs, w_in, w_down),
        ids=ids,
        mib=24,
    )


def attend_back_kernel(
    q_ref, o_ref, do_ref, k_ref, v_ref, bias_ref, lse_ref, dq_ref, dk_ref, dv_ref, dq_s
):
    step = pl.program_id(1)
    q2 = head_stack(q_ref[...])
    do = do_ref[...]
    do2 = head_stack(do)
    prod = head_stack(do.astype(F32) * o_ref[...].astype(F32))
    delta = dot(jnp.ones((8, PW), F32), prod, 1, 1, lax.Precision.HIGHEST)[0:1]
    k = k_ref[...]
    p = jnp.exp(biased_scores(k, q2, bias_ref[0]) - lse_ref[0, 0])
    dp = dot(v_ref[...], do2, 1, 1)
    ds = (p * (dp - delta)).astype(BF)
    dv_ref[...] = dot(p.astype(BF), do2).astype(BF)
    dk_ref[...] = dot(ds, q2).astype(BF)
    dq_t = dot(k, ds, 0, 0)

    @pl.when(step == 0)
    def _():
        dq_s[...] = dq_t

    @pl.when(step > 0)
    def _():
        dq_s[...] += dq_t

    @pl.when(step == pl.num_programs(1) - 1)
    def _():
        dq_ref[...] = (head_select(dq_s[...].T) * SCALE).astype(BF)


def attend_back(run, q, o, do, k, v, bias, lse, window, windows):
    rows, d = q.shape
    tok = rows // windows
    keys = k.shape[0]
    chunk = min(keys, 1024)
    parts = keys // chunk
    nkb = chunk // BS
    q_spec = pl.BlockSpec((tok, PW), lambda p, c: (window, p))
    k_spec = pl.BlockSpec((chunk, PW), lambda p, c: (c, p))
    return run.call(
        attend_back_kernel,
        (PAIRS, parts),
        [
            q_spec,
            q_spec,
            q_spec,
            k_spec,
            k_spec,
            pl.BlockSpec((1, nkb, 2 * tok), lambda p, c: (p, c, 0)),
            pl.BlockSpec((1, 1, 1, 2 * tok), lambda p, c: (window, p, 0, 0)),
        ],
        [pl.BlockSpec((tok, PW), lambda p, c: (0, p)), k_spec, k_spec],
        [jax.ShapeDtypeStruct((tok, d), BF)] + [jax.ShapeDtypeStruct((keys, d), BF)] * 2,
        [pltpu.VMEM((PW, 2 * tok), F32)],
        cost(7.1),
        "attend_back",
        (q, o, do, k, v, bias, lse),
        mib=10,
    )


def token_back_kernel(a_ref, dk_ref, dv_ref, al_ref, dq_ref, wq_ref, wk_ref, wv_ref, keep_ref, send_ref, dal_ref, sum_ref):
    side = pl.program_id(0)

    @pl.when((side == 0) & (pl.program_id(1) == 0))
    def _():
        dq = dq_ref[...]
        dal = dot(dq, wq_ref[...], 1, 1)
        dal_ref[...] = dal
        sum_ref[0:1] = jnp.sum(dal * al_ref[...].astype(F32), axis=0, keepdims=True)
        sum_ref[1:2] = jnp.sum(dal, axis=0, keepdims=True)
        sum_ref[2:3] = jnp.sum(dq.astype(F32), axis=0, keepdims=True)
        sum_ref[3:8] = jnp.zeros((5, sum_ref.shape[1]), F32)

    dv = dv_ref[...]
    da = dot(dk_ref[...], wk_ref[...], 1, 1) + dot(dv, wv_ref[...], 1, 1)
    low = da.astype(BF).reshape(keep_ref.shape)

    @pl.when(side == 0)
    def _():
        keep_ref[...] = low

    @pl.when(side == 1)
    def _():
        send_ref[...] = low

    sum_ref[0:1] += jnp.sum(da * a_ref[0].astype(F32), axis=0, keepdims=True)
    sum_ref[1:2] += jnp.sum(da, axis=0, keepdims=True)
    sum_ref[3:4] += jnp.sum(dv.astype(F32), axis=0, keepdims=True)


def token_back(run, a, dk, dv, a_own, dq, w_qkv, tok, window):
    keys, d = dk.shape
    chips = keys // tok // 2
    size = min(chips, 4)
    half = chips // size
    tile = size * tok
    row = pl.BlockSpec((tile, d), lambda c, i: (c * half + i, 0))
    own_row = pl.BlockSpec((tok, d), lambda c, i: (0, 0))
    keep = pl.BlockSpec((size, tok, d), lambda c, i: (jnp.where(c == 0, i, half - 1), 0, 0))
    send = pl.BlockSpec((size, tok, d), lambda c, i: (jnp.where(c == 0, 0, i), 0, 0))
    part = jax.ShapeDtypeStruct((chips, tok, d), BF)
    return run.call(
        token_back_kernel,
        (2, half),
        [
            pl.BlockSpec((1, tile, d), lambda c, i: (window, c * half + i, 0)),
            row,
            row,
            pl.BlockSpec((tok, d), lambda c, i: (window, 0)),
            own_row,
            pl.BlockSpec((d, d), lambda c, i: (0, 0)),
            pl.BlockSpec((d, d), lambda c, i: (0, 1)),
            pl.BlockSpec((d, d), lambda c, i: (0, 2)),
        ],
        [keep, send, own_row, pl.BlockSpec((8, d), lambda c, i: (0, 0))],
        [part, part, jax.ShapeDtypeStruct((tok, d), F32), jax.ShapeDtypeStruct((8, d), F32)],
        [],
        cost(4.5),
        "token_back",
        (a, dk, dv, a_own, dq, w_qkv, w_qkv, w_qkv),
        mib=16,
    )


VECS = 16


def split_low(x):
    high = x.astype(BF)
    return high, (x - high.astype(F32)).astype(BF)


def qkv_grad_kernel(a_ref, al_ref, *refs):
    g_ref = refs[-1]
    windows = (len(refs) - 1) // 3
    dks, dvs, dqs = (refs[i * windows : (i + 1) * windows] for i in range(3))
    window = pl.program_id(0)
    tok = dqs[0].shape[0]

    @pl.when((window == 0) & (pl.program_id(1) == 0))
    def _():
        total = dot(al_ref[:tok], dqs[0][...], 0, 0)
        for w in range(1, windows):
            total = total + dot(al_ref[w * tok : (w + 1) * tok], dqs[w][...], 0, 0)
        g_ref[0] = total
        g_ref[1:] = jnp.zeros((2,) + g_ref.shape[1:], F32)

    a_t = a_ref[0].T
    dk, dv = dks[0][...], dvs[0][...]
    for w in range(1, windows):
        dk = jnp.where(window == w, dks[w][...], dk)
        dv = jnp.where(window == w, dvs[w][...], dv)
    g_ref[1] += dot(a_t, dk)
    g_ref[2] += dot(a_t, dv)


def qkv_grad(run, a, dks, dvs, a_own, dqs):
    windows, keys, d = a.shape
    tok = dqs[0].shape[0]
    tile = min(keys, 512)
    steps = keys // tile

    def rows_of(window):
        def where(w, i):
            return (jnp.where(w < window, 0, jnp.where(w > window, steps - 1, i)), 0)

        return pl.BlockSpec((tile, d), where)

    per_window = [rows_of(w) for w in range(windows)]
    [out] = run.call(
        qkv_grad_kernel,
        (windows, steps),
        [pl.BlockSpec((1, tile, d), lambda w, i: (w, i, 0)), pl.BlockSpec(a_own.shape, lambda w, i: (0, 0))]
        + per_window * 2
        + [pl.BlockSpec((tok, d), lambda w, i: (0, 0))] * windows,
        [pl.BlockSpec((3, d, d), lambda w, i: (0, 0, 0))],
        [jax.ShapeDtypeStruct((3, d, d), F32)],
        [],
        cost(7.5),
        "qkv_grad",
        (a, a_own, *dks, *dvs, *dqs),
        mib=14,
        mark=True,
    )
    return out


def pack_kernel(ids_ref, g_ref, gwo_ref, sum2_ref, *refs, wins, chips):
    sums, keep_ref, sends = refs[: -wins - 1], refs[-wins - 1], refs[-wins:]
    core = ids_ref[2 * wins]
    chip = ids_ref[2 * wins + 1]
    slots = wins * chips
    sub = (keep_ref.shape[0] - 2 * VECS) // slots
    per = wins // 2
    even = (g_ref[0], gwo_ref[...].astype(F32))
    odd = (g_ref[1], g_ref[2])
    for m in range(2):
        mine = jnp.where(core == 0, even[m], odd[m]).astype(BF)
        other = jnp.where(core == 0, odd[m], even[m]).astype(BF)
        for h in range(per):
            slot = ids_ref[wins + m * per + h]
            for q in range(chips):
                rows = slice((h * chips + q) * sub, (h * chips + q + 1) * sub)
                place = flip(q ^ chip, chips)
                keep_ref[pl.ds(pl.multiple_of((slot * chips + place) * sub, sub), sub)] = mine[rows]
                for to, ref in enumerate(sends):

                    @pl.when(flip(slot, wins) == to)
                    def _():
                        ref[pl.ds(pl.multiple_of(place * sub, sub), sub)] = other[rows]

    first = sums[0][0:4]
    for ref in sums[1:]:
        first = first + ref[0:4]
    high, rest = split_low(jnp.concatenate([first, sum2_ref[4:]]))
    for ref, at in ((keep_ref, slots * sub), (sends[-1], chips * sub)):
        ref[at : at + VECS] = high
        ref[at + VECS :] = rest


def pack(run, ids, g, g_out, sums1, sums2, wins, chips):
    d = g_out.shape[0]
    total = 2 * d + 2 * VECS
    size = 2 * d // wins
    shapes = [total] + [size] * (wins - 1) + [size + 2 * VECS]
    return run.call(
        functools.partial(pack_kernel, wins=wins, chips=chips),
        (1,),
        [
            pl.BlockSpec((3, d, d), lambda i, ids: (0, 0, 0)),
            pl.BlockSpec((d, d), lambda i, ids: (0, 0)),
            pl.BlockSpec((16, d), lambda i, ids: (0, 0)),
        ]
        + [pl.BlockSpec((8, d), lambda i, ids: (0, 0))] * len(sums1),
        [pl.BlockSpec((n, d), lambda i, ids: (0, 0)) for n in shapes],
        [jax.ShapeDtypeStruct((n, d), BF) for n in shapes],
        [],
        cost(2),
        "pack",
        (g, g_out, sums2, *sums1),
        ids=ids,
        mib=18,
    )


def fold_kernel(keep_ref, *refs):
    gots, (away_ref, keep_out_ref) = refs[:-2], refs[-2:]
    half = away_ref.shape[0]
    size = gots[0].shape[0]
    for i in range(0, 2 * half, min(size, half)):
        rows = min(size, half)
        got = gots[i // size][i % size : i % size + rows]
        value = (keep_ref[i : i + rows].astype(F32) + got.astype(F32)).astype(BF)
        if i < half:
            keep_out_ref[i : i + rows] = value
        else:
            away_ref[i - half : i - half + rows] = value


def fold(run, keep, gots):
    half = keep.shape[0] // 2
    whole = lambda part: pl.BlockSpec(part.shape, lambda i: (0,) * keep.ndim)
    out = jax.ShapeDtypeStruct((half,) + keep.shape[1:], BF)
    return run.call(
        fold_kernel,
        (1,),
        [whole(keep)] + [whole(got) for got in gots],
        [whole(out), whole(out)],
        [out, out],
        [],
        cost(0.5),
        "fold",
        (keep, *gots),
    )


def total_kernel(keep_ref, got_ref, out_ref):
    out_ref[...] = (keep_ref[...].astype(F32) + got_ref[...].astype(F32)).astype(BF)


def total(run, keep, got):
    spec = pl.BlockSpec(keep.shape, lambda i: (0,) * keep.ndim)
    [out] = run.call(
        total_kernel,
        (1,),
        [spec, spec],
        [spec],
        [jax.ShapeDtypeStruct(keep.shape, BF)],
        [],
        cost(0.2),
        "total",
        (keep, got),
    )
    return out


def add_vecs(keep_ref, gots):
    rows = keep_ref.shape[0] - 2 * VECS
    size = rows // len(gots)
    both = [keep_ref[i * size : (i + 1) * size].astype(F32) + got[:size].astype(F32) for i, got in enumerate(gots)]
    mine = keep_ref[rows : rows + VECS].astype(F32) + keep_ref[rows + VECS :].astype(F32)
    other = gots[-1][size : size + VECS].astype(F32) + gots[-1][size + VECS :].astype(F32)
    return both[0] if len(both) == 1 else jnp.concatenate(both), mine + other


def fold_vecs_kernel(keep_ref, *refs):
    gots, (away_out_ref, keep_out_ref) = refs[:-2], refs[-2:]
    both, sums = add_vecs(keep_ref, gots)
    cut = both.shape[0] // 2
    high, rest = split_low(sums)
    for ref, part in ((away_out_ref, both[cut:]), (keep_out_ref, both[:cut])):
        ref[:cut] = part.astype(BF)
        ref[cut : cut + VECS] = high
        ref[cut + VECS :] = rest


def last_vecs_kernel(keep_ref, got_ref, out_ref, sum_ref):
    both, sums = add_vecs(keep_ref, [got_ref])
    out_ref[...] = both.astype(BF)
    sum_ref[...] = sums


def fold_vecs(run, keep, gots, last):
    rows, d = keep.shape
    spec = pl.BlockSpec((rows, d), lambda i: (0, 0))
    body = rows - 2 * VECS
    if last:
        shapes = [((body, d), BF), ((VECS, d), F32)]
    else:
        shapes = [((body // 2 + 2 * VECS, d), BF)] * 2

    return run.call(
        last_vecs_kernel if last else fold_vecs_kernel,
        (1,),
        [spec] + [pl.BlockSpec(got.shape, lambda i: (0, 0)) for got in gots],
        [pl.BlockSpec(shape, lambda i: (0, 0)) for shape, _ in shapes],
        [jax.ShapeDtypeStruct(*shape) for shape in shapes],
        [],
        cost(0.6),
        "fold_vecs",
        (keep, *gots),
    )


def gather_kernel(*refs):
    size = refs[0].shape[0]
    for i, ref in enumerate(refs[:-1]):
        refs[-1][i * size : (i + 1) * size] = ref[...]


def gather_parts(run, parts):
    size, tok, d = parts[0].shape
    spec = pl.BlockSpec((size, tok, d), lambda i: (0, 0, 0))
    shape = (size * len(parts), tok, d)
    [out] = run.call(
        gather_kernel,
        (1,),
        [spec] * len(parts),
        [pl.BlockSpec(shape, lambda i: (0, 0, 0))],
        [jax.ShapeDtypeStruct(shape, BF)],
        [],
        cost(0.3),
        "gather_parts",
        parts,
    )
    return out


def input_back_kernel(x_ref, dx1_ref, vec_ref, *refs):
    g_ref = refs[-1]
    windows = (len(refs) - 1) // 3
    tok = refs[0].shape[-2]
    for w in range(windows):
        keep_ref, got_ref, dal_ref = refs[3 * w : 3 * w + 3]
        rows = slice(w * tok, (w + 1) * tok)
        xhat, rstd = norm_stats(x_ref[rows].astype(F32))
        da = keep_ref[0].astype(F32) + got_ref[0].astype(F32) + dal_ref[...]
        g_ref[rows] = (dx1_ref[rows] + norm_back(da * vec_ref[0:1], xhat, rstd)).astype(BF)


def input_back(run, x, dx1, vecs, parts):
    rows, d = x.shape
    row = pl.BlockSpec((rows, d), lambda i: (0, 0))
    flat = [part for window in parts for part in window]
    [out] = run.call(
        input_back_kernel,
        (1,),
        [row, row, pl.BlockSpec(vecs.shape, lambda i: (0, 0))]
        + [pl.BlockSpec(part.shape, lambda i, n=part.ndim: (0,) * n) for part in flat],
        [row],
        [jax.ShapeDtypeStruct((rows, d), BF)],
        [],
        cost(1.4),
        "input_back",
        (x, dx1, vecs, *flat),
        mark=True,
    )
    return out


def tile_parts(refs, wins):
    size = wins // len(refs)
    return [(ref, i, size) for ref in refs for i in range(size)]


def unpack_ffn_kernel(ids_ref, *refs, wins, count, chips, part, parts):
    owns, gots = refs[:count], refs[count : 2 * count]
    down_ref, in_ref, down_s, in_s, sems = refs[-5:]
    even = ids_ref[2 * wins] == 0
    chip, win = ids_ref[2 * wins + 1], ids_ref[2 * wins + 2]
    sub, cols = owns[0].shape[1:]
    tile = chips * sub
    copies = []
    for slot, ((own_ref, at, _), (got_ref, _, _)) in enumerate(zip(tile_parts(owns, wins), tile_parts(gots, wins))):
        for q in range(chips):
            place = at * chips + flip(q ^ chip, chips)
            own = own_ref[place].astype(F32)
            got = got_ref[place].astype(F32)
            down_s[slot, q * sub : (q + 1) * sub] = jnp.where(even, own, got)
            in_s[slot, q * sub : (q + 1) * sub] = jnp.where(even, got, own)
        down_row = pl.multiple_of((win ^ flip(slot, wins)) * tile, tile)
        in_col = pl.multiple_of((win ^ slot) * (parts * cols) + part * cols, cols)
        for i, (src, dst) in enumerate(
            (
                (down_s, down_ref.at[pl.ds(down_row, tile), part * cols : (part + 1) * cols]),
                (in_s, in_ref.at[:, pl.ds(in_col, cols)]),
            )
        ):
            copies.append(pltpu.make_async_copy(src.at[slot], dst, sems.at[i, slot]))
            copies[-1].start()
    for copy in copies:
        copy.wait()


def unpack_ffn(run, ids, owns, gots, chips, wins, part, parts, before):
    _, sub, cols = owns[0].shape
    tile = chips * sub
    d = parts * cols
    whole = [pl.BlockSpec(own.shape, lambda i, ids: (0, 0, 0)) for own in owns]
    far = pl.BlockSpec(memory_space=pltpu.HBM)
    return run.call(
        functools.partial(unpack_ffn_kernel, wins=wins, count=len(owns), chips=chips, part=part, parts=parts),
        (1,),
        whole * 2 + [far] * len(before),
        [far, far],
        [
            pltpu.HBM((wins * tile, d), F32),
            pltpu.HBM((d, wins * tile), F32),
        ],
        [
            pltpu.VMEM((wins, tile, cols), F32),
            pltpu.VMEM((wins, tile, cols), F32),
            pltpu.SemaphoreType.DMA((2, wins)),
        ],
        cost(4.6),
        "unpack_ffn",
        (*owns, *gots, *before),
        ids=ids,
        alias={2 * len(owns): 0, 2 * len(owns) + 1: 1} if before else None,
        mib=22,
        mark=True,
    )


def unpack_qkvo_kernel(ids_ref, *refs, wins, count, chips):
    owns, gots = refs[:count], refs[count : 2 * count]
    qkv_ref, out_ref, stage, sems = refs[-4:]
    even = ids_ref[2 * wins] == 0
    chip, win = ids_ref[2 * wins + 1], ids_ref[2 * wins + 2]
    sub, d = owns[0].shape[1:]
    per = wins // 2
    size = chips * sub
    pairs = list(zip(tile_parts(owns, wins), tile_parts(gots, wins)))
    copies = []
    for slot, ((own_ref, at, _), (got_ref, _, _)) in enumerate(pairs):
        for side in range(2):
            for q in range(chips):
                place = at * chips + flip(q ^ chip, chips)
                first, second = (got_ref, own_ref) if side else (own_ref, got_ref)
                value = jnp.where(even, first[place], second[place]).astype(F32)
                stage[slot, side, q * sub : (q + 1) * sub] = value
            tile = win ^ (slot if side else flip(slot, wins))
            rows = pl.ds(pl.multiple_of((tile % per) * size, size), size)
            high = qkv_ref.at[rows, 2 * d : 3 * d] if side else out_ref.at[rows]
            low = qkv_ref.at[rows, side * d : (side + 1) * d]
            for flag, dst in ((tile < per, low), (tile >= per, high)):
                copy = pltpu.make_async_copy(stage.at[slot, side], dst, sems.at[slot, side])
                copies.append((flag, copy))
                pl.when(flag)(copy.start)
    for flag, copy in copies:
        pl.when(flag)(copy.wait)


def unpack_qkvo(run, ids, owns, gots, chips, wins):
    _, sub, d = owns[0].shape
    whole = [pl.BlockSpec(own.shape, lambda i, ids: (0, 0, 0)) for own in owns]
    far = pl.BlockSpec(memory_space=pltpu.HBM)
    return run.call(
        functools.partial(unpack_qkvo_kernel, wins=wins, count=len(owns), chips=chips),
        (1,),
        whole * 2,
        [far, far],
        [pltpu.HBM((d, 3 * d), F32), pltpu.HBM((d, d), F32)],
        [pltpu.VMEM((wins, 2, chips * sub, d), F32), pltpu.SemaphoreType.DMA((wins, 2))],
        cost(5),
        "unpack_qkvo",
        (*owns, *gots),
        ids=ids,
        mib=22,
        mark=True,
    )


def copy_kernel(x_ref, out_ref):
    out_ref[...] = x_ref[...]


def copied(run, x):
    spec = pl.BlockSpec(x.shape, lambda i: (0,) * x.ndim)
    [out] = run.call(
        copy_kernel, (1,), [spec], [spec], [jax.ShapeDtypeStruct(x.shape, x.dtype)], [], cost(0.5), "copied", (x,)
    )
    return out


def place_kernel(ids_ref, species_ref, *refs, wins):
    out_ref = refs[-1]
    count = refs[0].shape[0]
    me = ids_ref[2 * wins + 2]
    out_ref[...] = jnp.zeros_like(out_ref)
    for s, ref in enumerate(refs[:-1]):
        for j in range(count):
            group, rank = slot_of(species_ref, (me ^ s) * count + j)

            @pl.when(group == me)
            def _():
                out_ref[jnp.minimum(rank, out_ref.shape[0] - 1)] = ref[j]


def place_rows(run, ids, species, parts, slots, wins):
    count, tok, d = parts[0].shape
    spec = pl.BlockSpec((count, tok, d), lambda i, *_: (0, 0, 0))
    [out] = run.call(
        functools.partial(place_kernel, wins=wins),
        (1,),
        [spec] * len(parts),
        [pl.BlockSpec((slots, tok, d), lambda i, *_: (0, 0, 0))],
        [jax.ShapeDtypeStruct((slots, tok, d), BF)],
        [],
        cost(1.7),
        "place_rows",
        parts,
        ids=(ids, species),
        mark=True,
    )
    return out


def swap(x, partner):
    wins, blks = lax.axis_size("win"), lax.axis_size("blk")
    perm = []
    for w in range(wins):
        for b in range(blks):
            pw, pb = partner(w, b)
            perm.append((w * blks + b, pw * blks + pb))
    return lax.ppermute(x, BOTH, perm)


def core_swap(x):
    return swap(x, lambda w, b: (w, b ^ 1))


def chip_swap(x, s):
    return swap(x, lambda w, b: (w, b ^ (2 * s)))


def win_swap(x, s):
    return swap(x, lambda w, b: (w ^ s, b))


def win_turns(wins):
    bits = (wins - 1).bit_length()
    even = [1 << i for i in range(bits)]
    return list(zip(even, even[::-1]))


def turn_swap(x, turn):
    even, odd = turn
    return swap(x, lambda w, b: (w ^ (odd if b % 2 else even), b))


def exchange_ids(wins, blks):
    rows = []
    for w in range(wins):
        for b in range(blks):
            core, chip = b % 2, b // 2
            tiles = [w ^ (i if core else flip(i, wins)) for i in range(wins)]
            rows.append(tiles + [tiles.index(t) for t in range(wins)] + [core, chip, w, b])
    me = lax.axis_index("win") * blks + lax.axis_index("blk")
    return lax.dynamic_index_in_dim(jnp.asarray(np.array(rows, np.int32)), me, 0, keepdims=False)


def stacked(rows, width):
    parts = []
    for row in rows:
        parts += [row[i : i + width] for i in range(0, row.shape[0], width)]
    count = -(-len(parts) // 8) * 8
    index = lax.broadcasted_iota(jnp.int32, (count, width), 0)
    out = jnp.zeros((count, width), F32)
    for r, part in enumerate(parts):
        out = jnp.where(index == r, part[None, :], out)
    return out


def turns(wins, chips):
    def chip_turn(s):
        return lambda x: chip_swap(x, s)

    out = [functools.partial(turn_swap, turn=turn) for turn in win_turns(wins)]
    bits = (chips - 1).bit_length()
    return out + [chip_turn(1 << i) for i in range(bits)]


class Sum:
    def __init__(self, run, keep, sends, swaps, chip_turns):
        self.run, self.keep, self.swaps, self.chip_turns = run, keep, swaps, chip_turns
        self.turn, self.x = 0, None
        self.got = [core_swap(send) for send in sends]

    def fold(self):
        return fold(self.run, self.keep, self.got)

    def total(self):
        return total(self.run, self.keep, self.got[0])

    def step(self):
        if self.x is None and self.turn < len(self.swaps):
            away, self.keep = self.fold()
            self.got = [self.swaps[self.turn](away)]
            self.turn += 1
            return
        if self.x is None:
            self.x, self.owns, self.gots = self.total(), [], []
        else:
            [arrived] = self.got
            if self.turn == 0:
                arrived = copied(self.run, arrived)
            if self.turn == 0:
                self.own(arrived)
            else:
                self.x = gather_parts(self.run, [self.x, arrived])
        self.turn -= 1
        if self.turn >= 0:
            self.got = [self.swaps[self.turn](self.x)]
        if self.turn == 0:
            self.own(self.x)

    def own(self, part):
        self.owns.append(part)
        self.gots.append(core_swap(part))


class VecSum(Sum):
    def fold(self):
        return fold_vecs(self.run, self.keep, self.got, False)

    def total(self):
        x, sums = fold_vecs(self.run, self.keep, self.got, True)
        self.sums = jnp.where(lax.axis_index("blk") % 2 == 0, sums, core_swap(sums))
        return x[None]


ORDER = (
    "b0", "0", "1", "bb", "t0", "tt", "T0", "T1", "weight", "pack", "0", "1", "Q", "T0", "T1", "0", "1",
    "Q", "r", "0", "1", "Q", "0", "1", "uT", "place", "Q", "0", "1", "Q", "v", "0", "1", "Q", "0", "1",
    "Q", "Q", "0", "1", "u0", "Q", "u1", "uQ",
)


def schedule(more):
    steps = list(ORDER)
    for name in ("0", "1", "Q", "T0", "T1") if more else ():
        places = [i for i, step in enumerate(steps) if step == name]
        if name in "01Q":
            steps[places[-1] : places[-1]] = [name] * more
            steps[places[3] : places[3]] = [name] * more
        else:
            steps[places[1] : places[1]] = [name] * more
    return steps


def per_device(
    inputs,
    species,
    random_blocks,
    qkv_weight,
    q_bias,
    v_bias,
    out_weight,
    out_bias,
    norm1_gain,
    norm1_bias,
    norm2_gain,
    norm2_bias,
    ffn_in_weight,
    ffn_in_bias,
    ffn_out_weight,
    ffn_out_bias,
    cotangent,
):
    count, tok, d = inputs.shape
    rows = count * tok
    wins, blks = lax.axis_size("win"), lax.axis_size("blk")
    chips = blks // 2
    ids = exchange_ids(wins, blks)
    run = Order()
    vecs = stacked(
        [norm1_gain, norm1_bias, q_bias, v_bias, out_bias, norm2_gain, norm2_bias, ffn_out_bias, ffn_in_bias], d
    )
    swaps = turns(wins, chips)
    chip_bits = [1 << i for i in range((chips - 1).bit_length())]

    def chip_parts(row):
        parts = [row]
        for s in chip_bits[::-1]:
            parts = parts + [chip_swap(part, s) for part in parts]
        return parts

    parts = [chip_parts(inputs[w : w + 1]) for w in range(count)]
    x = inputs.reshape(rows, d)
    a_own, q, bias, *cots = query_rows(
        run, ids, species, random_blocks.transpose(2, 0, 1), x, vecs, qkv_weight, cotangent, count, wins, blks
    )
    cots = [cots[0]] + [win_swap(cots[s], s) for s in range(1, wins)]
    mine = [gather_parts(run, parts[w]) for w in range(count)]
    theirs = [core_swap(part) for part in mine]
    keys, before, a = [], (), ()
    for w in range(count):
        a, k, v = kv_rows(run, mine[w], theirs[w], vecs, qkv_weight, w, count, a)
        a = (a,)
        keys.append((k, v))
        before = attend(run, q, k, v, bias, w, count, before)
    [a] = a
    o, lse = before
    y, dx1, do, keep0, keep1, *sends, g_out, sums2 = ffn(
        run, ids, x, o, cots, out_weight, vecs, ffn_in_weight, ffn_out_weight, wins, chips
    )
    slotted = lambda part: part.reshape(wins * chips, part.shape[2], part.shape[3])
    bits = len(chip_bits)
    f0 = Sum(run, slotted(keep0), sends[:wins], swaps, bits)
    f1 = Sum(run, slotted(keep1), sends[wins:], swaps, bits)
    got = {"back": [], "T": []}

    def back(w):
        got["back"].append(attend_back(run, q, o, do, *keys[w], bias, lse, w, count))

    def token(w):
        dq, dk, dv = got["back"][w]
        keep, send, own, sums = token_back(run, a, dk, dv, a_own, dq, qkv_weight, tok, w)
        got["T"].append((Sum(run, keep, [send], swaps[-bits:], bits), own, sums))

    def weight():
        dqs, dks, dvs = zip(*got["back"])
        got["g"] = qkv_grad(run, a, dks, dvs, a_own, dqs)

    def packed():
        keep, *sends = pack(run, ids, got["g"], g_out, [part[2] for part in got["T"]], sums2, wins, chips)
        got["Q"] = VecSum(run, keep, sends, swaps, bits)

    def send_result():
        own = copied(run, y.reshape(count, tok, d))
        got["y"] = [own] + [win_swap(own, s) for s in range(1, wins)]

    def place():
        got["result"] = place_rows(run, ids, species, got["y"], cotangent.shape[0], wins)

    def tokens_end():
        parts = [(part.keep, part.got[0], own) for part, own, _ in got["T"]]
        got["input"] = input_back(run, x, dx1, vecs, parts).reshape(count, tok, d)

    def unpack(part, piece):
        got["ffn"] = unpack_ffn(run, ids, piece.owns, piece.gots, chips, wins, part, 2, got.get("ffn", ()))

    def vectors():
        sums = got["Q"].sums
        gain = (sums[0] - norm1_bias * sums[1]) / norm1_gain
        got["vectors"] = [gain] + [sums[i] for i in range(1, 8)] + [sums[8 : 8 + wins].reshape(-1)]
        run.touch(*got["vectors"])

    def unpack_last():
        got["qkvo"] = unpack_qkvo(run, ids, got["Q"].owns, got["Q"].gots, chips, wins)

    todo = {
        "b0": lambda: back(0),
        "bb": lambda: [back(w) for w in range(1, count)],
        "t0": lambda: token(0),
        "tt": lambda: [token(w) for w in range(1, count)],
        "T0": lambda: got["T"][0][0].step(),
        "T1": lambda: [part[0].step() for part in got["T"][1:]],
        "r": send_result,
        "place": place,
        "weight": weight,
        "pack": packed,
        "0": f0.step,
        "1": f1.step,
        "Q": lambda: got["Q"].step(),
        "v": vectors,
        "u0": lambda: unpack(0, f0),
        "u1": lambda: unpack(1, f1),
        "uQ": unpack_last,
        "uT": tokens_end,
    }
    for name in schedule(len(swaps) - 4):
        todo[name]()
    ffn_out_grad, ffn_in_grad = got["ffn"]
    qkv_grad_all, out_grad = got["qkvo"]
    result, input_grad = got["result"], got["input"]
    gain1, shift1, q_grad, v_grad, down, gain2, shift2, out_bias_grad, hidden = got["vectors"]
    return (
        result,
        input_grad,
        qkv_grad_all,
        q_grad,
        v_grad,
        out_grad,
        out_bias_grad,
        gain1,
        shift1,
        gain2,
        shift2,
        ffn_in_grad,
        hidden,
        ffn_out_grad,
        down,
    )


def solution(mesh):
    split = P("win", "blk", None)
    return jax.shard_map(
        per_device,
        mesh=mesh,
        in_specs=(split,) + (P(),) * 15 + (split,),
        out_specs=(split, split) + (P(),) * 13,
        check_vma=False,
    )
```

```python
import functools

import jax
import jax.numpy as jnp
import numpy as np
from jax import lax
from jax.experimental import pallas as pl
from jax.experimental.pallas import tpu as pltpu
from jax.sharding import PartitionSpec as P

HEADS = 12
HD = 64
BS = 64
PAIRS = HEADS // 2
PW = 2 * HD

EPS = 1e-05
SCALE = 0.125
MASKED = -1e30
BF = jnp.bfloat16
F32 = jnp.float32
BOTH = ("win", "blk")
MIB = 1024 * 1024


def dot(a, b, ca=1, cb=0, precision=None):
    return lax.dot_general(
        a, b, (((ca,), (cb,)), ((), ())), precision=precision, preferred_element_type=F32
    )


def flip(i, size):
    bits = (size - 1).bit_length()
    out = 0
    for k in range(bits):
        out = out | (((i >> k) & 1) << (bits - 1 - k))
    return out


def params(grid_dims, mib):
    return pltpu.CompilerParams(
        dimension_semantics=("arbitrary",) * grid_dims, vmem_limit_bytes=mib * MIB
    )


def cost(us):
    return pl.CostEstimate(flops=1, bytes_accessed=int(us * 0.1 * 3.6e6), transcendentals=0)


def norm_stats(x):
    width = x.shape[-1]
    mean = jnp.sum(x, axis=-1, keepdims=True) * (1.0 / width)
    c = x - mean
    var = jnp.sum(c * c, axis=-1, keepdims=True) * (1.0 / width)
    rstd = lax.rsqrt(var + EPS)
    return c * rstd, rstd


def norm_back(g, xhat, rstd):
    width = g.shape[-1]
    m1 = jnp.sum(g, axis=-1, keepdims=True) * (1.0 / width)
    m2 = jnp.sum(g * xhat, axis=-1, keepdims=True) * (1.0 / width)
    return rstd * (g - m1 - xhat * m2)


class Order:
    def __init__(self):
        self.last = None
        self.touched = []

    def touch(self, *arrays):
        self.touched += arrays

    def call(
        self, kernel, grid, in_specs, out_specs, out_shape, scratch, estimate, name, args, ids=None, alias=None, mib=8, mark=False
    ):
        scalars = [] if ids is None else list(ids) if isinstance(ids, tuple) else [ids]
        after = [] if self.last is None or any(self.last is arg for arg in args) else [self.last]
        after += self.touched
        count, outs = len(scalars) + len(in_specs), len(out_specs)
        if mark:
            out_specs = list(out_specs) + [pl.BlockSpec((8, 128), lambda *_: (0, 0))]
            out_shape = list(out_shape) + [jax.ShapeDtypeStruct((8, 128), F32)]

        def body(*refs):
            at = count + len(after)
            if mark:
                refs[at + outs][...] = jnp.zeros((8, 128), F32)
            kernel(*refs[:count], *refs[at : at + outs], *refs[at + len(out_specs) :])

        out = pl.pallas_call(
            body,
            grid_spec=pltpu.PrefetchScalarGridSpec(
                num_scalar_prefetch=len(scalars),
                grid=grid,
                in_specs=list(in_specs) + [pl.BlockSpec(memory_space=pl.ANY)] * len(after),
                out_specs=out_specs,
                scratch_shapes=scratch,
            ),
            out_shape=out_shape,
            input_output_aliases={len(scalars) + i: o for i, o in (alias or {}).items()},
            compiler_params=params(len(grid), mib),
            cost_estimate=estimate,
            name=name,
        )(*scalars, *args, *after)
        self.last = min(out, key=lambda part: part.size * part.dtype.itemsize)
        self.touched = []
        return out[:outs]


def slot_of(species_ref, w):
    group = species_ref[w]
    rank = jnp.int32(0)
    for other in range(species_ref.shape[0]):
        rank = rank + ((species_ref[other] == group) & (other < w)).astype(jnp.int32)
    return group, rank


def query_kernel(
    ids_ref, species_ref, picks_ref, x_ref, vec_ref, w_ref, cot_ref, a_ref, q_ref, bias_ref, *part_refs, wins, blks
):
    count, tok, _ = part_refs[0].shape
    me, blk = ids_ref[2 * wins + 2], ids_ref[2 * wins + 3]
    for s, ref in enumerate(part_refs):
        for j in range(count):
            group, rank = slot_of(species_ref, (me ^ s) * count + j)
            here = group == me
            row = cot_ref[jnp.minimum(rank, cot_ref.shape[0] - 1)]
            ref[j] = jnp.where(here, row, jnp.zeros_like(row))

    xhat, _ = norm_stats(x_ref[...].astype(F32))
    a = (xhat * vec_ref[0:1] + vec_ref[1:2]).astype(BF)
    a_ref[...] = a
    q = (dot(a, w_ref[...]) + vec_ref[2:3]).astype(BF)
    q_ref[...] = (q.astype(F32) * SCALE).astype(BF)

    per, chips = tok // BS, blks // 2
    total = blks * per
    shape = bias_ref.shape[1:]
    place = lax.broadcasted_iota(jnp.int32, shape, 0)
    lane = lax.broadcasted_iota(jnp.int32, shape, 1)
    j = (lane % tok) // BS
    group = place // per
    owner = blk ^ (2 * flip(group % chips, chips) + group // chips)
    kb = owner * per + place % per
    i = blk * per + j
    one, zero = jnp.float32(1), jnp.float32(0)

    def hits(flag):
        return jnp.where(flag, one, zero)

    near = hits(kb == i - 1) + hits(kb == i) + hits(kb == i + 1)
    near = near + hits((kb == 0) & (i >= 2)) + hits((kb == total - 1) & (i <= total - 3))
    rand = picks_ref.shape[0]
    for pair in range(PAIRS):
        m = near
        for r in range(rand):
            picked = jnp.zeros(shape, jnp.int32)
            for h in range(2):
                for b in range(per):
                    value = picks_ref[r, blk * per + b, 2 * pair + h]
                    picked = jnp.where(lane // BS == h * per + b, value, picked)
            m = m + hits(picked == kb)
        m = jnp.where((i == 0) | (i == total - 1), one, m)
        bias_ref[pair] = jnp.where(m > 0, jnp.log(jnp.maximum(m, one)), MASKED)


def query_rows(run, ids, species, picks, x, vecs, w_qkv, cot, count, wins, blks):
    rows, d = x.shape
    slots, tok, _ = cot.shape
    row = pl.BlockSpec((rows, d), lambda i, *_: (0, 0))
    part = pl.BlockSpec((count, tok, d), lambda i, *_: (0, 0, 0))
    keys = (PAIRS, blks * (tok // BS), 2 * tok)
    return run.call(
        functools.partial(query_kernel, wins=wins, blks=blks),
        (1,),
        [
            row,
            pl.BlockSpec(vecs.shape, lambda i, *_: (0, 0)),
            pl.BlockSpec((d, d), lambda i, *_: (0, 0)),
            pl.BlockSpec((slots, tok, d), lambda i, *_: (0, 0, 0)),
        ],
        [row, row, pl.BlockSpec(keys, lambda i, *_: (0, 0, 0))] + [part] * wins,
        [jax.ShapeDtypeStruct((rows, d), BF)] * 2
        + [jax.ShapeDtypeStruct(keys, F32)]
        + [jax.ShapeDtypeStruct((count, tok, d), BF)] * wins,
        [],
        cost(1.7),
        "query_rows",
        (x, vecs, w_qkv, cot),
        ids=(ids, species, picks),
        mib=16,
    )


def kv_kernel(x0_ref, x1_ref, vec_ref, wk_ref, wv_ref, *refs):
    a_ref, k_ref, v_ref = refs[-3:]
    step, half = pl.program_id(0), pl.num_programs(0) // 2
    groups, tok, d = x0_ref.shape
    x = jnp.where(step < half, x0_ref[...], x1_ref[...]).reshape(groups * tok, d)
    xhat, _ = norm_stats(x.astype(F32))
    a = (xhat * vec_ref[0:1] + vec_ref[1:2]).astype(BF)
    a_ref[0] = a
    k_ref[...] = dot(a, wk_ref[...]).astype(BF)
    v_ref[...] = (dot(a, wv_ref[...]) + vec_ref[3:4]).astype(BF)


def kv_rows(run, mine, theirs, vecs, w_qkv, window, windows, before):
    chips, tok, d = mine.shape
    size = min(chips, 4)
    half = chips // size
    rows = 2 * chips * tok
    tile = size * tok
    row = pl.BlockSpec((tile, d), lambda i: (i, 0))
    return run.call(
        kv_kernel,
        (2 * half,),
        [
            pl.BlockSpec((size, tok, d), lambda i: (jnp.minimum(i, half - 1), 0, 0)),
            pl.BlockSpec((size, tok, d), lambda i: (jnp.maximum(i - half, 0), 0, 0)),
            pl.BlockSpec(vecs.shape, lambda i: (0, 0)),
            pl.BlockSpec((d, d), lambda i: (0, 1)),
            pl.BlockSpec((d, d), lambda i: (0, 2)),
        ]
        + [pl.BlockSpec(memory_space=pl.ANY)] * len(before),
        [pl.BlockSpec((1, tile, d), lambda i: (window, i, 0)), row, row],
        [jax.ShapeDtypeStruct((windows, rows, d), BF)] + [jax.ShapeDtypeStruct((rows, d), BF)] * 2,
        [],
        cost(3.7),
        "kv_rows",
        (mine, theirs, vecs, w_qkv, w_qkv, *before),
        alias={5: 0} if before else None,
        mib=14,
    )


def head_stack(pair):
    lane = lax.broadcasted_iota(jnp.int32, pair.shape, 1)
    zero = jnp.zeros_like(pair)
    return jnp.concatenate([jnp.where(lane < HD, pair, zero), jnp.where(lane < HD, zero, pair)], axis=0)


def head_select(both):
    rows = both.shape[0] // 2
    lane = lax.broadcasted_iota(jnp.int32, (rows, both.shape[1]), 1)
    return jnp.where(lane < HD, both[:rows], both[rows:])


def biased_scores(k, q2, bias):
    s = dot(k, q2, 1, 1)
    keys, lanes = s.shape
    return (s.reshape(keys // BS, BS, lanes) + bias[:, None, :]).reshape(keys, lanes)


def attend_kernel(q_ref, k_ref, v_ref, bias_ref, *refs):
    o_ref, lse_ref = refs[-2:]
    for pair in range(bias_ref.shape[0]):
        lanes = slice(pair * PW, (pair + 1) * PW)
        q2 = head_stack(q_ref[:, lanes])
        s = biased_scores(k_ref[:, lanes], q2, bias_ref[pair])
        top = jnp.max(s, axis=0, keepdims=True)
        e = jnp.exp(s - top)
        total = jnp.sum(e, axis=0, keepdims=True)
        o_t = dot(v_ref[:, lanes], e.astype(BF), 0, 0) * (1.0 / total)
        o_ref[:, lanes] = head_select(o_t.T).astype(BF)
        lse_ref[0, pair] = top + jnp.log(total)


def attend(run, q, k, v, bias, window, windows, before):
    rows, d = q.shape
    tok = rows // windows
    keys = k.shape[0]
    nkb = keys // BS
    many = 2 if keys <= 1024 else 1
    q_spec = pl.BlockSpec((tok, many * PW), lambda p: (window, p))
    k_spec = pl.BlockSpec((keys, many * PW), lambda p: (0, p))
    return run.call(
        attend_kernel,
        (PAIRS // many,),
        [q_spec, k_spec, k_spec, pl.BlockSpec((many, nkb, 2 * tok), lambda p: (p, 0, 0))]
        + [pl.BlockSpec(memory_space=pl.ANY)] * len(before),
        [q_spec, pl.BlockSpec((1, many, 1, 2 * tok), lambda p: (window, p, 0, 0))],
        [
            jax.ShapeDtypeStruct((rows, d), BF),
            jax.ShapeDtypeStruct((windows, PAIRS, 1, 2 * tok), F32),
        ],
        [],
        cost(6.6),
        "attend",
        (q, k, v, bias, *before),
        alias={4: 0, 5: 1} if before else None,
        mib=6 + keys // 256,
    )


def ffn_kernel(
    ids_ref,
    x_ref,
    o_ref,
    *refs,
    wins,
):
    ends = (wins, wins + 9, 3 * wins + 9)
    cots, head, sends, tail = (refs[a:b] for a, b in zip((0,) + ends, ends + (None,)))
    ffn_body(ids_ref, x_ref, o_ref, cots, *head, sends, *tail, wins=wins)


def ffn_body(
    ids_ref,
    x_ref,
    o_ref,
    cot_refs,
    wo_ref,
    vec_ref,
    wi_ref,
    wd_ref,
    y_ref,
    dx1_ref,
    do_ref,
    keep0_ref,
    keep1_ref,
    send_refs,
    gwo_ref,
    sum_ref,
    x1_s,
    h2_s,
    h2t_s,
    y_s,
    dh_s,
    dy_s,
    send_s,
    *,
    wins,
):
    step = pl.program_id(0)
    core = ids_ref[2 * wins]
    chip = ids_ref[2 * wins + 1]
    gain = vec_ref[5:6]

    @pl.when(step == 0)
    def _():
        x1 = x_ref[...].astype(F32) + (dot(o_ref[...], wo_ref[...]) + vec_ref[4:5])
        x1_s[...] = x1
        xhat, _ = norm_stats(x1)
        h2 = xhat * gain + vec_ref[6:7]
        h2_s[...] = h2.astype(BF)
        h2t_s[...] = h2.T.astype(BF)
        y_s[...] = jnp.zeros_like(y_s)
        dh_s[...] = jnp.zeros_like(dh_s)
        sum_ref[...] = jnp.zeros_like(sum_ref)
        total = cot_refs[0][...].astype(F32)
        for ref in cot_refs[1:]:
            total = total + ref[...].astype(F32)
        dy_s[...] = total.reshape(dy_s.shape).astype(BF)

    dy = dy_s[...]
    wi = wi_ref[...]
    wd = wd_ref[...]
    u = dot(h2_s[...], wi) + vec_ref[pl.ds(8 + ids_ref[step], 1)]
    half = 0.5 * (1.0 + lax.erf(u * 0.7071067811865476))
    f = (u * half).astype(BF)
    slope = half + u * (jnp.exp(u * u * -0.5) * 0.3989422804014327)
    du = dot(dy, wd, 1, 1) * slope
    du_low = du.astype(BF)
    y_s[...] += dot(f, wd)
    dh_s[...] += dot(du_low, wi, 1, 1)
    gd = dot(f, dy, 0, 0)
    gi = dot(h2t_s[...], du_low)
    keep = jnp.where(core == 0, gd, gi).astype(BF)
    send = jnp.where(core == 0, gi, gd).astype(BF)
    _, chips, sub, cols = keep0_ref.shape
    for q in range(chips):
        rows = slice(q * sub, (q + 1) * sub)
        keep0_ref[0, flip(q ^ chip, chips)] = keep[rows, :cols]
        keep1_ref[flip(q ^ chip, chips), 0] = keep[rows, cols:]
    send_s[...] = send[:, cols:]
    for p in range(chips):
        rows = pl.ds(pl.multiple_of((flip(p, chips) ^ chip) * sub, sub), sub)
        group = chips // wins
        send_refs[wins + p // group][p % group * wins + flip(step, wins)] = send_s[rows]
    for slot in range(wins):

        @pl.when(step == flip(slot, wins))
        def _():
            for q in range(chips):
                send_refs[slot][flip(q ^ chip, chips)] = send[q * sub : (q + 1) * sub, :cols]

    sum_ref[pl.ds(8 + ids_ref[step], 1)] = jnp.sum(du_low.astype(F32), axis=0, keepdims=True)

    @pl.when(step == pl.num_programs(0) - 1)
    def _():
        x1 = x1_s[...]
        y_ref[...] = (x1 + (y_s[...] + vec_ref[7:8])).astype(BF)
        dyf = dy.astype(F32)
        dh = dh_s[...]
        xhat, rstd = norm_stats(x1)
        dx1 = dyf + norm_back(dh * gain, xhat, rstd)
        dx1_ref[...] = dx1
        dx1r = dx1.astype(BF)
        do_ref[...] = dot(dx1r, wo_ref[...], 1, 1).astype(BF)
        gwo_ref[...] = dot(o_ref[...], dx1r, 0, 0).astype(BF)
        sum_ref[4:5] = jnp.sum(dyf, axis=0, keepdims=True)
        sum_ref[5:6] = jnp.sum(dh * xhat, axis=0, keepdims=True)
        sum_ref[6:7] = jnp.sum(dh, axis=0, keepdims=True)
        sum_ref[7:8] = jnp.sum(dx1r.astype(F32), axis=0, keepdims=True)


def ffn(run, ids, x, o, cots, w_out, vecs, w_in, w_down, wins, chips):
    rows, d = x.shape
    ff = w_in.shape[1]
    tile = ff // wins
    sub = tile // chips
    cols = d // 2
    row = pl.BlockSpec((rows, d), lambda t, ids: (0, 0))
    square = pl.BlockSpec((d, d), lambda t, ids: (0, 0))
    keep = pl.BlockSpec((1, chips, sub, cols), lambda t, ids: (t, 0, 0, 0))
    keep_chips = pl.BlockSpec((chips, 1, sub, cols), lambda t, ids: (0, t, 0, 0))
    send = pl.BlockSpec((chips, sub, cols), lambda t, ids: (0, 0, 0))
    part = jax.ShapeDtypeStruct((wins, chips, sub, cols), BF)
    return run.call(
        functools.partial(ffn_kernel, wins=wins),
        (wins,),
        [row, row]
        + [pl.BlockSpec(cots[0].shape, lambda t, ids: (0, 0, 0))] * wins
        + [
            square,
            pl.BlockSpec(vecs.shape, lambda t, ids: (0, 0)),
            pl.BlockSpec((d, tile), lambda t, ids: (0, ids[t])),
            pl.BlockSpec((tile, d), lambda t, ids: (ids[t], 0)),
        ],
        [row, row, row, keep, keep_chips] + [send] * (2 * wins) + [square, pl.BlockSpec((16, d), lambda t, ids: (0, 0))],
        [
            jax.ShapeDtypeStruct((rows, d), BF),
            jax.ShapeDtypeStruct((rows, d), F32),
            jax.ShapeDtypeStruct((rows, d), BF),
            part,
            jax.ShapeDtypeStruct((chips, wins, sub, cols), BF),
        ]
        + [jax.ShapeDtypeStruct((chips, sub, cols), BF)] * (2 * wins)
        + [
            jax.ShapeDtypeStruct((d, d), BF),
            jax.ShapeDtypeStruct((16, d), F32),
        ],
        [
            pltpu.VMEM((rows, d), F32),
            pltpu.VMEM((rows, d), BF),
            pltpu.VMEM((d, rows), BF),
            pltpu.VMEM((rows, d), F32),
            pltpu.VMEM((rows, d), F32),
            pltpu.VMEM((rows, d), BF),
            pltpu.VMEM((tile, cols), BF),
        ],
        cost(14),
        "ffn",
        (x, o, *cots, w_out, vecs, w_in, w_down),
        ids=ids,
        mib=24,
    )


def attend_back_kernel(
    q_ref, o_ref, do_ref, k_ref, v_ref, bias_ref, lse_ref, dq_ref, dk_ref, dv_ref, dq_s
):
    step = pl.program_id(1)
    for pair in range(bias_ref.shape[0]):
        lanes = slice(pair * PW, (pair + 1) * PW)
        q2 = head_stack(q_ref[:, lanes])
        do = do_ref[:, lanes]
        do2 = head_stack(do)
        prod = head_stack(do.astype(F32) * o_ref[:, lanes].astype(F32))
        delta = dot(jnp.ones((8, PW), F32), prod, 1, 1, lax.Precision.HIGHEST)[0:1]
        k = k_ref[:, lanes]
        p = jnp.exp(biased_scores(k, q2, bias_ref[pair]) - lse_ref[0, pair])
        dp = dot(v_ref[:, lanes], do2, 1, 1)
        ds = (p * (dp - delta)).astype(BF)
        dv_ref[:, lanes] = dot(p.astype(BF), do2).astype(BF)
        dk_ref[:, lanes] = dot(ds, q2).astype(BF)
        dq_t = dot(k, ds, 0, 0)

        @pl.when(step == 0)
        def _():
            dq_s[pair] = dq_t

        @pl.when(step > 0)
        def _():
            dq_s[pair] += dq_t

        @pl.when(step == pl.num_programs(1) - 1)
        def _():
            dq_ref[:, lanes] = (head_select(dq_s[pair].T) * SCALE).astype(BF)


def attend_back(run, q, o, do, k, v, bias, lse, window, windows):
    rows, d = q.shape
    tok = rows // windows
    keys = k.shape[0]
    chunk = min(keys, 1024)
    parts = keys // chunk
    nkb = chunk // BS
    many = 2
    q_spec = pl.BlockSpec((tok, many * PW), lambda p, c: (window, p))
    k_spec = pl.BlockSpec((chunk, many * PW), lambda p, c: (c, p))
    return run.call(
        attend_back_kernel,
        (PAIRS // many, parts),
        [
            q_spec,
            q_spec,
            q_spec,
            k_spec,
            k_spec,
            pl.BlockSpec((many, nkb, 2 * tok), lambda p, c: (p, c, 0)),
            pl.BlockSpec((1, many, 1, 2 * tok), lambda p, c: (window, p, 0, 0)),
        ],
        [pl.BlockSpec((tok, many * PW), lambda p, c: (0, p)), k_spec, k_spec],
        [jax.ShapeDtypeStruct((tok, d), BF)] + [jax.ShapeDtypeStruct((keys, d), BF)] * 2,
        [pltpu.VMEM((many, PW, 2 * tok), F32)],
        cost(7.1),
        "attend_back",
        (q, o, do, k, v, bias, lse),
        mib=16,
    )


def token_back_kernel(a_ref, dk_ref, dv_ref, al_ref, dq_ref, wq_ref, wk_ref, wv_ref, keep_ref, send_ref, dal_ref, sum_ref):
    side = pl.program_id(0)

    @pl.when((side == 0) & (pl.program_id(1) == 0))
    def _():
        dq = dq_ref[...]
        dal = dot(dq, wq_ref[...], 1, 1)
        dal_ref[...] = dal
        sum_ref[0:1] = jnp.sum(dal * al_ref[...].astype(F32), axis=0, keepdims=True)
        sum_ref[1:2] = jnp.sum(dal, axis=0, keepdims=True)
        sum_ref[2:3] = jnp.sum(dq.astype(F32), axis=0, keepdims=True)
        sum_ref[3:8] = jnp.zeros((5, sum_ref.shape[1]), F32)

    dv = dv_ref[...]
    da = dot(dk_ref[...], wk_ref[...], 1, 1) + dot(dv, wv_ref[...], 1, 1)
    low = da.astype(BF).reshape(keep_ref.shape)

    @pl.when(side == 0)
    def _():
        keep_ref[...] = low

    @pl.when(side == 1)
    def _():
        send_ref[...] = low

    sum_ref[0:1] += jnp.sum(da * a_ref[0].astype(F32), axis=0, keepdims=True)
    sum_ref[1:2] += jnp.sum(da, axis=0, keepdims=True)
    sum_ref[3:4] += jnp.sum(dv.astype(F32), axis=0, keepdims=True)


def token_back(run, a, dk, dv, a_own, dq, w_qkv, tok, window):
    keys, d = dk.shape
    chips = keys // tok // 2
    size = min(chips, 4)
    half = chips // size
    tile = size * tok
    row = pl.BlockSpec((tile, d), lambda c, i: (c * half + i, 0))
    own_row = pl.BlockSpec((tok, d), lambda c, i: (0, 0))
    keep = pl.BlockSpec((size, tok, d), lambda c, i: (jnp.where(c == 0, i, half - 1), 0, 0))
    send = pl.BlockSpec((size, tok, d), lambda c, i: (jnp.where(c == 0, 0, i), 0, 0))
    part = jax.ShapeDtypeStruct((chips, tok, d), BF)
    return run.call(
        token_back_kernel,
        (2, half),
        [
            pl.BlockSpec((1, tile, d), lambda c, i: (window, c * half + i, 0)),
            row,
            row,
            pl.BlockSpec((tok, d), lambda c, i: (window, 0)),
            own_row,
            pl.BlockSpec((d, d), lambda c, i: (0, 0)),
            pl.BlockSpec((d, d), lambda c, i: (0, 1)),
            pl.BlockSpec((d, d), lambda c, i: (0, 2)),
        ],
        [keep, send, own_row, pl.BlockSpec((8, d), lambda c, i: (0, 0))],
        [part, part, jax.ShapeDtypeStruct((tok, d), F32), jax.ShapeDtypeStruct((8, d), F32)],
        [],
        cost(4.5),
        "token_back",
        (a, dk, dv, a_own, dq, w_qkv, w_qkv, w_qkv),
        mib=16,
    )


VECS = 16


def split_low(x):
    high = x.astype(BF)
    return high, (x - high.astype(F32)).astype(BF)


def qkv_grad_kernel(a_ref, al_ref, *refs):
    g_ref = refs[-1]
    windows = (len(refs) - 1) // 3
    dks, dvs, dqs = (refs[i * windows : (i + 1) * windows] for i in range(3))
    window = pl.program_id(0)
    tok = dqs[0].shape[0]

    @pl.when((window == 0) & (pl.program_id(1) == 0))
    def _():
        total = dot(al_ref[:tok], dqs[0][...], 0, 0)
        for w in range(1, windows):
            total = total + dot(al_ref[w * tok : (w + 1) * tok], dqs[w][...], 0, 0)
        g_ref[0] = total
        g_ref[1:] = jnp.zeros((2,) + g_ref.shape[1:], F32)

    a_t = a_ref[0].T
    dk, dv = dks[0][...], dvs[0][...]
    for w in range(1, windows):
        dk = jnp.where(window == w, dks[w][...], dk)
        dv = jnp.where(window == w, dvs[w][...], dv)
    g_ref[1] += dot(a_t, dk)
    g_ref[2] += dot(a_t, dv)


def qkv_grad(run, a, dks, dvs, a_own, dqs):
    windows, keys, d = a.shape
    tok = dqs[0].shape[0]
    tile = min(keys, 512)
    steps = keys // tile

    def rows_of(window):
        def where(w, i):
            return (jnp.where(w < window, 0, jnp.where(w > window, steps - 1, i)), 0)

        return pl.BlockSpec((tile, d), where)

    per_window = [rows_of(w) for w in range(windows)]
    [out] = run.call(
        qkv_grad_kernel,
        (windows, steps),
        [pl.BlockSpec((1, tile, d), lambda w, i: (w, i, 0)), pl.BlockSpec(a_own.shape, lambda w, i: (0, 0))]
        + per_window * 2
        + [pl.BlockSpec((tok, d), lambda w, i: (0, 0))] * windows,
        [pl.BlockSpec((3, d, d), lambda w, i: (0, 0, 0))],
        [jax.ShapeDtypeStruct((3, d, d), F32)],
        [],
        cost(7.5),
        "qkv_grad",
        (a, a_own, *dks, *dvs, *dqs),
        mib=14,
        mark=True,
    )
    return out


def pack_kernel(ids_ref, g_ref, gwo_ref, sum2_ref, *refs, wins, chips):
    sums, keep_ref, sends = refs[: -wins - 1], refs[-wins - 1], refs[-wins:]
    core = ids_ref[2 * wins]
    chip = ids_ref[2 * wins + 1]
    slots = wins * chips
    sub = (keep_ref.shape[0] - 2 * VECS) // slots
    per = wins // 2
    even = (g_ref[0], gwo_ref[...].astype(F32))
    odd = (g_ref[1], g_ref[2])
    for m in range(2):
        mine = jnp.where(core == 0, even[m], odd[m]).astype(BF)
        other = jnp.where(core == 0, odd[m], even[m]).astype(BF)
        for h in range(per):
            slot = ids_ref[wins + m * per + h]
            for q in range(chips):
                rows = slice((h * chips + q) * sub, (h * chips + q + 1) * sub)
                place = flip(q ^ chip, chips)
                keep_ref[pl.ds(pl.multiple_of((slot * chips + place) * sub, sub), sub)] = mine[rows]
                for to, ref in enumerate(sends):

                    @pl.when(flip(slot, wins) == to)
                    def _():
                        ref[pl.ds(pl.multiple_of(place * sub, sub), sub)] = other[rows]

    first = sums[0][0:4]
    for ref in sums[1:]:
        first = first + ref[0:4]
    high, rest = split_low(jnp.concatenate([first, sum2_ref[4:]]))
    for ref, at in ((keep_ref, slots * sub), (sends[-1], chips * sub)):
        ref[at : at + VECS] = high
        ref[at + VECS :] = rest


def pack(run, ids, g, g_out, sums1, sums2, wins, chips):
    d = g_out.shape[0]
    total = 2 * d + 2 * VECS
    size = 2 * d // wins
    shapes = [total] + [size] * (wins - 1) + [size + 2 * VECS]
    return run.call(
        functools.partial(pack_kernel, wins=wins, chips=chips),
        (1,),
        [
            pl.BlockSpec((3, d, d), lambda i, ids: (0, 0, 0)),
            pl.BlockSpec((d, d), lambda i, ids: (0, 0)),
            pl.BlockSpec((16, d), lambda i, ids: (0, 0)),
        ]
        + [pl.BlockSpec((8, d), lambda i, ids: (0, 0))] * len(sums1),
        [pl.BlockSpec((n, d), lambda i, ids: (0, 0)) for n in shapes],
        [jax.ShapeDtypeStruct((n, d), BF) for n in shapes],
        [],
        cost(2),
        "pack",
        (g, g_out, sums2, *sums1),
        ids=ids,
        mib=18,
    )


def fold_kernel(keep_ref, *refs):
    gots, (away_ref, keep_out_ref) = refs[:-2], refs[-2:]
    half = away_ref.shape[0]
    size = gots[0].shape[0]
    for i in range(0, 2 * half, min(size, half)):
        rows = min(size, half)
        got = gots[i // size][i % size : i % size + rows]
        value = (keep_ref[i : i + rows].astype(F32) + got.astype(F32)).astype(BF)
        if i < half:
            keep_out_ref[i : i + rows] = value
        else:
            away_ref[i - half : i - half + rows] = value


def fold(run, keep, gots):
    half = keep.shape[0] // 2
    whole = lambda part: pl.BlockSpec(part.shape, lambda i: (0,) * keep.ndim)
    out = jax.ShapeDtypeStruct((half,) + keep.shape[1:], BF)
    return run.call(
        fold_kernel,
        (1,),
        [whole(keep)] + [whole(got) for got in gots],
        [whole(out), whole(out)],
        [out, out],
        [],
        cost(0.5),
        "fold",
        (keep, *gots),
    )


def fold_windows_kernel(*refs):
    count = (len(refs) - 2) // 2
    away_ref, keep_ref = refs[-2:]
    half = away_ref.shape[0]
    for w in range(count):
        value = (refs[w][...].astype(F32) + refs[count + w][...].astype(F32)).astype(BF)
        rows = slice(w * value.shape[1], (w + 1) * value.shape[1])
        keep_ref[:, rows] = value[:half]
        away_ref[:, rows] = value[half:]


def fold_windows(run, keeps, gots):
    chips, tok, d = keeps[0].shape
    whole = pl.BlockSpec((chips, tok, d), lambda i: (0, 0, 0))
    shape = (chips // 2, len(keeps) * tok, d)
    return run.call(
        fold_windows_kernel,
        (1,),
        [whole] * (2 * len(keeps)),
        [pl.BlockSpec(shape, lambda i: (0, 0, 0))] * 2,
        [jax.ShapeDtypeStruct(shape, BF)] * 2,
        [],
        cost(0.5),
        "fold_windows",
        (*keeps, *gots),
        mib=12,
    )


def total_kernel(keep_ref, got_ref, out_ref):
    out_ref[...] = (keep_ref[...].astype(F32) + got_ref[...].astype(F32)).astype(BF)


def total(run, keep, got):
    spec = pl.BlockSpec(keep.shape, lambda i: (0,) * keep.ndim)
    [out] = run.call(
        total_kernel,
        (1,),
        [spec, spec],
        [spec],
        [jax.ShapeDtypeStruct(keep.shape, BF)],
        [],
        cost(0.2),
        "total",
        (keep, got),
    )
    return out


def add_vecs(keep_ref, gots):
    rows = keep_ref.shape[0] - 2 * VECS
    size = rows // len(gots)
    both = [keep_ref[i * size : (i + 1) * size].astype(F32) + got[:size].astype(F32) for i, got in enumerate(gots)]
    mine = keep_ref[rows : rows + VECS].astype(F32) + keep_ref[rows + VECS :].astype(F32)
    other = gots[-1][size : size + VECS].astype(F32) + gots[-1][size + VECS :].astype(F32)
    return both[0] if len(both) == 1 else jnp.concatenate(both), mine + other


def fold_vecs_kernel(keep_ref, *refs):
    gots, (away_out_ref, keep_out_ref) = refs[:-2], refs[-2:]
    both, sums = add_vecs(keep_ref, gots)
    cut = both.shape[0] // 2
    high, rest = split_low(sums)
    for ref, part in ((away_out_ref, both[cut:]), (keep_out_ref, both[:cut])):
        ref[:cut] = part.astype(BF)
        ref[cut : cut + VECS] = high
        ref[cut + VECS :] = rest


def last_vecs_kernel(keep_ref, got_ref, out_ref, sum_ref):
    both, sums = add_vecs(keep_ref, [got_ref])
    out_ref[...] = both.astype(BF)
    sum_ref[...] = sums


def fold_vecs(run, keep, gots, last):
    rows, d = keep.shape
    spec = pl.BlockSpec((rows, d), lambda i: (0, 0))
    body = rows - 2 * VECS
    if last:
        shapes = [((body, d), BF), ((VECS, d), F32)]
    else:
        shapes = [((body // 2 + 2 * VECS, d), BF)] * 2

    return run.call(
        last_vecs_kernel if last else fold_vecs_kernel,
        (1,),
        [spec] + [pl.BlockSpec(got.shape, lambda i: (0, 0)) for got in gots],
        [pl.BlockSpec(shape, lambda i: (0, 0)) for shape, _ in shapes],
        [jax.ShapeDtypeStruct(*shape) for shape in shapes],
        [],
        cost(0.6),
        "fold_vecs",
        (keep, *gots),
    )


def gather_kernel(*refs):
    size = refs[0].shape[0]
    for i, ref in enumerate(refs[:-1]):
        refs[-1][i * size : (i + 1) * size] = ref[...]


def gather_parts(run, parts):
    size, tok, d = parts[0].shape
    spec = pl.BlockSpec((size, tok, d), lambda i: (0, 0, 0))
    shape = (size * len(parts), tok, d)
    [out] = run.call(
        gather_kernel,
        (1,),
        [spec] * len(parts),
        [pl.BlockSpec(shape, lambda i: (0, 0, 0))],
        [jax.ShapeDtypeStruct(shape, BF)],
        [],
        cost(0.3),
        "gather_parts",
        parts,
    )
    return out


def input_back_kernel(x_ref, dx1_ref, vec_ref, keep_ref, got_ref, *refs):
    g_ref = refs[-1]
    tok = refs[0].shape[0]
    for w, own_ref in enumerate(refs[:-1]):
        rows = slice(w * tok, (w + 1) * tok)
        xhat, rstd = norm_stats(x_ref[rows].astype(F32))
        da = keep_ref[0, rows].astype(F32) + got_ref[0, rows].astype(F32) + own_ref[...]
        g_ref[rows] = (dx1_ref[rows] + norm_back(da * vec_ref[0:1], xhat, rstd)).astype(BF)


def input_back(run, x, dx1, vecs, keep, got, owns):
    rows, d = x.shape
    row = pl.BlockSpec((rows, d), lambda i: (0, 0))
    first = pl.BlockSpec((1, rows, d), lambda i: (0, 0, 0))
    [out] = run.call(
        input_back_kernel,
        (1,),
        [row, row, pl.BlockSpec(vecs.shape, lambda i: (0, 0)), first, first]
        + [pl.BlockSpec(own.shape, lambda i: (0, 0)) for own in owns],
        [row],
        [jax.ShapeDtypeStruct((rows, d), BF)],
        [],
        cost(1.4),
        "input_back",
        (x, dx1, vecs, keep, got, *owns),
        mark=True,
    )
    return out


def slot_parts(refs):
    size = refs[0].shape[0]
    return [(ref, i) for ref in refs for i in range(size)]


def unpack_ffn_kernel(ids_ref, *refs, wins, count, chips, part, parts):
    owns, gots = refs[:count], refs[count : 2 * count]
    down_ref, in_ref, down_s, in_s, sems = refs[-5:]
    even = ids_ref[2 * wins] == 0
    chip, win = ids_ref[2 * wins + 1], ids_ref[2 * wins + 2]
    sub, cols = owns[0].shape[1:]
    tile = chips * sub
    owns, gots = slot_parts(owns), slot_parts(gots)
    copies = []
    for slot in range(wins):
        for p in range(chips):
            at = p * wins + slot if part else slot * chips + p
            (own_ref, i), (got_ref, _) = owns[at], gots[at]
            own = own_ref[i].astype(F32)
            got = got_ref[i].astype(F32)
            rows = pl.ds(pl.multiple_of((flip(p, chips) ^ chip) * sub, sub), sub)
            down_s[slot, rows] = jnp.where(even, own, got)
            in_s[slot, rows] = jnp.where(even, got, own)
        down_row = pl.multiple_of((win ^ flip(slot, wins)) * tile, tile)
        in_col = pl.multiple_of((win ^ slot) * (parts * cols) + part * cols, cols)
        for i, (src, dst) in enumerate(
            (
                (down_s, down_ref.at[pl.ds(down_row, tile), part * cols : (part + 1) * cols]),
                (in_s, in_ref.at[:, pl.ds(in_col, cols)]),
            )
        ):
            copies.append(pltpu.make_async_copy(src.at[slot], dst, sems.at[i, slot]))
            copies[-1].start()
    for copy in copies:
        copy.wait()


def unpack_ffn(run, ids, owns, gots, chips, wins, part, parts, before):
    _, sub, cols = owns[0].shape
    tile = chips * sub
    d = parts * cols
    whole = [pl.BlockSpec(own.shape, lambda i, ids: (0, 0, 0)) for own in owns]
    far = pl.BlockSpec(memory_space=pltpu.HBM)
    return run.call(
        functools.partial(unpack_ffn_kernel, wins=wins, count=len(owns), chips=chips, part=part, parts=parts),
        (1,),
        whole * 2 + [far] * len(before),
        [far, far],
        [
            pltpu.HBM((wins * tile, d), F32),
            pltpu.HBM((d, wins * tile), F32),
        ],
        [
            pltpu.VMEM((wins, tile, cols), F32),
            pltpu.VMEM((wins, tile, cols), F32),
            pltpu.SemaphoreType.DMA((2, wins)),
        ],
        cost(4.6),
        "unpack_ffn",
        (*owns, *gots, *before),
        ids=ids,
        alias={2 * len(owns): 0, 2 * len(owns) + 1: 1} if before else None,
        mib=22,
        mark=True,
    )


def unpack_qkvo_kernel(ids_ref, *refs, wins, count, chips):
    owns, gots = refs[:count], refs[count : 2 * count]
    qkv_ref, out_ref, stage, sems = refs[-4:]
    even = ids_ref[2 * wins] == 0
    chip, win = ids_ref[2 * wins + 1], ids_ref[2 * wins + 2]
    sub, d = owns[0].shape[1:]
    per = wins // 2
    size = chips * sub
    owns, gots = slot_parts(owns), slot_parts(gots)
    copies = []
    for slot in range(wins):
        for side in range(2):
            for p in range(chips):
                (own_ref, i), (got_ref, _) = owns[slot * chips + p], gots[slot * chips + p]
                own, got = own_ref[i], got_ref[i]
                value = (jnp.where(even, got, own) if side else jnp.where(even, own, got)).astype(F32)
                rows = pl.ds(pl.multiple_of((flip(p, chips) ^ chip) * sub, sub), sub)
                stage[slot, side, rows] = value
            tile = win ^ (slot if side else flip(slot, wins))
            rows = pl.ds(pl.multiple_of((tile % per) * size, size), size)
            high = qkv_ref.at[rows, 2 * d : 3 * d] if side else out_ref.at[rows]
            low = qkv_ref.at[rows, side * d : (side + 1) * d]
            for flag, dst in ((tile < per, low), (tile >= per, high)):
                copy = pltpu.make_async_copy(stage.at[slot, side], dst, sems.at[slot, side])
                copies.append((flag, copy))
                pl.when(flag)(copy.start)
    for flag, copy in copies:
        pl.when(flag)(copy.wait)


def unpack_qkvo(run, ids, owns, gots, chips, wins):
    _, sub, d = owns[0].shape
    whole = [pl.BlockSpec(own.shape, lambda i, ids: (0, 0, 0)) for own in owns]
    far = pl.BlockSpec(memory_space=pltpu.HBM)
    return run.call(
        functools.partial(unpack_qkvo_kernel, wins=wins, count=len(owns), chips=chips),
        (1,),
        whole * 2,
        [far, far],
        [pltpu.HBM((d, 3 * d), F32), pltpu.HBM((d, d), F32)],
        [pltpu.VMEM((wins, 2, chips * sub, d), F32), pltpu.SemaphoreType.DMA((wins, 2))],
        cost(5),
        "unpack_qkvo",
        (*owns, *gots),
        ids=ids,
        mib=22,
        mark=True,
    )


def copy_kernel(x_ref, out_ref):
    out_ref[...] = x_ref[...]


def copied(run, x):
    spec = pl.BlockSpec(x.shape, lambda i: (0,) * x.ndim)
    [out] = run.call(
        copy_kernel, (1,), [spec], [spec], [jax.ShapeDtypeStruct(x.shape, x.dtype)], [], cost(0.5), "copied", (x,)
    )
    return out


def place_kernel(ids_ref, species_ref, *refs, wins):
    out_ref = refs[-1]
    count = refs[0].shape[0]
    me = ids_ref[2 * wins + 2]
    out_ref[...] = jnp.zeros_like(out_ref)
    for s, ref in enumerate(refs[:-1]):
        for j in range(count):
            group, rank = slot_of(species_ref, (me ^ s) * count + j)

            @pl.when(group == me)
            def _():
                out_ref[jnp.minimum(rank, out_ref.shape[0] - 1)] = ref[j]


def place_rows(run, ids, species, parts, slots, wins):
    count, tok, d = parts[0].shape
    spec = pl.BlockSpec((count, tok, d), lambda i, *_: (0, 0, 0))
    [out] = run.call(
        functools.partial(place_kernel, wins=wins),
        (1,),
        [spec] * len(parts),
        [pl.BlockSpec((slots, tok, d), lambda i, *_: (0, 0, 0))],
        [jax.ShapeDtypeStruct((slots, tok, d), BF)],
        [],
        cost(1.7),
        "place_rows",
        parts,
        ids=(ids, species),
        mark=True,
    )
    return out


def swap(x, partner):
    wins, blks = lax.axis_size("win"), lax.axis_size("blk")
    perm = []
    for w in range(wins):
        for b in range(blks):
            pw, pb = partner(w, b)
            perm.append((w * blks + b, pw * blks + pb))
    return lax.ppermute(x, BOTH, perm)


def core_swap(x):
    return swap(x, lambda w, b: (w, b ^ 1))


def chip_swap(x, s):
    return swap(x, lambda w, b: (w, b ^ (2 * s)))


def win_swap(x, s):
    return swap(x, lambda w, b: (w ^ s, b))


def win_turns(wins):
    bits = (wins - 1).bit_length()
    even = [1 << i for i in range(bits)]
    return list(zip(even, even[::-1]))


def turn_swap(x, turn):
    even, odd = turn
    return swap(x, lambda w, b: (w ^ (odd if b % 2 else even), b))


def exchange_ids(wins, blks):
    rows = []
    for w in range(wins):
        for b in range(blks):
            core, chip = b % 2, b // 2
            tiles = [w ^ (i if core else flip(i, wins)) for i in range(wins)]
            rows.append(tiles + [tiles.index(t) for t in range(wins)] + [core, chip, w, b])
    me = lax.axis_index("win") * blks + lax.axis_index("blk")
    return lax.dynamic_index_in_dim(jnp.asarray(np.array(rows, np.int32)), me, 0, keepdims=False)


def stacked(rows, width):
    parts = []
    for row in rows:
        parts += [row[i : i + width] for i in range(0, row.shape[0], width)]
    count = -(-len(parts) // 8) * 8
    index = lax.broadcasted_iota(jnp.int32, (count, width), 0)
    out = jnp.zeros((count, width), F32)
    for r, part in enumerate(parts):
        out = jnp.where(index == r, part[None, :], out)
    return out


def turns(wins, chips):
    def chip_turn(s):
        return lambda x: chip_swap(x, s)

    out = [functools.partial(turn_swap, turn=turn) for turn in win_turns(wins)]
    bits = (chips - 1).bit_length()
    return out + [chip_turn(1 << i) for i in range(bits)]


class Sum:
    def __init__(self, run, keep, sends, swaps, chip_turns):
        self.run, self.keep, self.swaps, self.chip_turns = run, keep, swaps, chip_turns
        self.turn, self.x = 0, None
        self.got = [core_swap(send) for send in sends]

    def fold(self):
        return fold(self.run, self.keep, self.got)

    def total(self):
        return total(self.run, self.keep, self.got[0])

    def step(self):
        if self.x is None and self.turn < len(self.swaps):
            away, self.keep = self.fold()
            self.got = [self.swaps[self.turn](away)]
            self.turn += 1
            return
        if self.x is None:
            self.x, self.owns, self.gots = self.total(), [], []
        else:
            [arrived] = self.got
            if self.turn == 0:
                arrived = copied(self.run, arrived)
            if self.turn == 0:
                self.own(arrived)
            else:
                self.x = gather_parts(self.run, [self.x, arrived])
        self.turn -= 1
        if self.turn >= 0:
            self.got = [self.swaps[self.turn](self.x)]
        if self.turn == 0:
            self.own(self.x)

    def own(self, part):
        self.owns.append(part)
        self.gots.append(core_swap(part))


class TokenSum(Sum):
    def fold(self):
        return fold_windows(self.run, self.keep, self.got) if self.turn == 0 else fold(self.run, self.keep, self.got)


class VecSum(Sum):
    def fold(self):
        return fold_vecs(self.run, self.keep, self.got, False)

    def total(self):
        x, sums = fold_vecs(self.run, self.keep, self.got, True)
        self.sums = jnp.where(lax.axis_index("blk") % 2 == 0, sums, core_swap(sums))
        return x[None]


ORDER = (
    "b0", "1", "0", "bb", "t0", "tt", "0", "weight", "pack", "1", "0", "T", "Q", "0", "Q", "r", "0",
    "1", "Q", "T", "1", "0", "Q", "1", "uT", "place", "1", "0", "Q", "1", "0", "Q", "v", "Q", "0", "1",
    "Q", "u0", "1", "Q", "uQ", "u1",
)


def schedule(more):
    steps = list(ORDER)
    for name in ("0", "1", "Q", "T") if more else ():
        places = [i for i, step in enumerate(steps) if step == name]
        if name in "01Q":
            steps[places[-1] : places[-1]] = [name] * more
            steps[places[3] : places[3]] = [name] * more
        else:
            steps[places[1] : places[1]] = [name] * more
    return steps


def per_device(
    inputs,
    species,
    random_blocks,
    qkv_weight,
    q_bias,
    v_bias,
    out_weight,
    out_bias,
    norm1_gain,
    norm1_bias,
    norm2_gain,
    norm2_bias,
    ffn_in_weight,
    ffn_in_bias,
    ffn_out_weight,
    ffn_out_bias,
    cotangent,
):
    count, tok, d = inputs.shape
    rows = count * tok
    wins, blks = lax.axis_size("win"), lax.axis_size("blk")
    chips = blks // 2
    ids = exchange_ids(wins, blks)
    run = Order()
    vecs = stacked(
        [norm1_gain, norm1_bias, q_bias, v_bias, out_bias, norm2_gain, norm2_bias, ffn_out_bias, ffn_in_bias], d
    )
    swaps = turns(wins, chips)
    chip_bits = [1 << i for i in range((chips - 1).bit_length())]

    first, *later = chip_bits[::-1]
    parts = [[row, chip_swap(row, first)] for row in (inputs[w : w + 1] for w in range(count))]
    x = inputs.reshape(rows, d)
    a_own, q, bias, *cots = query_rows(
        run, ids, species, random_blocks.transpose(2, 0, 1), x, vecs, qkv_weight, cotangent, count, wins, blks
    )
    cots = [cots[0]] + [win_swap(cots[s], s) for s in range(1, wins)]
    parts[0][1] = copied(run, parts[0][1])
    for s in later:
        parts = [window + [chip_swap(part, s) for part in window] for window in parts]
    mine = [gather_parts(run, parts[w]) for w in range(count)]
    theirs = [core_swap(part) for part in mine]
    keys, before, a = [], (), ()
    for w in range(count):
        a, k, v = kv_rows(run, mine[w], theirs[w], vecs, qkv_weight, w, count, a)
        a = (a,)
        keys.append((k, v))
        before = attend(run, q, k, v, bias, w, count, before)
    [a] = a
    o, lse = before
    y, dx1, do, keep0, keep1, *sends, g_out, sums2 = ffn(
        run, ids, x, o, cots, out_weight, vecs, ffn_in_weight, ffn_out_weight, wins, chips
    )
    slotted = lambda part: part.reshape(wins * chips, part.shape[2], part.shape[3])
    bits = len(chip_bits)
    f0 = Sum(run, slotted(keep0), sends[:wins], swaps, bits)
    f1 = Sum(run, slotted(keep1), sends[wins:], swaps[-bits:] + swaps[:-bits], bits)
    got = {"back": [], "t": []}

    def back(w):
        got["back"].append(attend_back(run, q, o, do, *keys[w], bias, lse, w, count))

    def token(w):
        dq, dk, dv = got["back"][w]
        got["t"].append(token_back(run, a, dk, dv, a_own, dq, qkv_weight, tok, w))
        if w == 0:
            got["T"] = TokenSum(run, [], [], swaps[-bits:], bits)
        part = got["T"]
        part.keep.append(got["t"][w][0])
        part.got.append(core_swap(got["t"][w][1]))

    def weight():
        dqs, dks, dvs = zip(*got["back"])
        got["g"] = qkv_grad(run, a, dks, dvs, a_own, dqs)

    def packed():
        keep, *sends = pack(run, ids, got["g"], g_out, [part[3] for part in got["t"]], sums2, wins, chips)
        got["Q"] = VecSum(run, keep, sends, swaps, bits)

    def send_result():
        own = copied(run, y.reshape(count, tok, d))
        got["y"] = [own] + [win_swap(own, s) for s in range(1, wins)]

    def place():
        got["result"] = place_rows(run, ids, species, got["y"], cotangent.shape[0], wins)

    def tokens_end():
        part, owns = got["T"], [part[2] for part in got["t"]]
        got["input"] = input_back(run, x, dx1, vecs, part.keep, part.got[0], owns).reshape(count, tok, d)

    def unpack(part, piece):
        got["ffn"] = unpack_ffn(run, ids, piece.owns, piece.gots, chips, wins, part, 2, got.get("ffn", ()))

    def vectors():
        sums = got["Q"].sums
        gain = (sums[0] - norm1_bias * sums[1]) / norm1_gain
        got["vectors"] = [gain] + [sums[i] for i in range(1, 8)] + [sums[8 : 8 + wins].reshape(-1)]
        run.touch(*got["vectors"])

    def unpack_last():
        got["qkvo"] = unpack_qkvo(run, ids, got["Q"].owns, got["Q"].gots, chips, wins)

    todo = {
        "b0": lambda: back(0),
        "bb": lambda: [back(w) for w in range(1, count)],
        "t0": lambda: token(0),
        "tt": lambda: [token(w) for w in range(1, count)],
        "T": lambda: got["T"].step(),
        "r": send_result,
        "place": place,
        "weight": weight,
        "pack": packed,
        "0": f0.step,
        "1": f1.step,
        "Q": lambda: got["Q"].step(),
        "v": vectors,
        "u0": lambda: unpack(0, f0),
        "u1": lambda: unpack(1, f1),
        "uQ": unpack_last,
        "uT": tokens_end,
    }
    for name in schedule(len(swaps) - 4):
        todo[name]()
    ffn_out_grad, ffn_in_grad = got["ffn"]
    qkv_grad_all, out_grad = got["qkvo"]
    result, input_grad = got["result"], got["input"]
    gain1, shift1, q_grad, v_grad, down, gain2, shift2, out_bias_grad, hidden = got["vectors"]
    return (
        result,
        input_grad,
        qkv_grad_all,
        q_grad,
        v_grad,
        out_grad,
        out_bias_grad,
        gain1,
        shift1,
        gain2,
        shift2,
        ffn_in_grad,
        hidden,
        ffn_out_grad,
        down,
    )


def solution(mesh):
    split = P("win", "blk", None)
    return jax.shard_map(
        per_device,
        mesh=mesh,
        in_specs=(split,) + (P(),) * 15 + (split,),
        out_specs=(split, split) + (P(),) * 13,
        check_vma=False,
    )
```

```python
import functools

import jax
import jax.numpy as jnp
import numpy as np
from jax import lax
from jax.experimental import pallas as pl
from jax.experimental.pallas import tpu as pltpu
from jax.sharding import PartitionSpec as P

HEADS = 12
HD = 64
BS = 64
PAIRS = HEADS // 2
PW = 2 * HD

EPS = 1e-05
SCALE = 0.125
MASKED = -1e30
BF = jnp.bfloat16
F32 = jnp.float32
BOTH = ("win", "blk")
MIB = 1024 * 1024


def dot(a, b, ca=1, cb=0, precision=None):
    return lax.dot_general(
        a, b, (((ca,), (cb,)), ((), ())), precision=precision, preferred_element_type=F32
    )


def flip(i, size):
    bits = (size - 1).bit_length()
    out = 0
    for k in range(bits):
        out = out | (((i >> k) & 1) << (bits - 1 - k))
    return out


def params(grid_dims, mib):
    return pltpu.CompilerParams(
        dimension_semantics=("arbitrary",) * grid_dims, vmem_limit_bytes=mib * MIB
    )


def cost(us):
    return pl.CostEstimate(flops=1, bytes_accessed=int(us * 0.1 * 3.6e6), transcendentals=0)


def norm_stats(x):
    width = x.shape[-1]
    mean = jnp.sum(x, axis=-1, keepdims=True) * (1.0 / width)
    c = x - mean
    var = jnp.sum(c * c, axis=-1, keepdims=True) * (1.0 / width)
    rstd = lax.rsqrt(var + EPS)
    return c * rstd, rstd


def norm_back(g, xhat, rstd):
    width = g.shape[-1]
    m1 = jnp.sum(g, axis=-1, keepdims=True) * (1.0 / width)
    m2 = jnp.sum(g * xhat, axis=-1, keepdims=True) * (1.0 / width)
    return rstd * (g - m1 - xhat * m2)


class Order:
    def __init__(self):
        self.last = None
        self.touched = []

    def touch(self, *arrays):
        self.touched += arrays

    def call(
        self, kernel, grid, in_specs, out_specs, out_shape, scratch, estimate, name, args, ids=None, alias=None, mib=8, mark=False
    ):
        scalars = [] if ids is None else list(ids) if isinstance(ids, tuple) else [ids]
        after = [] if self.last is None or any(self.last is arg for arg in args) else [self.last]
        after += self.touched
        count, outs = len(scalars) + len(in_specs), len(out_specs)
        if mark:
            out_specs = list(out_specs) + [pl.BlockSpec((8, 128), lambda *_: (0, 0))]
            out_shape = list(out_shape) + [jax.ShapeDtypeStruct((8, 128), F32)]

        def body(*refs):
            at = count + len(after)
            if mark:
                refs[at + outs][...] = jnp.zeros((8, 128), F32)
            kernel(*refs[:count], *refs[at : at + outs], *refs[at + len(out_specs) :])

        out = pl.pallas_call(
            body,
            grid_spec=pltpu.PrefetchScalarGridSpec(
                num_scalar_prefetch=len(scalars),
                grid=grid,
                in_specs=list(in_specs) + [pl.BlockSpec(memory_space=pl.ANY)] * len(after),
                out_specs=out_specs,
                scratch_shapes=scratch,
            ),
            out_shape=out_shape,
            input_output_aliases={len(scalars) + i: o for i, o in (alias or {}).items()},
            compiler_params=params(len(grid), mib),
            cost_estimate=estimate,
            name=name,
        )(*scalars, *args, *after)
        self.last = min(out, key=lambda part: part.size * part.dtype.itemsize)
        self.touched = []
        return out[:outs]


def slot_of(species_ref, w):
    group = species_ref[w]
    rank = jnp.int32(0)
    for other in range(species_ref.shape[0]):
        rank = rank + ((species_ref[other] == group) & (other < w)).astype(jnp.int32)
    return group, rank


def query_kernel(
    ids_ref, species_ref, picks_ref, x_ref, vec_ref, w_ref, cot_ref, a_ref, q_ref, bias_ref, *part_refs, wins, blks
):
    count, tok, _ = part_refs[0].shape
    me, blk = ids_ref[2 * wins + 2], ids_ref[2 * wins + 3]
    for s, ref in enumerate(part_refs):
        for j in range(count):
            group, rank = slot_of(species_ref, (me ^ s) * count + j)
            here = group == me
            row = cot_ref[jnp.minimum(rank, cot_ref.shape[0] - 1)]
            ref[j] = jnp.where(here, row, jnp.zeros_like(row))

    xhat, _ = norm_stats(x_ref[...].astype(F32))
    a = (xhat * vec_ref[0:1] + vec_ref[1:2]).astype(BF)
    a_ref[...] = a
    q = (dot(a, w_ref[...]) + vec_ref[2:3]).astype(BF)
    q_ref[...] = (q.astype(F32) * SCALE).astype(BF)

    per, chips = tok // BS, blks // 2
    total = blks * per
    shape = bias_ref.shape[1:]
    place = lax.broadcasted_iota(jnp.int32, shape, 0)
    lane = lax.broadcasted_iota(jnp.int32, shape, 1)
    j = (lane % tok) // BS
    group = place // per
    owner = blk ^ (2 * flip(group % chips, chips) + group // chips)
    kb = owner * per + place % per
    i = blk * per + j
    one, zero = jnp.float32(1), jnp.float32(0)

    def hits(flag):
        return jnp.where(flag, one, zero)

    near = hits(kb == i - 1) + hits(kb == i) + hits(kb == i + 1)
    near = near + hits((kb == 0) & (i >= 2)) + hits((kb == total - 1) & (i <= total - 3))
    rand = picks_ref.shape[0]
    for pair in range(PAIRS):
        m = near
        for r in range(rand):
            picked = jnp.zeros(shape, jnp.int32)
            for h in range(2):
                for b in range(per):
                    value = picks_ref[r, blk * per + b, 2 * pair + h]
                    picked = jnp.where(lane // BS == h * per + b, value, picked)
            m = m + hits(picked == kb)
        m = jnp.where((i == 0) | (i == total - 1), one, m)
        bias_ref[pair] = jnp.where(m > 0, jnp.log(jnp.maximum(m, one)), MASKED)


def query_rows(run, ids, species, picks, x, vecs, w_qkv, cot, count, wins, blks):
    rows, d = x.shape
    slots, tok, _ = cot.shape
    row = pl.BlockSpec((rows, d), lambda i, *_: (0, 0))
    part = pl.BlockSpec((count, tok, d), lambda i, *_: (0, 0, 0))
    keys = (PAIRS, blks * (tok // BS), 2 * tok)
    return run.call(
        functools.partial(query_kernel, wins=wins, blks=blks),
        (1,),
        [
            row,
            pl.BlockSpec(vecs.shape, lambda i, *_: (0, 0)),
            pl.BlockSpec((d, d), lambda i, *_: (0, 0)),
            pl.BlockSpec((slots, tok, d), lambda i, *_: (0, 0, 0)),
        ],
        [row, row, pl.BlockSpec(keys, lambda i, *_: (0, 0, 0))] + [part] * wins,
        [jax.ShapeDtypeStruct((rows, d), BF)] * 2
        + [jax.ShapeDtypeStruct(keys, F32)]
        + [jax.ShapeDtypeStruct((count, tok, d), BF)] * wins,
        [],
        cost(1.7),
        "query_rows",
        (x, vecs, w_qkv, cot),
        ids=(ids, species, picks),
        mib=16,
    )


def kv_kernel(x0_ref, x1_ref, vec_ref, wk_ref, wv_ref, *refs):
    a_ref, k_ref, v_ref = refs[-3:]
    step, half = pl.program_id(0), pl.num_programs(0) // 2
    groups, tok, d = x0_ref.shape
    x = jnp.where(step < half, x0_ref[...], x1_ref[...]).reshape(groups * tok, d)
    xhat, _ = norm_stats(x.astype(F32))
    a = (xhat * vec_ref[0:1] + vec_ref[1:2]).astype(BF)
    a_ref[0] = a
    k_ref[...] = dot(a, wk_ref[...]).astype(BF)
    v_ref[...] = (dot(a, wv_ref[...]) + vec_ref[3:4]).astype(BF)


def kv_rows(run, mine, theirs, vecs, w_qkv, window, windows, before):
    chips, tok, d = mine.shape
    size = min(chips, 4)
    half = chips // size
    rows = 2 * chips * tok
    tile = size * tok
    row = pl.BlockSpec((tile, d), lambda i: (i, 0))
    return run.call(
        kv_kernel,
        (2 * half,),
        [
            pl.BlockSpec((size, tok, d), lambda i: (jnp.minimum(i, half - 1), 0, 0)),
            pl.BlockSpec((size, tok, d), lambda i: (jnp.maximum(i - half, 0), 0, 0)),
            pl.BlockSpec(vecs.shape, lambda i: (0, 0)),
            pl.BlockSpec((d, d), lambda i: (0, 1)),
            pl.BlockSpec((d, d), lambda i: (0, 2)),
        ]
        + [pl.BlockSpec(memory_space=pl.ANY)] * len(before),
        [pl.BlockSpec((1, tile, d), lambda i: (window, i, 0)), row, row],
        [jax.ShapeDtypeStruct((windows, rows, d), BF)] + [jax.ShapeDtypeStruct((rows, d), BF)] * 2,
        [],
        cost(3.7),
        "kv_rows",
        (mine, theirs, vecs, w_qkv, w_qkv, *before),
        alias={5: 0} if before else None,
        mib=14,
    )


def head_stack(pair):
    lane = lax.broadcasted_iota(jnp.int32, pair.shape, 1)
    zero = jnp.zeros_like(pair)
    return jnp.concatenate([jnp.where(lane < HD, pair, zero), jnp.where(lane < HD, zero, pair)], axis=0)


def head_select(both):
    rows = both.shape[0] // 2
    lane = lax.broadcasted_iota(jnp.int32, (rows, both.shape[1]), 1)
    return jnp.where(lane < HD, both[:rows], both[rows:])


def biased_scores(k, q2, bias):
    s = dot(k, q2, 1, 1)
    keys, lanes = s.shape
    return (s.reshape(keys // BS, BS, lanes) + bias[:, None, :]).reshape(keys, lanes)


def attend_kernel(q_ref, k_ref, v_ref, bias_ref, *refs):
    o_ref, lse_ref = refs[-2:]
    for pair in range(bias_ref.shape[0]):
        lanes = slice(pair * PW, (pair + 1) * PW)
        q2 = head_stack(q_ref[:, lanes])
        s = biased_scores(k_ref[:, lanes], q2, bias_ref[pair])
        top = jnp.max(s, axis=0, keepdims=True)
        e = jnp.exp(s - top)
        total = jnp.sum(e, axis=0, keepdims=True)
        o_t = dot(v_ref[:, lanes], e.astype(BF), 0, 0) * (1.0 / total)
        o_ref[:, lanes] = head_select(o_t.T).astype(BF)
        lse_ref[0, pair] = top + jnp.log(total)


def attend(run, q, k, v, bias, window, windows, before):
    rows, d = q.shape
    tok = rows // windows
    keys = k.shape[0]
    nkb = keys // BS
    many = 2 if keys <= 1024 else 1
    q_spec = pl.BlockSpec((tok, many * PW), lambda p: (window, p))
    k_spec = pl.BlockSpec((keys, many * PW), lambda p: (0, p))
    return run.call(
        attend_kernel,
        (PAIRS // many,),
        [q_spec, k_spec, k_spec, pl.BlockSpec((many, nkb, 2 * tok), lambda p: (p, 0, 0))]
        + [pl.BlockSpec(memory_space=pl.ANY)] * len(before),
        [q_spec, pl.BlockSpec((1, many, 1, 2 * tok), lambda p: (window, p, 0, 0))],
        [
            jax.ShapeDtypeStruct((rows, d), BF),
            jax.ShapeDtypeStruct((windows, PAIRS, 1, 2 * tok), F32),
        ],
        [],
        cost(6.6),
        "attend",
        (q, k, v, bias, *before),
        alias={4: 0, 5: 1} if before else None,
        mib=6 + keys // 256,
    )


def ffn_kernel(
    ids_ref,
    x_ref,
    o_ref,
    *refs,
    wins,
):
    ends = (wins, wins + 9, 3 * wins + 9)
    cots, head, sends, tail = (refs[a:b] for a, b in zip((0,) + ends, ends + (None,)))
    ffn_body(ids_ref, x_ref, o_ref, cots, *head, sends, *tail, wins=wins)


def ffn_body(
    ids_ref,
    x_ref,
    o_ref,
    cot_refs,
    wo_ref,
    vec_ref,
    wi_ref,
    wd_ref,
    y_ref,
    dx1_ref,
    do_ref,
    keep0_ref,
    keep1_ref,
    send_refs,
    gwo_ref,
    sum_ref,
    x1_s,
    h2_s,
    h2t_s,
    y_s,
    dh_s,
    dy_s,
    send_s,
    *,
    wins,
):
    step = pl.program_id(0)
    core = ids_ref[2 * wins]
    chip = ids_ref[2 * wins + 1]
    gain = vec_ref[5:6]

    @pl.when(step == 0)
    def _():
        x1 = x_ref[...].astype(F32) + (dot(o_ref[...], wo_ref[...]) + vec_ref[4:5])
        x1_s[...] = x1
        xhat, _ = norm_stats(x1)
        h2 = xhat * gain + vec_ref[6:7]
        h2_s[...] = h2.astype(BF)
        h2t_s[...] = h2.T.astype(BF)
        y_s[...] = jnp.zeros_like(y_s)
        dh_s[...] = jnp.zeros_like(dh_s)
        sum_ref[...] = jnp.zeros_like(sum_ref)
        total = cot_refs[0][...].astype(F32)
        for ref in cot_refs[1:]:
            total = total + ref[...].astype(F32)
        dy_s[...] = total.reshape(dy_s.shape).astype(BF)

    dy = dy_s[...]
    wi = wi_ref[...]
    wd = wd_ref[...]
    u = dot(h2_s[...], wi) + vec_ref[pl.ds(8 + ids_ref[step], 1)]
    half = 0.5 * (1.0 + lax.erf(u * 0.7071067811865476))
    f = (u * half).astype(BF)
    slope = half + u * (jnp.exp(u * u * -0.5) * 0.3989422804014327)
    du = dot(dy, wd, 1, 1) * slope
    du_low = du.astype(BF)
    y_s[...] += dot(f, wd)
    dh_s[...] += dot(du_low, wi, 1, 1)
    gd = dot(f, dy, 0, 0)
    gi = dot(h2t_s[...], du_low)
    keep = jnp.where(core == 0, gd, gi).astype(BF)
    send = jnp.where(core == 0, gi, gd).astype(BF)
    _, chips, sub, cols = keep0_ref.shape
    for q in range(chips):
        rows = slice(q * sub, (q + 1) * sub)
        keep0_ref[0, flip(q ^ chip, chips)] = keep[rows, :cols]
        keep1_ref[flip(q ^ chip, chips), 0] = keep[rows, cols:]
    send_s[...] = send[:, cols:]
    for p in range(chips):
        rows = pl.ds(pl.multiple_of((flip(p, chips) ^ chip) * sub, sub), sub)
        group = chips // wins
        send_refs[wins + p // group][p % group * wins + flip(step, wins)] = send_s[rows]
    for slot in range(wins):

        @pl.when(step == flip(slot, wins))
        def _():
            for q in range(chips):
                send_refs[slot][flip(q ^ chip, chips)] = send[q * sub : (q + 1) * sub, :cols]

    sum_ref[pl.ds(8 + ids_ref[step], 1)] = jnp.sum(du_low.astype(F32), axis=0, keepdims=True)

    @pl.when(step == pl.num_programs(0) - 1)
    def _():
        x1 = x1_s[...]
        y_ref[...] = (x1 + (y_s[...] + vec_ref[7:8])).astype(BF)
        dyf = dy.astype(F32)
        dh = dh_s[...]
        xhat, rstd = norm_stats(x1)
        dx1 = dyf + norm_back(dh * gain, xhat, rstd)
        dx1_ref[...] = dx1
        dx1r = dx1.astype(BF)
        do_ref[...] = dot(dx1r, wo_ref[...], 1, 1).astype(BF)
        gwo_ref[...] = dot(o_ref[...], dx1r, 0, 0).astype(BF)
        sum_ref[4:5] = jnp.sum(dyf, axis=0, keepdims=True)
        sum_ref[5:6] = jnp.sum(dh * xhat, axis=0, keepdims=True)
        sum_ref[6:7] = jnp.sum(dh, axis=0, keepdims=True)
        sum_ref[7:8] = jnp.sum(dx1r.astype(F32), axis=0, keepdims=True)


def ffn(run, ids, x, o, cots, w_out, vecs, w_in, w_down, wins, chips):
    rows, d = x.shape
    ff = w_in.shape[1]
    tile = ff // wins
    sub = tile // chips
    cols = d // 2
    row = pl.BlockSpec((rows, d), lambda t, ids: (0, 0))
    square = pl.BlockSpec((d, d), lambda t, ids: (0, 0))
    keep = pl.BlockSpec((1, chips, sub, cols), lambda t, ids: (t, 0, 0, 0))
    keep_chips = pl.BlockSpec((chips, 1, sub, cols), lambda t, ids: (0, t, 0, 0))
    send = pl.BlockSpec((chips, sub, cols), lambda t, ids: (0, 0, 0))
    part = jax.ShapeDtypeStruct((wins, chips, sub, cols), BF)
    return run.call(
        functools.partial(ffn_kernel, wins=wins),
        (wins,),
        [row, row]
        + [pl.BlockSpec(cots[0].shape, lambda t, ids: (0, 0, 0))] * wins
        + [
            square,
            pl.BlockSpec(vecs.shape, lambda t, ids: (0, 0)),
            pl.BlockSpec((d, tile), lambda t, ids: (0, ids[t])),
            pl.BlockSpec((tile, d), lambda t, ids: (ids[t], 0)),
        ],
        [row, row, row, keep, keep_chips] + [send] * (2 * wins) + [square, pl.BlockSpec((16, d), lambda t, ids: (0, 0))],
        [
            jax.ShapeDtypeStruct((rows, d), BF),
            jax.ShapeDtypeStruct((rows, d), F32),
            jax.ShapeDtypeStruct((rows, d), BF),
            part,
            jax.ShapeDtypeStruct((chips, wins, sub, cols), BF),
        ]
        + [jax.ShapeDtypeStruct((chips, sub, cols), BF)] * (2 * wins)
        + [
            jax.ShapeDtypeStruct((d, d), BF),
            jax.ShapeDtypeStruct((16, d), F32),
        ],
        [
            pltpu.VMEM((rows, d), F32),
            pltpu.VMEM((rows, d), BF),
            pltpu.VMEM((d, rows), BF),
            pltpu.VMEM((rows, d), F32),
            pltpu.VMEM((rows, d), F32),
            pltpu.VMEM((rows, d), BF),
            pltpu.VMEM((tile, cols), BF),
        ],
        cost(14),
        "ffn",
        (x, o, *cots, w_out, vecs, w_in, w_down),
        ids=ids,
        mib=24,
    )


def attend_back_kernel(
    q_ref, o_ref, do_ref, k_ref, v_ref, bias_ref, lse_ref, dq_ref, dk_ref, dv_ref, dq_s
):
    step = pl.program_id(1)
    for pair in range(bias_ref.shape[0]):
        lanes = slice(pair * PW, (pair + 1) * PW)
        q2 = head_stack(q_ref[:, lanes])
        do = do_ref[:, lanes]
        do2 = head_stack(do)
        prod = head_stack(do.astype(F32) * o_ref[:, lanes].astype(F32))
        delta = dot(jnp.ones((8, PW), F32), prod, 1, 1, lax.Precision.HIGHEST)[0:1]
        k = k_ref[:, lanes]
        p = jnp.exp(biased_scores(k, q2, bias_ref[pair]) - lse_ref[0, pair])
        dp = dot(v_ref[:, lanes], do2, 1, 1)
        ds = (p * (dp - delta)).astype(BF)
        dv_ref[:, lanes] = dot(p.astype(BF), do2).astype(BF)
        dk_ref[:, lanes] = dot(ds, q2).astype(BF)
        dq_t = dot(k, ds, 0, 0)

        @pl.when(step == 0)
        def _():
            dq_s[pair] = dq_t

        @pl.when(step > 0)
        def _():
            dq_s[pair] += dq_t

        @pl.when(step == pl.num_programs(1) - 1)
        def _():
            dq_ref[:, lanes] = (head_select(dq_s[pair].T) * SCALE).astype(BF)


def attend_back(run, q, o, do, k, v, bias, lse, window, windows):
    rows, d = q.shape
    tok = rows // windows
    keys = k.shape[0]
    chunk = min(keys, 1024)
    parts = keys // chunk
    nkb = chunk // BS
    many = 2
    q_spec = pl.BlockSpec((tok, many * PW), lambda p, c: (window, p))
    k_spec = pl.BlockSpec((chunk, many * PW), lambda p, c: (c, p))
    return run.call(
        attend_back_kernel,
        (PAIRS // many, parts),
        [
            q_spec,
            q_spec,
            q_spec,
            k_spec,
            k_spec,
            pl.BlockSpec((many, nkb, 2 * tok), lambda p, c: (p, c, 0)),
            pl.BlockSpec((1, many, 1, 2 * tok), lambda p, c: (window, p, 0, 0)),
        ],
        [pl.BlockSpec((tok, many * PW), lambda p, c: (0, p)), k_spec, k_spec],
        [jax.ShapeDtypeStruct((tok, d), BF)] + [jax.ShapeDtypeStruct((keys, d), BF)] * 2,
        [pltpu.VMEM((many, PW, 2 * tok), F32)],
        cost(7.1),
        "attend_back",
        (q, o, do, k, v, bias, lse),
        mib=16,
    )


def token_back_kernel(a_ref, dk_ref, dv_ref, al_ref, dq_ref, wq_ref, wk_ref, wv_ref, keep_ref, send_ref, dal_ref, sum_ref):
    side = pl.program_id(0)

    @pl.when((side == 0) & (pl.program_id(1) == 0))
    def _():
        dq = dq_ref[...]
        dal = dot(dq, wq_ref[...], 1, 1)
        dal_ref[...] = dal
        sum_ref[0:1] = jnp.sum(dal * al_ref[...].astype(F32), axis=0, keepdims=True)
        sum_ref[1:2] = jnp.sum(dal, axis=0, keepdims=True)
        sum_ref[2:3] = jnp.sum(dq.astype(F32), axis=0, keepdims=True)
        sum_ref[3:8] = jnp.zeros((5, sum_ref.shape[1]), F32)

    dv = dv_ref[...]
    da = dot(dk_ref[...], wk_ref[...], 1, 1) + dot(dv, wv_ref[...], 1, 1)
    low = da.astype(BF).reshape(keep_ref.shape)

    @pl.when(side == 0)
    def _():
        keep_ref[...] = low

    @pl.when(side == 1)
    def _():
        send_ref[...] = low

    sum_ref[0:1] += jnp.sum(da * a_ref[0].astype(F32), axis=0, keepdims=True)
    sum_ref[1:2] += jnp.sum(da, axis=0, keepdims=True)
    sum_ref[3:4] += jnp.sum(dv.astype(F32), axis=0, keepdims=True)


def token_back(run, a, dk, dv, a_own, dq, w_qkv, tok, window):
    keys, d = dk.shape
    chips = keys // tok // 2
    size = min(chips, 4)
    half = chips // size
    tile = size * tok
    row = pl.BlockSpec((tile, d), lambda c, i: (c * half + i, 0))
    own_row = pl.BlockSpec((tok, d), lambda c, i: (0, 0))
    keep = pl.BlockSpec((size, tok, d), lambda c, i: (jnp.where(c == 0, i, half - 1), 0, 0))
    send = pl.BlockSpec((size, tok, d), lambda c, i: (jnp.where(c == 0, 0, i), 0, 0))
    part = jax.ShapeDtypeStruct((chips, tok, d), BF)
    return run.call(
        token_back_kernel,
        (2, half),
        [
            pl.BlockSpec((1, tile, d), lambda c, i: (window, c * half + i, 0)),
            row,
            row,
            pl.BlockSpec((tok, d), lambda c, i: (window, 0)),
            own_row,
            pl.BlockSpec((d, d), lambda c, i: (0, 0)),
            pl.BlockSpec((d, d), lambda c, i: (0, 1)),
            pl.BlockSpec((d, d), lambda c, i: (0, 2)),
        ],
        [keep, send, own_row, pl.BlockSpec((8, d), lambda c, i: (0, 0))],
        [part, part, jax.ShapeDtypeStruct((tok, d), F32), jax.ShapeDtypeStruct((8, d), F32)],
        [],
        cost(4.5),
        "token_back",
        (a, dk, dv, a_own, dq, w_qkv, w_qkv, w_qkv),
        mib=16,
    )


VECS = 16


def split_low(x):
    high = x.astype(BF)
    return high, (x - high.astype(F32)).astype(BF)


def qkv_grad_kernel(a_ref, al_ref, *refs):
    g_ref = refs[-1]
    windows = (len(refs) - 1) // 3
    dks, dvs, dqs = (refs[i * windows : (i + 1) * windows] for i in range(3))
    window = pl.program_id(0)
    tok = dqs[0].shape[0]

    @pl.when((window == 0) & (pl.program_id(1) == 0))
    def _():
        total = dot(al_ref[:tok], dqs[0][...], 0, 0)
        for w in range(1, windows):
            total = total + dot(al_ref[w * tok : (w + 1) * tok], dqs[w][...], 0, 0)
        g_ref[0] = total
        g_ref[1:] = jnp.zeros((2,) + g_ref.shape[1:], F32)

    a_t = a_ref[0].T
    dk, dv = dks[0][...], dvs[0][...]
    for w in range(1, windows):
        dk = jnp.where(window == w, dks[w][...], dk)
        dv = jnp.where(window == w, dvs[w][...], dv)
    g_ref[1] += dot(a_t, dk)
    g_ref[2] += dot(a_t, dv)


def qkv_grad(run, a, dks, dvs, a_own, dqs):
    windows, keys, d = a.shape
    tok = dqs[0].shape[0]
    tile = min(keys, 512)
    steps = keys // tile

    def rows_of(window):
        def where(w, i):
            return (jnp.where(w < window, 0, jnp.where(w > window, steps - 1, i)), 0)

        return pl.BlockSpec((tile, d), where)

    per_window = [rows_of(w) for w in range(windows)]
    [out] = run.call(
        qkv_grad_kernel,
        (windows, steps),
        [pl.BlockSpec((1, tile, d), lambda w, i: (w, i, 0)), pl.BlockSpec(a_own.shape, lambda w, i: (0, 0))]
        + per_window * 2
        + [pl.BlockSpec((tok, d), lambda w, i: (0, 0))] * windows,
        [pl.BlockSpec((3, d, d), lambda w, i: (0, 0, 0))],
        [jax.ShapeDtypeStruct((3, d, d), F32)],
        [],
        cost(7.5),
        "qkv_grad",
        (a, a_own, *dks, *dvs, *dqs),
        mib=14,
        mark=True,
    )
    return out


def pack_kernel(ids_ref, g_ref, gwo_ref, sum2_ref, *refs, wins, chips):
    sums, keep_ref, sends = refs[: -wins - 1], refs[-wins - 1], refs[-wins:]
    core = ids_ref[2 * wins]
    chip = ids_ref[2 * wins + 1]
    slots = wins * chips
    sub = (keep_ref.shape[0] - 2 * VECS) // slots
    per = wins // 2
    even = (g_ref[0], gwo_ref[...].astype(F32))
    odd = (g_ref[1], g_ref[2])
    for m in range(2):
        mine = jnp.where(core == 0, even[m], odd[m]).astype(BF)
        other = jnp.where(core == 0, odd[m], even[m]).astype(BF)
        for h in range(per):
            slot = ids_ref[wins + m * per + h]
            for q in range(chips):
                rows = slice((h * chips + q) * sub, (h * chips + q + 1) * sub)
                place = flip(q ^ chip, chips)
                keep_ref[pl.ds(pl.multiple_of((slot * chips + place) * sub, sub), sub)] = mine[rows]
                for to, ref in enumerate(sends):

                    @pl.when(flip(slot, wins) == to)
                    def _():
                        ref[pl.ds(pl.multiple_of(place * sub, sub), sub)] = other[rows]

    first = sums[0][0:4]
    for ref in sums[1:]:
        first = first + ref[0:4]
    high, rest = split_low(jnp.concatenate([first, sum2_ref[4:]]))
    for ref, at in ((keep_ref, slots * sub), (sends[-1], chips * sub)):
        ref[at : at + VECS] = high
        ref[at + VECS :] = rest


def pack(run, ids, g, g_out, sums1, sums2, wins, chips):
    d = g_out.shape[0]
    total = 2 * d + 2 * VECS
    size = 2 * d // wins
    shapes = [total] + [size] * (wins - 1) + [size + 2 * VECS]
    return run.call(
        functools.partial(pack_kernel, wins=wins, chips=chips),
        (1,),
        [
            pl.BlockSpec((3, d, d), lambda i, ids: (0, 0, 0)),
            pl.BlockSpec((d, d), lambda i, ids: (0, 0)),
            pl.BlockSpec((16, d), lambda i, ids: (0, 0)),
        ]
        + [pl.BlockSpec((8, d), lambda i, ids: (0, 0))] * len(sums1),
        [pl.BlockSpec((n, d), lambda i, ids: (0, 0)) for n in shapes],
        [jax.ShapeDtypeStruct((n, d), BF) for n in shapes],
        [],
        cost(2),
        "pack",
        (g, g_out, sums2, *sums1),
        ids=ids,
        mib=18,
    )


def fold_kernel(keep_ref, *refs):
    gots, (away_ref, keep_out_ref) = refs[:-2], refs[-2:]
    half = away_ref.shape[0]
    size = gots[0].shape[0]
    for i in range(0, 2 * half, min(size, half)):
        rows = min(size, half)
        got = gots[i // size][i % size : i % size + rows]
        value = (keep_ref[i : i + rows].astype(F32) + got.astype(F32)).astype(BF)
        if i < half:
            keep_out_ref[i : i + rows] = value
        else:
            away_ref[i - half : i - half + rows] = value


def fold(run, keep, gots):
    half = keep.shape[0] // 2
    whole = lambda part: pl.BlockSpec(part.shape, lambda i: (0,) * keep.ndim)
    out = jax.ShapeDtypeStruct((half,) + keep.shape[1:], BF)
    return run.call(
        fold_kernel,
        (1,),
        [whole(keep)] + [whole(got) for got in gots],
        [whole(out), whole(out)],
        [out, out],
        [],
        cost(0.5),
        "fold",
        (keep, *gots),
    )


def fold_windows_kernel(*refs):
    count = (len(refs) - 2) // 2
    away_ref, keep_ref = refs[-2:]
    half = away_ref.shape[0]
    for w in range(count):
        value = (refs[w][...].astype(F32) + refs[count + w][...].astype(F32)).astype(BF)
        rows = slice(w * value.shape[1], (w + 1) * value.shape[1])
        keep_ref[:, rows] = value[:half]
        away_ref[:, rows] = value[half:]


def fold_windows(run, keeps, gots):
    chips, tok, d = keeps[0].shape
    whole = pl.BlockSpec((chips, tok, d), lambda i: (0, 0, 0))
    shape = (chips // 2, len(keeps) * tok, d)
    return run.call(
        fold_windows_kernel,
        (1,),
        [whole] * (2 * len(keeps)),
        [pl.BlockSpec(shape, lambda i: (0, 0, 0))] * 2,
        [jax.ShapeDtypeStruct(shape, BF)] * 2,
        [],
        cost(0.5),
        "fold_windows",
        (*keeps, *gots),
        mib=12,
    )


def total_kernel(keep_ref, got_ref, out_ref):
    out_ref[...] = (keep_ref[...].astype(F32) + got_ref[...].astype(F32)).astype(BF)


def total(run, keep, got):
    spec = pl.BlockSpec(keep.shape, lambda i: (0,) * keep.ndim)
    [out] = run.call(
        total_kernel,
        (1,),
        [spec, spec],
        [spec],
        [jax.ShapeDtypeStruct(keep.shape, BF)],
        [],
        cost(0.2),
        "total",
        (keep, got),
    )
    return out


def add_vecs(keep_ref, gots):
    rows = keep_ref.shape[0] - 2 * VECS
    size = rows // len(gots)
    both = [keep_ref[i * size : (i + 1) * size].astype(F32) + got[:size].astype(F32) for i, got in enumerate(gots)]
    mine = keep_ref[rows : rows + VECS].astype(F32) + keep_ref[rows + VECS :].astype(F32)
    other = gots[-1][size : size + VECS].astype(F32) + gots[-1][size + VECS :].astype(F32)
    return both[0] if len(both) == 1 else jnp.concatenate(both), mine + other


def fold_vecs_kernel(keep_ref, *refs):
    gots, (away_out_ref, keep_out_ref) = refs[:-2], refs[-2:]
    both, sums = add_vecs(keep_ref, gots)
    cut = both.shape[0] // 2
    high, rest = split_low(sums)
    for ref, part in ((away_out_ref, both[cut:]), (keep_out_ref, both[:cut])):
        ref[:cut] = part.astype(BF)
        ref[cut : cut + VECS] = high
        ref[cut + VECS :] = rest


def last_vecs_kernel(keep_ref, got_ref, out_ref, sum_ref):
    both, sums = add_vecs(keep_ref, [got_ref])
    out_ref[...] = both.astype(BF)
    sum_ref[...] = sums


def fold_vecs(run, keep, gots, last):
    rows, d = keep.shape
    spec = pl.BlockSpec((rows, d), lambda i: (0, 0))
    body = rows - 2 * VECS
    if last:
        shapes = [((body, d), BF), ((VECS, d), F32)]
    else:
        shapes = [((body // 2 + 2 * VECS, d), BF)] * 2

    return run.call(
        last_vecs_kernel if last else fold_vecs_kernel,
        (1,),
        [spec] + [pl.BlockSpec(got.shape, lambda i: (0, 0)) for got in gots],
        [pl.BlockSpec(shape, lambda i: (0, 0)) for shape, _ in shapes],
        [jax.ShapeDtypeStruct(*shape) for shape in shapes],
        [],
        cost(0.6),
        "fold_vecs",
        (keep, *gots),
    )


def gather_kernel(*refs):
    size = refs[0].shape[0]
    for i, ref in enumerate(refs[:-1]):
        refs[-1][i * size : (i + 1) * size] = ref[...]


def gather_parts(run, parts):
    size, tok, d = parts[0].shape
    spec = pl.BlockSpec((size, tok, d), lambda i: (0, 0, 0))
    shape = (size * len(parts), tok, d)
    [out] = run.call(
        gather_kernel,
        (1,),
        [spec] * len(parts),
        [pl.BlockSpec(shape, lambda i: (0, 0, 0))],
        [jax.ShapeDtypeStruct(shape, BF)],
        [],
        cost(0.3),
        "gather_parts",
        parts,
    )
    return out


def input_back_kernel(x_ref, dx1_ref, vec_ref, keep_ref, got_ref, *refs):
    g_ref = refs[-1]
    tok = refs[0].shape[0]
    for w, own_ref in enumerate(refs[:-1]):
        rows = slice(w * tok, (w + 1) * tok)
        xhat, rstd = norm_stats(x_ref[rows].astype(F32))
        da = keep_ref[0, rows].astype(F32) + got_ref[0, rows].astype(F32) + own_ref[...]
        g_ref[rows] = (dx1_ref[rows] + norm_back(da * vec_ref[0:1], xhat, rstd)).astype(BF)


def input_back(run, x, dx1, vecs, keep, got, owns):
    rows, d = x.shape
    row = pl.BlockSpec((rows, d), lambda i: (0, 0))
    first = pl.BlockSpec((1, rows, d), lambda i: (0, 0, 0))
    [out] = run.call(
        input_back_kernel,
        (1,),
        [row, row, pl.BlockSpec(vecs.shape, lambda i: (0, 0)), first, first]
        + [pl.BlockSpec(own.shape, lambda i: (0, 0)) for own in owns],
        [row],
        [jax.ShapeDtypeStruct((rows, d), BF)],
        [],
        cost(1.4),
        "input_back",
        (x, dx1, vecs, keep, got, *owns),
        mark=True,
    )
    return out


def unpack_ffn_kernel(ids_ref, own_ref, got_ref, *refs, wins, chips, part, parts, start):
    down_ref, in_ref, down_s, in_s, sems = refs[-5:]
    even = ids_ref[2 * wins] == 0
    chip, win = ids_ref[2 * wins + 1], ids_ref[2 * wins + 2]
    count, sub, cols = own_ref.shape
    copies = []
    for k in range(count):
        slot, p = ((start + k) % wins, (start + k) // wins) if part else ((start + k) // chips, (start + k) % chips)
        own = own_ref[k].astype(F32)
        got = got_ref[k].astype(F32)
        down_s[k] = jnp.where(even, own, got)
        in_s[k] = jnp.where(even, got, own)
        row = (flip(p, chips) ^ chip) * sub
        down_row = pl.multiple_of((win ^ flip(slot, wins)) * (chips * sub) + row, sub)
        in_row = pl.multiple_of(row, sub)
        in_col = pl.multiple_of((win ^ slot) * (parts * cols) + part * cols, cols)
        for i, (src, dst) in enumerate(
            (
                (down_s, down_ref.at[pl.ds(down_row, sub), part * cols : (part + 1) * cols]),
                (in_s, in_ref.at[pl.ds(in_row, sub), pl.ds(in_col, cols)]),
            )
        ):
            copies.append(pltpu.make_async_copy(src.at[k], dst, sems.at[i, k]))
            copies[-1].start()
    for copy in copies:
        copy.wait()


def unpack_ffn(run, ids, own, got, chips, wins, part, parts, start, before):
    count, sub, cols = own.shape
    tile = chips * sub
    d = parts * cols
    whole = pl.BlockSpec(own.shape, lambda i, ids: (0, 0, 0))
    far = pl.BlockSpec(memory_space=pltpu.HBM)
    return run.call(
        functools.partial(unpack_ffn_kernel, wins=wins, chips=chips, part=part, parts=parts, start=start),
        (1,),
        [whole] * 2 + [far] * len(before),
        [far, far],
        [
            pltpu.HBM((wins * tile, d), F32),
            pltpu.HBM((d, wins * tile), F32),
        ],
        [
            pltpu.VMEM((count, sub, cols), F32),
            pltpu.VMEM((count, sub, cols), F32),
            pltpu.SemaphoreType.DMA((2, count)),
        ],
        cost(2.4),
        "unpack_ffn",
        (own, got, *before),
        ids=ids,
        alias={2: 0, 3: 1} if before else None,
        mib=14,
        mark=True,
    )


def unpack_qkvo_kernel(ids_ref, own_ref, got_ref, *refs, wins, chips, start):
    qkv_ref, out_ref, stage, sems = refs[-4:]
    even = ids_ref[2 * wins] == 0
    chip, win = ids_ref[2 * wins + 1], ids_ref[2 * wins + 2]
    count, sub, d = own_ref.shape
    per = wins // 2
    copies = []
    for k in range(count):
        slot, p = (start + k) // chips, (start + k) % chips
        own, got = own_ref[k].astype(F32), got_ref[k].astype(F32)
        for side in range(2):
            stage[k, side] = jnp.where(even, got, own) if side else jnp.where(even, own, got)
            tile = win ^ (slot if side else flip(slot, wins))
            row = ((tile % per) * chips + (flip(p, chips) ^ chip)) * sub
            rows = pl.ds(pl.multiple_of(row, sub), sub)
            high = qkv_ref.at[rows, 2 * d : 3 * d] if side else out_ref.at[rows]
            low = qkv_ref.at[rows, side * d : (side + 1) * d]
            for flag, dst in ((tile < per, low), (tile >= per, high)):
                copy = pltpu.make_async_copy(stage.at[k, side], dst, sems.at[k, side])
                copies.append((flag, copy))
                pl.when(flag)(copy.start)
    for flag, copy in copies:
        pl.when(flag)(copy.wait)


def unpack_qkvo(run, ids, own, got, chips, wins, start, before):
    count, sub, d = own.shape
    whole = pl.BlockSpec(own.shape, lambda i, ids: (0, 0, 0))
    far = pl.BlockSpec(memory_space=pltpu.HBM)
    return run.call(
        functools.partial(unpack_qkvo_kernel, wins=wins, chips=chips, start=start),
        (1,),
        [whole] * 2 + [far] * len(before),
        [far, far],
        [pltpu.HBM((d, 3 * d), F32), pltpu.HBM((d, d), F32)],
        [pltpu.VMEM((count, 2, sub, d), F32), pltpu.SemaphoreType.DMA((count, 2))],
        cost(2.4),
        "unpack_qkvo",
        (own, got, *before),
        ids=ids,
        alias={2: 0, 3: 1} if before else None,
        mib=14,
        mark=True,
    )


def copy_kernel(x_ref, out_ref):
    out_ref[...] = x_ref[...]


def copied(run, x):
    spec = pl.BlockSpec(x.shape, lambda i: (0,) * x.ndim)
    [out] = run.call(
        copy_kernel, (1,), [spec], [spec], [jax.ShapeDtypeStruct(x.shape, x.dtype)], [], cost(0.5), "copied", (x,)
    )
    return out


def place_kernel(ids_ref, species_ref, *refs, wins):
    out_ref = refs[-1]
    count = refs[0].shape[0]
    me = ids_ref[2 * wins + 2]
    out_ref[...] = jnp.zeros_like(out_ref)
    for s, ref in enumerate(refs[:-1]):
        for j in range(count):
            group, rank = slot_of(species_ref, (me ^ s) * count + j)

            @pl.when(group == me)
            def _():
                out_ref[jnp.minimum(rank, out_ref.shape[0] - 1)] = ref[j]


def place_rows(run, ids, species, parts, slots, wins):
    count, tok, d = parts[0].shape
    spec = pl.BlockSpec((count, tok, d), lambda i, *_: (0, 0, 0))
    [out] = run.call(
        functools.partial(place_kernel, wins=wins),
        (1,),
        [spec] * len(parts),
        [pl.BlockSpec((slots, tok, d), lambda i, *_: (0, 0, 0))],
        [jax.ShapeDtypeStruct((slots, tok, d), BF)],
        [],
        cost(1.7),
        "place_rows",
        parts,
        ids=(ids, species),
        mark=True,
    )
    return out


def swap(x, partner):
    wins, blks = lax.axis_size("win"), lax.axis_size("blk")
    perm = []
    for w in range(wins):
        for b in range(blks):
            pw, pb = partner(w, b)
            perm.append((w * blks + b, pw * blks + pb))
    return lax.ppermute(x, BOTH, perm)


def core_swap(x):
    return swap(x, lambda w, b: (w, b ^ 1))


def chip_swap(x, s):
    return swap(x, lambda w, b: (w, b ^ (2 * s)))


def win_swap(x, s):
    return swap(x, lambda w, b: (w ^ s, b))


def win_turns(wins):
    bits = (wins - 1).bit_length()
    even = [1 << i for i in range(bits)]
    return list(zip(even, even[::-1]))


def turn_swap(x, turn):
    even, odd = turn
    return swap(x, lambda w, b: (w ^ (odd if b % 2 else even), b))


def exchange_ids(wins, blks):
    rows = []
    for w in range(wins):
        for b in range(blks):
            core, chip = b % 2, b // 2
            tiles = [w ^ (i if core else flip(i, wins)) for i in range(wins)]
            rows.append(tiles + [tiles.index(t) for t in range(wins)] + [core, chip, w, b])
    me = lax.axis_index("win") * blks + lax.axis_index("blk")
    return lax.dynamic_index_in_dim(jnp.asarray(np.array(rows, np.int32)), me, 0, keepdims=False)


def stacked(rows, width):
    parts = []
    for row in rows:
        parts += [row[i : i + width] for i in range(0, row.shape[0], width)]
    count = -(-len(parts) // 8) * 8
    index = lax.broadcasted_iota(jnp.int32, (count, width), 0)
    out = jnp.zeros((count, width), F32)
    for r, part in enumerate(parts):
        out = jnp.where(index == r, part[None, :], out)
    return out


def turns(wins, chips):
    def chip_turn(s):
        return lambda x: chip_swap(x, s)

    out = [functools.partial(turn_swap, turn=turn) for turn in win_turns(wins)]
    bits = (chips - 1).bit_length()
    return out + [chip_turn(1 << i) for i in range(bits)]


class Sum:
    def __init__(self, run, keep, sends, swaps, chip_turns):
        self.run, self.keep, self.swaps, self.chip_turns = run, keep, swaps, chip_turns
        self.turn, self.x, self.unpacked = 0, None, 0
        self.got = [core_swap(send) for send in sends]

    def fold(self):
        return fold(self.run, self.keep, self.got)

    def total(self):
        return total(self.run, self.keep, self.got[0])

    def step(self):
        if self.x is None and self.turn < len(self.swaps):
            away, self.keep = self.fold()
            self.got = [self.swaps[self.turn](away)]
            self.turn += 1
            return
        if self.x is None:
            self.x, self.owns, self.gots = self.total(), [], []
        else:
            [arrived] = self.got
            if self.turn == 0:
                arrived = copied(self.run, arrived)
            if self.turn == 0:
                self.own(arrived)
            else:
                self.x = gather_parts(self.run, [self.x, arrived])
        self.turn -= 1
        if self.turn >= 0:
            self.got = [self.swaps[self.turn](self.x)]
        if self.turn == 0:
            self.own(self.x)

    def own(self, part):
        self.owns.append(part)
        self.gots.append(core_swap(part))


class TokenSum(Sum):
    def fold(self):
        return fold_windows(self.run, self.keep, self.got) if self.turn == 0 else fold(self.run, self.keep, self.got)


class VecSum(Sum):
    def fold(self):
        return fold_vecs(self.run, self.keep, self.got, False)

    def total(self):
        x, sums = fold_vecs(self.run, self.keep, self.got, True)
        self.sums = jnp.where(lax.axis_index("blk") % 2 == 0, sums, core_swap(sums))
        return x[None]


ORDER = (
    "b0", "0", "1", "bb", "t0", "tt", "0", "weight", "pack", "1", "0", "T", "Q", "0", "Q", "r", "0",
    "1", "Q", "T", "1", "1", "0", "Q", "uT", "place", "1", "0", "Q", "1", "0", "Q", "v", "Q", "0", "1",
    "Q", "u0", "u0", "u1", "uQ", "Q", "1", "uQ", "u1",
)


def schedule(more):
    steps = list(ORDER)
    for name in ("0", "1", "Q", "T") if more else ():
        places = [i for i, step in enumerate(steps) if step == name]
        if name in "01Q":
            steps[places[5] : places[5]] = [name] * more
            steps[places[3] : places[3]] = [name] * more
        else:
            steps[places[1] : places[1]] = [name] * more
    return steps


def per_device(
    inputs,
    species,
    random_blocks,
    qkv_weight,
    q_bias,
    v_bias,
    out_weight,
    out_bias,
    norm1_gain,
    norm1_bias,
    norm2_gain,
    norm2_bias,
    ffn_in_weight,
    ffn_in_bias,
    ffn_out_weight,
    ffn_out_bias,
    cotangent,
):
    count, tok, d = inputs.shape
    rows = count * tok
    wins, blks = lax.axis_size("win"), lax.axis_size("blk")
    chips = blks // 2
    ids = exchange_ids(wins, blks)
    run = Order()
    vecs = stacked(
        [norm1_gain, norm1_bias, q_bias, v_bias, out_bias, norm2_gain, norm2_bias, ffn_out_bias, ffn_in_bias], d
    )
    swaps = turns(wins, chips)
    chip_bits = [1 << i for i in range((chips - 1).bit_length())]

    first, *later = chip_bits[::-1]
    parts = [[row, chip_swap(row, first)] for row in (inputs[w : w + 1] for w in range(count))]
    x = inputs.reshape(rows, d)
    a_own, q, bias, *cots = query_rows(
        run, ids, species, random_blocks.transpose(2, 0, 1), x, vecs, qkv_weight, cotangent, count, wins, blks
    )
    cots = [cots[0]] + [win_swap(cots[s], s) for s in range(1, wins)]
    parts[0][1] = copied(run, parts[0][1])
    for s in later:
        parts = [window + [chip_swap(part, s) for part in window] for window in parts]
    mine = [gather_parts(run, parts[w]) for w in range(count)]
    theirs = [core_swap(part) for part in mine]
    keys, before, a = [], (), ()
    for w in range(count):
        a, k, v = kv_rows(run, mine[w], theirs[w], vecs, qkv_weight, w, count, a)
        a = (a,)
        keys.append((k, v))
        before = attend(run, q, k, v, bias, w, count, before)
    [a] = a
    o, lse = before
    y, dx1, do, keep0, keep1, *sends, g_out, sums2 = ffn(
        run, ids, x, o, cots, out_weight, vecs, ffn_in_weight, ffn_out_weight, wins, chips
    )
    slotted = lambda part: part.reshape(wins * chips, part.shape[2], part.shape[3])
    bits = len(chip_bits)
    f0 = Sum(run, slotted(keep0), sends[:wins], swaps, bits)
    f1 = Sum(run, slotted(keep1), sends[wins:], swaps[-bits:] + swaps[:-bits], bits)
    got = {"back": [], "t": []}

    def back(w):
        got["back"].append(attend_back(run, q, o, do, *keys[w], bias, lse, w, count))

    def token(w):
        dq, dk, dv = got["back"][w]
        got["t"].append(token_back(run, a, dk, dv, a_own, dq, qkv_weight, tok, w))
        if w == 0:
            got["T"] = TokenSum(run, [], [], swaps[-bits:], bits)
        part = got["T"]
        part.keep.append(got["t"][w][0])
        part.got.append(core_swap(got["t"][w][1]))

    def weight():
        dqs, dks, dvs = zip(*got["back"])
        got["g"] = qkv_grad(run, a, dks, dvs, a_own, dqs)

    def packed():
        keep, *sends = pack(run, ids, got["g"], g_out, [part[3] for part in got["t"]], sums2, wins, chips)
        got["Q"] = VecSum(run, keep, sends, swaps, bits)

    def send_result():
        own = copied(run, y.reshape(count, tok, d))
        got["y"] = [own] + [win_swap(own, s) for s in range(1, wins)]

    def place():
        got["result"] = place_rows(run, ids, species, got["y"], cotangent.shape[0], wins)

    def tokens_end():
        part, owns = got["T"], [part[2] for part in got["t"]]
        got["input"] = input_back(run, x, dx1, vecs, part.keep, part.got[0], owns).reshape(count, tok, d)

    def halves(piece):
        at = piece.unpacked
        piece.unpacked += 1
        return piece.owns[at], piece.gots[at], at * piece.owns[0].shape[0]

    def unpack(part, piece):
        own, arrived, start = halves(piece)
        got["ffn"] = unpack_ffn(run, ids, own, arrived, chips, wins, part, 2, start, got.get("ffn", ()))

    def vectors():
        sums = got["Q"].sums
        gain = (sums[0] - norm1_bias * sums[1]) / norm1_gain
        got["vectors"] = [gain] + [sums[i] for i in range(1, 8)] + [sums[8 : 8 + wins].reshape(-1)]
        run.touch(*got["vectors"])

    def unpack_last():
        own, arrived, start = halves(got["Q"])
        got["qkvo"] = unpack_qkvo(run, ids, own, arrived, chips, wins, start, got.get("qkvo", ()))

    todo = {
        "b0": lambda: back(0),
        "bb": lambda: [back(w) for w in range(1, count)],
        "t0": lambda: token(0),
        "tt": lambda: [token(w) for w in range(1, count)],
        "T": lambda: got["T"].step(),
        "r": send_result,
        "place": place,
        "weight": weight,
        "pack": packed,
        "0": f0.step,
        "1": f1.step,
        "Q": lambda: got["Q"].step(),
        "v": vectors,
        "u0": lambda: unpack(0, f0),
        "u1": lambda: unpack(1, f1),
        "uQ": unpack_last,
        "uT": tokens_end,
    }
    for name in schedule(len(swaps) - 4):
        todo[name]()
    ffn_out_grad, ffn_in_grad = got["ffn"]
    qkv_grad_all, out_grad = got["qkvo"]
    result, input_grad = got["result"], got["input"]
    gain1, shift1, q_grad, v_grad, down, gain2, shift2, out_bias_grad, hidden = got["vectors"]
    return (
        result,
        input_grad,
        qkv_grad_all,
        q_grad,
        v_grad,
        out_grad,
        out_bias_grad,
        gain1,
        shift1,
        gain2,
        shift2,
        ffn_in_grad,
        hidden,
        ffn_out_grad,
        down,
    )


def solution(mesh):
    split = P("win", "blk", None)
    return jax.shard_map(
        per_device,
        mesh=mesh,
        in_specs=(split,) + (P(),) * 15 + (split,),
        out_specs=(split, split) + (P(),) * 13,
        check_vma=False,
    )
```

```python
import functools

import jax
import jax.numpy as jnp
import numpy as np
from jax import lax
from jax.experimental import pallas as pl
from jax.experimental.pallas import tpu as pltpu
from jax.sharding import PartitionSpec as P

HEADS = 12
HD = 64
BS = 64
PAIRS = HEADS // 2
PW = 2 * HD

EPS = 1e-05
SCALE = 0.125
MASKED = -1e30
BF = jnp.bfloat16
F32 = jnp.float32
BOTH = ("win", "blk")
MIB = 1024 * 1024


def dot(a, b, ca=1, cb=0, precision=None):
    return lax.dot_general(
        a, b, (((ca,), (cb,)), ((), ())), precision=precision, preferred_element_type=F32
    )


def flip(i, size):
    bits = (size - 1).bit_length()
    out = 0
    for k in range(bits):
        out = out | (((i >> k) & 1) << (bits - 1 - k))
    return out


def params(grid_dims, mib):
    return pltpu.CompilerParams(
        dimension_semantics=("arbitrary",) * grid_dims, vmem_limit_bytes=mib * MIB
    )


def cost(us):
    return pl.CostEstimate(flops=1, bytes_accessed=int(us * 0.1 * 3.6e6), transcendentals=0)


def norm_stats(x):
    width = x.shape[-1]
    mean = jnp.sum(x, axis=-1, keepdims=True) * (1.0 / width)
    c = x - mean
    var = jnp.sum(c * c, axis=-1, keepdims=True) * (1.0 / width)
    rstd = lax.rsqrt(var + EPS)
    return c * rstd, rstd


def norm_back(g, xhat, rstd):
    width = g.shape[-1]
    m1 = jnp.sum(g, axis=-1, keepdims=True) * (1.0 / width)
    m2 = jnp.sum(g * xhat, axis=-1, keepdims=True) * (1.0 / width)
    return rstd * (g - m1 - xhat * m2)


class Order:
    def __init__(self):
        self.last = None
        self.touched = []

    def touch(self, *arrays):
        self.touched += arrays

    def call(
        self, kernel, grid, in_specs, out_specs, out_shape, scratch, estimate, name, args, ids=None, alias=None, mib=8, mark=False
    ):
        scalars = [] if ids is None else list(ids) if isinstance(ids, tuple) else [ids]
        after = [] if self.last is None or any(self.last is arg for arg in args) else [self.last]
        after += self.touched
        count, outs = len(scalars) + len(in_specs), len(out_specs)
        if mark:
            out_specs = list(out_specs) + [pl.BlockSpec((8, 128), lambda *_: (0, 0))]
            out_shape = list(out_shape) + [jax.ShapeDtypeStruct((8, 128), F32)]

        def body(*refs):
            at = count + len(after)
            if mark:
                refs[at + outs][...] = jnp.zeros((8, 128), F32)
            kernel(*refs[:count], *refs[at : at + outs], *refs[at + len(out_specs) :])

        out = pl.pallas_call(
            body,
            grid_spec=pltpu.PrefetchScalarGridSpec(
                num_scalar_prefetch=len(scalars),
                grid=grid,
                in_specs=list(in_specs) + [pl.BlockSpec(memory_space=pl.ANY)] * len(after),
                out_specs=out_specs,
                scratch_shapes=scratch,
            ),
            out_shape=out_shape,
            input_output_aliases={len(scalars) + i: o for i, o in (alias or {}).items()},
            compiler_params=params(len(grid), mib),
            cost_estimate=estimate,
            name=name,
        )(*scalars, *args, *after)
        self.last = min(out, key=lambda part: part.size * part.dtype.itemsize)
        self.touched = []
        return out[:outs]


def slot_of(species_ref, w):
    group = species_ref[w]
    rank = jnp.int32(0)
    for other in range(species_ref.shape[0]):
        rank = rank + ((species_ref[other] == group) & (other < w)).astype(jnp.int32)
    return group, rank


def query_kernel(
    ids_ref, species_ref, picks_ref, x_ref, vec_ref, w_ref, cot_ref, a_ref, q_ref, bias_ref, *part_refs, wins, blks
):
    count, tok, _ = part_refs[0].shape
    me, blk = ids_ref[2 * wins + 2], ids_ref[2 * wins + 3]
    for s, ref in enumerate(part_refs):
        for j in range(count):
            group, rank = slot_of(species_ref, (me ^ s) * count + j)
            here = group == me
            row = cot_ref[jnp.minimum(rank, cot_ref.shape[0] - 1)]
            ref[j] = jnp.where(here, row, jnp.zeros_like(row))

    xhat, _ = norm_stats(x_ref[...].astype(F32))
    a = (xhat * vec_ref[0:1] + vec_ref[1:2]).astype(BF)
    a_ref[...] = a
    q = (dot(a, w_ref[...]) + vec_ref[2:3]).astype(BF)
    q_ref[...] = (q.astype(F32) * SCALE).astype(BF)

    per, chips = tok // BS, blks // 2
    total = blks * per
    shape = bias_ref.shape[1:]
    place = lax.broadcasted_iota(jnp.int32, shape, 0)
    lane = lax.broadcasted_iota(jnp.int32, shape, 1)
    j = (lane % tok) // BS
    group = place // per
    owner = blk ^ (2 * flip(group % chips, chips) + group // chips)
    kb = owner * per + place % per
    i = blk * per + j
    one, zero = jnp.float32(1), jnp.float32(0)

    def hits(flag):
        return jnp.where(flag, one, zero)

    near = hits(kb == i - 1) + hits(kb == i) + hits(kb == i + 1)
    near = near + hits((kb == 0) & (i >= 2)) + hits((kb == total - 1) & (i <= total - 3))
    rand = picks_ref.shape[0]
    for pair in range(PAIRS):
        m = near
        for r in range(rand):
            picked = jnp.zeros(shape, jnp.int32)
            for h in range(2):
                for b in range(per):
                    value = picks_ref[r, blk * per + b, 2 * pair + h]
                    picked = jnp.where(lane // BS == h * per + b, value, picked)
            m = m + hits(picked == kb)
        m = jnp.where((i == 0) | (i == total - 1), one, m)
        bias_ref[pair] = jnp.where(m > 0, jnp.log(jnp.maximum(m, one)), MASKED)


def query_rows(run, ids, species, picks, x, vecs, w_qkv, cot, count, wins, blks):
    rows, d = x.shape
    slots, tok, _ = cot.shape
    row = pl.BlockSpec((rows, d), lambda i, *_: (0, 0))
    part = pl.BlockSpec((count, tok, d), lambda i, *_: (0, 0, 0))
    keys = (PAIRS, blks * (tok // BS), 2 * tok)
    return run.call(
        functools.partial(query_kernel, wins=wins, blks=blks),
        (1,),
        [
            row,
            pl.BlockSpec(vecs.shape, lambda i, *_: (0, 0)),
            pl.BlockSpec((d, d), lambda i, *_: (0, 0)),
            pl.BlockSpec((slots, tok, d), lambda i, *_: (0, 0, 0)),
        ],
        [row, row, pl.BlockSpec(keys, lambda i, *_: (0, 0, 0))] + [part] * wins,
        [jax.ShapeDtypeStruct((rows, d), BF)] * 2
        + [jax.ShapeDtypeStruct(keys, F32)]
        + [jax.ShapeDtypeStruct((count, tok, d), BF)] * wins,
        [],
        cost(1.7),
        "query_rows",
        (x, vecs, w_qkv, cot),
        ids=(ids, species, picks),
        mib=16,
    )


def kv_kernel(x0_ref, x1_ref, vec_ref, wk_ref, wv_ref, *refs):
    a_ref, k_ref, v_ref = refs[-3:]
    step, half = pl.program_id(0), pl.num_programs(0) // 2
    groups, tok, d = x0_ref.shape
    x = jnp.where(step < half, x0_ref[...], x1_ref[...]).reshape(groups * tok, d)
    xhat, _ = norm_stats(x.astype(F32))
    a = (xhat * vec_ref[0:1] + vec_ref[1:2]).astype(BF)
    a_ref[0] = a
    k_ref[...] = dot(a, wk_ref[...]).astype(BF)
    v_ref[...] = (dot(a, wv_ref[...]) + vec_ref[3:4]).astype(BF)


def kv_rows(run, mine, theirs, vecs, w_qkv, window, windows, before):
    chips, tok, d = mine.shape
    size = min(chips, 4)
    half = chips // size
    rows = 2 * chips * tok
    tile = size * tok
    row = pl.BlockSpec((tile, d), lambda i: (i, 0))
    return run.call(
        kv_kernel,
        (2 * half,),
        [
            pl.BlockSpec((size, tok, d), lambda i: (jnp.minimum(i, half - 1), 0, 0)),
            pl.BlockSpec((size, tok, d), lambda i: (jnp.maximum(i - half, 0), 0, 0)),
            pl.BlockSpec(vecs.shape, lambda i: (0, 0)),
            pl.BlockSpec((d, d), lambda i: (0, 1)),
            pl.BlockSpec((d, d), lambda i: (0, 2)),
        ]
        + [pl.BlockSpec(memory_space=pl.ANY)] * len(before),
        [pl.BlockSpec((1, tile, d), lambda i: (window, i, 0)), row, row],
        [jax.ShapeDtypeStruct((windows, rows, d), BF)] + [jax.ShapeDtypeStruct((rows, d), BF)] * 2,
        [],
        cost(3.7),
        "kv_rows",
        (mine, theirs, vecs, w_qkv, w_qkv, *before),
        alias={5: 0} if before else None,
        mib=14,
    )


def head_stack(pair):
    lane = lax.broadcasted_iota(jnp.int32, pair.shape, 1)
    zero = jnp.zeros_like(pair)
    return jnp.concatenate([jnp.where(lane < HD, pair, zero), jnp.where(lane < HD, zero, pair)], axis=0)


def head_select(both):
    rows = both.shape[0] // 2
    lane = lax.broadcasted_iota(jnp.int32, (rows, both.shape[1]), 1)
    return jnp.where(lane < HD, both[:rows], both[rows:])


def biased_scores(k, q2, bias):
    s = dot(k, q2, 1, 1)
    keys, lanes = s.shape
    return (s.reshape(keys // BS, BS, lanes) + bias[:, None, :]).reshape(keys, lanes)


def attend_kernel(q_ref, k_ref, v_ref, bias_ref, *refs):
    o_ref, lse_ref = refs[-2:]
    for pair in range(bias_ref.shape[0]):
        lanes = slice(pair * PW, (pair + 1) * PW)
        q2 = head_stack(q_ref[:, lanes])
        s = biased_scores(k_ref[:, lanes], q2, bias_ref[pair])
        top = jnp.max(s, axis=0, keepdims=True)
        e = jnp.exp(s - top)
        total = jnp.sum(e, axis=0, keepdims=True)
        o_t = dot(v_ref[:, lanes], e.astype(BF), 0, 0) * (1.0 / total)
        o_ref[:, lanes] = head_select(o_t.T).astype(BF)
        lse_ref[0, pair] = top + jnp.log(total)


def attend(run, q, k, v, bias, window, windows, before):
    rows, d = q.shape
    tok = rows // windows
    keys = k.shape[0]
    nkb = keys // BS
    many = 2 if keys <= 1024 else 1
    q_spec = pl.BlockSpec((tok, many * PW), lambda p: (window, p))
    k_spec = pl.BlockSpec((keys, many * PW), lambda p: (0, p))
    return run.call(
        attend_kernel,
        (PAIRS // many,),
        [q_spec, k_spec, k_spec, pl.BlockSpec((many, nkb, 2 * tok), lambda p: (p, 0, 0))]
        + [pl.BlockSpec(memory_space=pl.ANY)] * len(before),
        [q_spec, pl.BlockSpec((1, many, 1, 2 * tok), lambda p: (window, p, 0, 0))],
        [
            jax.ShapeDtypeStruct((rows, d), BF),
            jax.ShapeDtypeStruct((windows, PAIRS, 1, 2 * tok), F32),
        ],
        [],
        cost(6.6),
        "attend",
        (q, k, v, bias, *before),
        alias={4: 0, 5: 1} if before else None,
        mib=6 + keys // 256,
    )


def ffn_kernel(
    ids_ref,
    x_ref,
    o_ref,
    *refs,
    wins,
):
    ends = (wins, wins + 9, 3 * wins + 9)
    cots, head, sends, tail = (refs[a:b] for a, b in zip((0,) + ends, ends + (None,)))
    ffn_body(ids_ref, x_ref, o_ref, cots, *head, sends, *tail, wins=wins)


def ffn_body(
    ids_ref,
    x_ref,
    o_ref,
    cot_refs,
    wo_ref,
    vec_ref,
    wi_ref,
    wd_ref,
    y_ref,
    dx1_ref,
    do_ref,
    keep0_ref,
    keep1_ref,
    send_refs,
    gwo_ref,
    sum_ref,
    x1_s,
    h2_s,
    h2t_s,
    y_s,
    dh_s,
    dy_s,
    send_s,
    *,
    wins,
):
    step = pl.program_id(0)
    core = ids_ref[2 * wins]
    chip = ids_ref[2 * wins + 1]
    gain = vec_ref[5:6]

    @pl.when(step == 0)
    def _():
        x1 = x_ref[...].astype(F32) + (dot(o_ref[...], wo_ref[...]) + vec_ref[4:5])
        x1_s[...] = x1
        xhat, _ = norm_stats(x1)
        h2 = xhat * gain + vec_ref[6:7]
        h2_s[...] = h2.astype(BF)
        h2t_s[...] = h2.T.astype(BF)
        y_s[...] = jnp.zeros_like(y_s)
        dh_s[...] = jnp.zeros_like(dh_s)
        sum_ref[...] = jnp.zeros_like(sum_ref)
        total = cot_refs[0][...].astype(F32)
        for ref in cot_refs[1:]:
            total = total + ref[...].astype(F32)
        dy_s[...] = total.reshape(dy_s.shape).astype(BF)

    dy = dy_s[...]
    wi = wi_ref[...]
    wd = wd_ref[...]
    u = dot(h2_s[...], wi) + vec_ref[pl.ds(8 + ids_ref[step], 1)]
    half = 0.5 * (1.0 + lax.erf(u * 0.7071067811865476))
    f = (u * half).astype(BF)
    slope = half + u * (jnp.exp(u * u * -0.5) * 0.3989422804014327)
    du = dot(dy, wd, 1, 1) * slope
    du_low = du.astype(BF)
    y_s[...] += dot(f, wd)
    dh_s[...] += dot(du_low, wi, 1, 1)
    gd = dot(f, dy, 0, 0)
    gi = dot(h2t_s[...], du_low)
    keep = jnp.where(core == 0, gd, gi).astype(BF)
    send = jnp.where(core == 0, gi, gd).astype(BF)
    _, chips, sub, cols = keep0_ref.shape
    for q in range(chips):
        rows = slice(q * sub, (q + 1) * sub)
        keep0_ref[0, flip(q ^ chip, chips)] = keep[rows, :cols]
        keep1_ref[flip(q ^ chip, chips), 0] = keep[rows, cols:]
    send_s[...] = send[:, cols:]
    for p in range(chips):
        rows = pl.ds(pl.multiple_of((flip(p, chips) ^ chip) * sub, sub), sub)
        group = chips // wins
        send_refs[wins + p // group][p % group * wins + flip(step, wins)] = send_s[rows]
    for slot in range(wins):

        @pl.when(step == flip(slot, wins))
        def _():
            for q in range(chips):
                send_refs[slot][flip(q ^ chip, chips)] = send[q * sub : (q + 1) * sub, :cols]

    sum_ref[pl.ds(8 + ids_ref[step], 1)] = jnp.sum(du_low.astype(F32), axis=0, keepdims=True)

    @pl.when(step == pl.num_programs(0) - 1)
    def _():
        x1 = x1_s[...]
        y_ref[...] = (x1 + (y_s[...] + vec_ref[7:8])).astype(BF)
        dyf = dy.astype(F32)
        dh = dh_s[...]
        xhat, rstd = norm_stats(x1)
        dx1 = dyf + norm_back(dh * gain, xhat, rstd)
        dx1_ref[...] = dx1
        dx1r = dx1.astype(BF)
        do_ref[...] = dot(dx1r, wo_ref[...], 1, 1).astype(BF)
        gwo_ref[...] = dot(o_ref[...], dx1r, 0, 0).astype(BF)
        sum_ref[4:5] = jnp.sum(dyf, axis=0, keepdims=True)
        sum_ref[5:6] = jnp.sum(dh * xhat, axis=0, keepdims=True)
        sum_ref[6:7] = jnp.sum(dh, axis=0, keepdims=True)
        sum_ref[7:8] = jnp.sum(dx1r.astype(F32), axis=0, keepdims=True)


def ffn(run, ids, x, o, cots, w_out, vecs, w_in, w_down, wins, chips):
    rows, d = x.shape
    ff = w_in.shape[1]
    tile = ff // wins
    sub = tile // chips
    cols = d // 2
    row = pl.BlockSpec((rows, d), lambda t, ids: (0, 0))
    square = pl.BlockSpec((d, d), lambda t, ids: (0, 0))
    keep = pl.BlockSpec((1, chips, sub, cols), lambda t, ids: (t, 0, 0, 0))
    keep_chips = pl.BlockSpec((chips, 1, sub, cols), lambda t, ids: (0, t, 0, 0))
    send = pl.BlockSpec((chips, sub, cols), lambda t, ids: (0, 0, 0))
    part = jax.ShapeDtypeStruct((wins, chips, sub, cols), BF)
    return run.call(
        functools.partial(ffn_kernel, wins=wins),
        (wins,),
        [row, row]
        + [pl.BlockSpec(cots[0].shape, lambda t, ids: (0, 0, 0))] * wins
        + [
            square,
            pl.BlockSpec(vecs.shape, lambda t, ids: (0, 0)),
            pl.BlockSpec((d, tile), lambda t, ids: (0, ids[t])),
            pl.BlockSpec((tile, d), lambda t, ids: (ids[t], 0)),
        ],
        [row, row, row, keep, keep_chips] + [send] * (2 * wins) + [square, pl.BlockSpec((16, d), lambda t, ids: (0, 0))],
        [
            jax.ShapeDtypeStruct((rows, d), BF),
            jax.ShapeDtypeStruct((rows, d), F32),
            jax.ShapeDtypeStruct((rows, d), BF),
            part,
            jax.ShapeDtypeStruct((chips, wins, sub, cols), BF),
        ]
        + [jax.ShapeDtypeStruct((chips, sub, cols), BF)] * (2 * wins)
        + [
            jax.ShapeDtypeStruct((d, d), BF),
            jax.ShapeDtypeStruct((16, d), F32),
        ],
        [
            pltpu.VMEM((rows, d), F32),
            pltpu.VMEM((rows, d), BF),
            pltpu.VMEM((d, rows), BF),
            pltpu.VMEM((rows, d), F32),
            pltpu.VMEM((rows, d), F32),
            pltpu.VMEM((rows, d), BF),
            pltpu.VMEM((tile, cols), BF),
        ],
        cost(14),
        "ffn",
        (x, o, *cots, w_out, vecs, w_in, w_down),
        ids=ids,
        mib=24,
    )


def attend_back_kernel(
    q_ref, o_ref, do_ref, k_ref, v_ref, bias_ref, lse_ref, dq_ref, dk_ref, dv_ref, dq_s
):
    step = pl.program_id(1)
    for pair in range(bias_ref.shape[0]):
        lanes = slice(pair * PW, (pair + 1) * PW)
        q2 = head_stack(q_ref[:, lanes])
        do = do_ref[:, lanes]
        do2 = head_stack(do)
        prod = head_stack(do.astype(F32) * o_ref[:, lanes].astype(F32))
        delta = dot(jnp.ones((8, PW), F32), prod, 1, 1, lax.Precision.HIGHEST)[0:1]
        k = k_ref[:, lanes]
        p = jnp.exp(biased_scores(k, q2, bias_ref[pair]) - lse_ref[0, pair])
        dp = dot(v_ref[:, lanes], do2, 1, 1)
        ds = (p * (dp - delta)).astype(BF)
        dv_ref[:, lanes] = dot(p.astype(BF), do2).astype(BF)
        dk_ref[:, lanes] = dot(ds, q2).astype(BF)
        dq_t = dot(k, ds, 0, 0)

        @pl.when(step == 0)
        def _():
            dq_s[pair] = dq_t

        @pl.when(step > 0)
        def _():
            dq_s[pair] += dq_t

        @pl.when(step == pl.num_programs(1) - 1)
        def _():
            dq_ref[:, lanes] = (head_select(dq_s[pair].T) * SCALE).astype(BF)


def attend_back(run, q, o, do, k, v, bias, lse, window, windows):
    rows, d = q.shape
    tok = rows // windows
    keys = k.shape[0]
    chunk = min(keys, 1024)
    parts = keys // chunk
    nkb = chunk // BS
    many = 2
    q_spec = pl.BlockSpec((tok, many * PW), lambda p, c: (window, p))
    k_spec = pl.BlockSpec((chunk, many * PW), lambda p, c: (c, p))
    return run.call(
        attend_back_kernel,
        (PAIRS // many, parts),
        [
            q_spec,
            q_spec,
            q_spec,
            k_spec,
            k_spec,
            pl.BlockSpec((many, nkb, 2 * tok), lambda p, c: (p, c, 0)),
            pl.BlockSpec((1, many, 1, 2 * tok), lambda p, c: (window, p, 0, 0)),
        ],
        [pl.BlockSpec((tok, many * PW), lambda p, c: (0, p)), k_spec, k_spec],
        [jax.ShapeDtypeStruct((tok, d), BF)] + [jax.ShapeDtypeStruct((keys, d), BF)] * 2,
        [pltpu.VMEM((many, PW, 2 * tok), F32)],
        cost(7.1),
        "attend_back",
        (q, o, do, k, v, bias, lse),
        mib=16,
    )


def token_back_kernel(a_ref, dk_ref, dv_ref, al_ref, dq_ref, wq_ref, wk_ref, wv_ref, keep_ref, send_ref, dal_ref, sum_ref):
    side = pl.program_id(0)

    @pl.when((side == 0) & (pl.program_id(1) == 0))
    def _():
        dq = dq_ref[...]
        dal = dot(dq, wq_ref[...], 1, 1)
        dal_ref[...] = dal
        sum_ref[0:1] = jnp.sum(dal * al_ref[...].astype(F32), axis=0, keepdims=True)
        sum_ref[1:2] = jnp.sum(dal, axis=0, keepdims=True)
        sum_ref[2:3] = jnp.sum(dq.astype(F32), axis=0, keepdims=True)
        sum_ref[3:8] = jnp.zeros((5, sum_ref.shape[1]), F32)

    dv = dv_ref[...]
    da = dot(dk_ref[...], wk_ref[...], 1, 1) + dot(dv, wv_ref[...], 1, 1)
    low = da.astype(BF).reshape(keep_ref.shape)

    @pl.when(side == 0)
    def _():
        keep_ref[...] = low

    @pl.when(side == 1)
    def _():
        send_ref[...] = low

    sum_ref[0:1] += jnp.sum(da * a_ref[0].astype(F32), axis=0, keepdims=True)
    sum_ref[1:2] += jnp.sum(da, axis=0, keepdims=True)
    sum_ref[3:4] += jnp.sum(dv.astype(F32), axis=0, keepdims=True)


def token_back(run, a, dk, dv, a_own, dq, w_qkv, tok, window):
    keys, d = dk.shape
    chips = keys // tok // 2
    size = min(chips, 4)
    half = chips // size
    tile = size * tok
    row = pl.BlockSpec((tile, d), lambda c, i: (c * half + i, 0))
    own_row = pl.BlockSpec((tok, d), lambda c, i: (0, 0))
    keep = pl.BlockSpec((size, tok, d), lambda c, i: (jnp.where(c == 0, i, half - 1), 0, 0))
    send = pl.BlockSpec((size, tok, d), lambda c, i: (jnp.where(c == 0, 0, i), 0, 0))
    part = jax.ShapeDtypeStruct((chips, tok, d), BF)
    return run.call(
        token_back_kernel,
        (2, half),
        [
            pl.BlockSpec((1, tile, d), lambda c, i: (window, c * half + i, 0)),
            row,
            row,
            pl.BlockSpec((tok, d), lambda c, i: (window, 0)),
            own_row,
            pl.BlockSpec((d, d), lambda c, i: (0, 0)),
            pl.BlockSpec((d, d), lambda c, i: (0, 1)),
            pl.BlockSpec((d, d), lambda c, i: (0, 2)),
        ],
        [keep, send, own_row, pl.BlockSpec((8, d), lambda c, i: (0, 0))],
        [part, part, jax.ShapeDtypeStruct((tok, d), F32), jax.ShapeDtypeStruct((8, d), F32)],
        [],
        cost(4.5),
        "token_back",
        (a, dk, dv, a_own, dq, w_qkv, w_qkv, w_qkv),
        mib=16,
    )


VECS = 16


def split_low(x):
    high = x.astype(BF)
    return high, (x - high.astype(F32)).astype(BF)


def qkv_grad_kernel(a_ref, al_ref, *refs):
    g_ref = refs[-1]
    windows = (len(refs) - 1) // 3
    dks, dvs, dqs = (refs[i * windows : (i + 1) * windows] for i in range(3))
    window = pl.program_id(0)
    tok = dqs[0].shape[0]

    @pl.when((window == 0) & (pl.program_id(1) == 0))
    def _():
        total = dot(al_ref[:tok], dqs[0][...], 0, 0)
        for w in range(1, windows):
            total = total + dot(al_ref[w * tok : (w + 1) * tok], dqs[w][...], 0, 0)
        g_ref[0] = total
        g_ref[1:] = jnp.zeros((2,) + g_ref.shape[1:], F32)

    a_t = a_ref[0].T
    dk, dv = dks[0][...], dvs[0][...]
    for w in range(1, windows):
        dk = jnp.where(window == w, dks[w][...], dk)
        dv = jnp.where(window == w, dvs[w][...], dv)
    g_ref[1] += dot(a_t, dk)
    g_ref[2] += dot(a_t, dv)


def qkv_grad(run, a, dks, dvs, a_own, dqs):
    windows, keys, d = a.shape
    tok = dqs[0].shape[0]
    tile = min(keys, 512)
    steps = keys // tile

    def rows_of(window):
        def where(w, i):
            return (jnp.where(w < window, 0, jnp.where(w > window, steps - 1, i)), 0)

        return pl.BlockSpec((tile, d), where)

    per_window = [rows_of(w) for w in range(windows)]
    [out] = run.call(
        qkv_grad_kernel,
        (windows, steps),
        [pl.BlockSpec((1, tile, d), lambda w, i: (w, i, 0)), pl.BlockSpec(a_own.shape, lambda w, i: (0, 0))]
        + per_window * 2
        + [pl.BlockSpec((tok, d), lambda w, i: (0, 0))] * windows,
        [pl.BlockSpec((3, d, d), lambda w, i: (0, 0, 0))],
        [jax.ShapeDtypeStruct((3, d, d), F32)],
        [],
        cost(7.5),
        "qkv_grad",
        (a, a_own, *dks, *dvs, *dqs),
        mib=14,
        mark=True,
    )
    return out


def pack_kernel(ids_ref, g_ref, gwo_ref, sum2_ref, *refs, wins, chips):
    sums, keep_ref, sends = refs[: -wins - 1], refs[-wins - 1], refs[-wins:]
    core = ids_ref[2 * wins]
    chip = ids_ref[2 * wins + 1]
    slots = wins * chips
    sub = (keep_ref.shape[0] - 2 * VECS) // slots
    per = wins // 2
    even = (g_ref[0], gwo_ref[...].astype(F32))
    odd = (g_ref[1], g_ref[2])
    for m in range(2):
        mine = jnp.where(core == 0, even[m], odd[m]).astype(BF)
        other = jnp.where(core == 0, odd[m], even[m]).astype(BF)
        for h in range(per):
            slot = ids_ref[wins + m * per + h]
            for q in range(chips):
                rows = slice((h * chips + q) * sub, (h * chips + q + 1) * sub)
                place = flip(q ^ chip, chips)
                keep_ref[pl.ds(pl.multiple_of((slot * chips + place) * sub, sub), sub)] = mine[rows]
                for to, ref in enumerate(sends):

                    @pl.when(flip(slot, wins) == to)
                    def _():
                        ref[pl.ds(pl.multiple_of(place * sub, sub), sub)] = other[rows]

    first = sums[0][0:4]
    for ref in sums[1:]:
        first = first + ref[0:4]
    high, rest = split_low(jnp.concatenate([first, sum2_ref[4:]]))
    for ref, at in ((keep_ref, slots * sub), (sends[-1], chips * sub)):
        ref[at : at + VECS] = high
        ref[at + VECS :] = rest


def pack(run, ids, g, g_out, sums1, sums2, wins, chips):
    d = g_out.shape[0]
    total = 2 * d + 2 * VECS
    size = 2 * d // wins
    shapes = [total] + [size] * (wins - 1) + [size + 2 * VECS]
    return run.call(
        functools.partial(pack_kernel, wins=wins, chips=chips),
        (1,),
        [
            pl.BlockSpec((3, d, d), lambda i, ids: (0, 0, 0)),
            pl.BlockSpec((d, d), lambda i, ids: (0, 0)),
            pl.BlockSpec((16, d), lambda i, ids: (0, 0)),
        ]
        + [pl.BlockSpec((8, d), lambda i, ids: (0, 0))] * len(sums1),
        [pl.BlockSpec((n, d), lambda i, ids: (0, 0)) for n in shapes],
        [jax.ShapeDtypeStruct((n, d), BF) for n in shapes],
        [],
        cost(2),
        "pack",
        (g, g_out, sums2, *sums1),
        ids=ids,
        mib=18,
    )


def fold_kernel(keep_ref, *refs):
    gots, (away_ref, keep_out_ref) = refs[:-2], refs[-2:]
    half = away_ref.shape[0]
    size = gots[0].shape[0]
    for i in range(0, 2 * half, min(size, half)):
        rows = min(size, half)
        got = gots[i // size][i % size : i % size + rows]
        value = (keep_ref[i : i + rows].astype(F32) + got.astype(F32)).astype(BF)
        if i < half:
            keep_out_ref[i : i + rows] = value
        else:
            away_ref[i - half : i - half + rows] = value


def fold(run, keep, gots):
    half = keep.shape[0] // 2
    whole = lambda part: pl.BlockSpec(part.shape, lambda i: (0,) * keep.ndim)
    out = jax.ShapeDtypeStruct((half,) + keep.shape[1:], BF)
    return run.call(
        fold_kernel,
        (1,),
        [whole(keep)] + [whole(got) for got in gots],
        [whole(out), whole(out)],
        [out, out],
        [],
        cost(0.5),
        "fold",
        (keep, *gots),
    )


def fold_windows_kernel(*refs):
    count = (len(refs) - 2) // 2
    away_ref, keep_ref = refs[-2:]
    half = away_ref.shape[0]
    for w in range(count):
        value = (refs[w][...].astype(F32) + refs[count + w][...].astype(F32)).astype(BF)
        rows = slice(w * value.shape[1], (w + 1) * value.shape[1])
        keep_ref[:, rows] = value[:half]
        away_ref[:, rows] = value[half:]


def fold_windows(run, keeps, gots):
    chips, tok, d = keeps[0].shape
    whole = pl.BlockSpec((chips, tok, d), lambda i: (0, 0, 0))
    shape = (chips // 2, len(keeps) * tok, d)
    return run.call(
        fold_windows_kernel,
        (1,),
        [whole] * (2 * len(keeps)),
        [pl.BlockSpec(shape, lambda i: (0, 0, 0))] * 2,
        [jax.ShapeDtypeStruct(shape, BF)] * 2,
        [],
        cost(0.5),
        "fold_windows",
        (*keeps, *gots),
        mib=12,
    )


def total_kernel(keep_ref, got_ref, out_ref):
    out_ref[...] = (keep_ref[...].astype(F32) + got_ref[...].astype(F32)).astype(BF)


def total(run, keep, got):
    spec = pl.BlockSpec(keep.shape, lambda i: (0,) * keep.ndim)
    [out] = run.call(
        total_kernel,
        (1,),
        [spec, spec],
        [spec],
        [jax.ShapeDtypeStruct(keep.shape, BF)],
        [],
        cost(0.2),
        "total",
        (keep, got),
    )
    return out


def add_vecs(keep_ref, gots):
    rows = keep_ref.shape[0] - 2 * VECS
    size = rows // len(gots)
    both = [keep_ref[i * size : (i + 1) * size].astype(F32) + got[:size].astype(F32) for i, got in enumerate(gots)]
    mine = keep_ref[rows : rows + VECS].astype(F32) + keep_ref[rows + VECS :].astype(F32)
    other = gots[-1][size : size + VECS].astype(F32) + gots[-1][size + VECS :].astype(F32)
    return both[0] if len(both) == 1 else jnp.concatenate(both), mine + other


def fold_vecs_kernel(keep_ref, *refs):
    gots, (away_out_ref, keep_out_ref) = refs[:-2], refs[-2:]
    both, sums = add_vecs(keep_ref, gots)
    cut = both.shape[0] // 2
    high, rest = split_low(sums)
    for ref, part in ((away_out_ref, both[cut:]), (keep_out_ref, both[:cut])):
        ref[:cut] = part.astype(BF)
        ref[cut : cut + VECS] = high
        ref[cut + VECS :] = rest


def last_vecs_kernel(keep_ref, got_ref, out_ref, sum_ref):
    both, sums = add_vecs(keep_ref, [got_ref])
    out_ref[...] = both.astype(BF)
    sum_ref[...] = sums


def fold_vecs(run, keep, gots, last):
    rows, d = keep.shape
    spec = pl.BlockSpec((rows, d), lambda i: (0, 0))
    body = rows - 2 * VECS
    if last:
        shapes = [((body, d), BF), ((VECS, d), F32)]
    else:
        shapes = [((body // 2 + 2 * VECS, d), BF)] * 2

    return run.call(
        last_vecs_kernel if last else fold_vecs_kernel,
        (1,),
        [spec] + [pl.BlockSpec(got.shape, lambda i: (0, 0)) for got in gots],
        [pl.BlockSpec(shape, lambda i: (0, 0)) for shape, _ in shapes],
        [jax.ShapeDtypeStruct(*shape) for shape in shapes],
        [],
        cost(0.6),
        "fold_vecs",
        (keep, *gots),
    )


def gather_kernel(*refs):
    size = refs[0].shape[0]
    for i, ref in enumerate(refs[:-1]):
        refs[-1][i * size : (i + 1) * size] = ref[...]


def gather_parts(run, parts):
    size, tok, d = parts[0].shape
    spec = pl.BlockSpec((size, tok, d), lambda i: (0, 0, 0))
    shape = (size * len(parts), tok, d)
    [out] = run.call(
        gather_kernel,
        (1,),
        [spec] * len(parts),
        [pl.BlockSpec(shape, lambda i: (0, 0, 0))],
        [jax.ShapeDtypeStruct(shape, BF)],
        [],
        cost(0.3),
        "gather_parts",
        parts,
    )
    return out


def input_back_kernel(x_ref, dx1_ref, vec_ref, keep_ref, got_ref, *refs):
    g_ref = refs[-1]
    tok = refs[0].shape[0]
    for w, own_ref in enumerate(refs[:-1]):
        rows = slice(w * tok, (w + 1) * tok)
        xhat, rstd = norm_stats(x_ref[rows].astype(F32))
        da = keep_ref[0, rows].astype(F32) + got_ref[0, rows].astype(F32) + own_ref[...]
        g_ref[rows] = (dx1_ref[rows] + norm_back(da * vec_ref[0:1], xhat, rstd)).astype(BF)


def input_back(run, x, dx1, vecs, keep, got, owns):
    rows, d = x.shape
    row = pl.BlockSpec((rows, d), lambda i: (0, 0))
    first = pl.BlockSpec((1, rows, d), lambda i: (0, 0, 0))
    [out] = run.call(
        input_back_kernel,
        (1,),
        [row, row, pl.BlockSpec(vecs.shape, lambda i: (0, 0)), first, first]
        + [pl.BlockSpec(own.shape, lambda i: (0, 0)) for own in owns],
        [row],
        [jax.ShapeDtypeStruct((rows, d), BF)],
        [],
        cost(1.4),
        "input_back",
        (x, dx1, vecs, keep, got, *owns),
        mark=True,
    )
    return out


def unpack_ffn_kernel(ids_ref, own_ref, got_ref, *refs, wins, chips, part, parts, start):
    down_ref, in_ref, down_s, in_s, sems = refs[-5:]
    even = ids_ref[2 * wins] == 0
    chip, win = ids_ref[2 * wins + 1], ids_ref[2 * wins + 2]
    count, sub, cols = own_ref.shape
    copies = []
    for k in range(count):
        slot, p = ((start + k) % wins, (start + k) // wins) if part else ((start + k) // chips, (start + k) % chips)
        own = own_ref[k].astype(F32)
        got = got_ref[k].astype(F32)
        down_s[k] = jnp.where(even, own, got)
        in_s[k] = jnp.where(even, got, own)
        row = (flip(p, chips) ^ chip) * sub
        down_row = pl.multiple_of((win ^ flip(slot, wins)) * (chips * sub) + row, sub)
        in_row = pl.multiple_of(row, sub)
        in_col = pl.multiple_of((win ^ slot) * (parts * cols) + part * cols, cols)
        for i, (src, dst) in enumerate(
            (
                (down_s, down_ref.at[pl.ds(down_row, sub), part * cols : (part + 1) * cols]),
                (in_s, in_ref.at[pl.ds(in_row, sub), pl.ds(in_col, cols)]),
            )
        ):
            copies.append(pltpu.make_async_copy(src.at[k], dst, sems.at[i, k]))
            copies[-1].start()
    for copy in copies:
        copy.wait()


def unpack_ffn(run, ids, own, got, chips, wins, part, parts, start, before):
    count, sub, cols = own.shape
    tile = chips * sub
    d = parts * cols
    whole = pl.BlockSpec(own.shape, lambda i, ids: (0, 0, 0))
    far = pl.BlockSpec(memory_space=pltpu.HBM)
    return run.call(
        functools.partial(unpack_ffn_kernel, wins=wins, chips=chips, part=part, parts=parts, start=start),
        (1,),
        [whole] * 2 + [far] * len(before),
        [far, far],
        [
            pltpu.HBM((wins * tile, d), F32),
            pltpu.HBM((d, wins * tile), F32),
        ],
        [
            pltpu.VMEM((count, sub, cols), F32),
            pltpu.VMEM((count, sub, cols), F32),
            pltpu.SemaphoreType.DMA((2, count)),
        ],
        cost(2.4),
        "unpack_ffn",
        (own, got, *before),
        ids=ids,
        alias={2: 0, 3: 1} if before else None,
        mib=14,
        mark=True,
    )


def unpack_qkvo_kernel(ids_ref, own_ref, got_ref, *refs, wins, chips, start):
    qkv_ref, out_ref, stage, sems = refs[-4:]
    even = ids_ref[2 * wins] == 0
    chip, win = ids_ref[2 * wins + 1], ids_ref[2 * wins + 2]
    count, sub, d = own_ref.shape
    per = wins // 2
    copies = []
    for k in range(count):
        slot, p = (start + k) // chips, (start + k) % chips
        own, got = own_ref[k].astype(F32), got_ref[k].astype(F32)
        for side in range(2):
            stage[k, side] = jnp.where(even, got, own) if side else jnp.where(even, own, got)
            tile = win ^ (slot if side else flip(slot, wins))
            row = ((tile % per) * chips + (flip(p, chips) ^ chip)) * sub
            rows = pl.ds(pl.multiple_of(row, sub), sub)
            high = qkv_ref.at[rows, 2 * d : 3 * d] if side else out_ref.at[rows]
            low = qkv_ref.at[rows, side * d : (side + 1) * d]
            for flag, dst in ((tile < per, low), (tile >= per, high)):
                copy = pltpu.make_async_copy(stage.at[k, side], dst, sems.at[k, side])
                copies.append((flag, copy))
                pl.when(flag)(copy.start)
    for flag, copy in copies:
        pl.when(flag)(copy.wait)


def unpack_qkvo(run, ids, own, got, chips, wins, start, before):
    count, sub, d = own.shape
    whole = pl.BlockSpec(own.shape, lambda i, ids: (0, 0, 0))
    far = pl.BlockSpec(memory_space=pltpu.HBM)
    return run.call(
        functools.partial(unpack_qkvo_kernel, wins=wins, chips=chips, start=start),
        (1,),
        [whole] * 2 + [far] * len(before),
        [far, far],
        [pltpu.HBM((d, 3 * d), F32), pltpu.HBM((d, d), F32)],
        [pltpu.VMEM((count, 2, sub, d), F32), pltpu.SemaphoreType.DMA((count, 2))],
        cost(2.4),
        "unpack_qkvo",
        (own, got, *before),
        ids=ids,
        alias={2: 0, 3: 1} if before else None,
        mib=14,
        mark=True,
    )


def copy_kernel(x_ref, out_ref):
    out_ref[...] = x_ref[...]


def copied(run, x):
    spec = pl.BlockSpec(x.shape, lambda i: (0,) * x.ndim)
    [out] = run.call(
        copy_kernel, (1,), [spec], [spec], [jax.ShapeDtypeStruct(x.shape, x.dtype)], [], cost(0.5), "copied", (x,)
    )
    return out


def place_kernel(ids_ref, species_ref, *refs, wins):
    out_ref = refs[-1]
    count = refs[0].shape[0]
    me = ids_ref[2 * wins + 2]
    out_ref[...] = jnp.zeros_like(out_ref)
    for s, ref in enumerate(refs[:-1]):
        for j in range(count):
            group, rank = slot_of(species_ref, (me ^ s) * count + j)

            @pl.when(group == me)
            def _():
                out_ref[jnp.minimum(rank, out_ref.shape[0] - 1)] = ref[j]


def place_rows(run, ids, species, parts, slots, wins):
    count, tok, d = parts[0].shape
    spec = pl.BlockSpec((count, tok, d), lambda i, *_: (0, 0, 0))
    [out] = run.call(
        functools.partial(place_kernel, wins=wins),
        (1,),
        [spec] * len(parts),
        [pl.BlockSpec((slots, tok, d), lambda i, *_: (0, 0, 0))],
        [jax.ShapeDtypeStruct((slots, tok, d), BF)],
        [],
        cost(1.7),
        "place_rows",
        parts,
        ids=(ids, species),
        mark=True,
    )
    return out


def swap(x, partner):
    wins, blks = lax.axis_size("win"), lax.axis_size("blk")
    perm = []
    for w in range(wins):
        for b in range(blks):
            pw, pb = partner(w, b)
            perm.append((w * blks + b, pw * blks + pb))
    return lax.ppermute(x, BOTH, perm)


def core_swap(x):
    return swap(x, lambda w, b: (w, b ^ 1))


def chip_swap(x, s):
    return swap(x, lambda w, b: (w, b ^ (2 * s)))


def win_swap(x, s):
    return swap(x, lambda w, b: (w ^ s, b))


def win_turns(wins):
    bits = (wins - 1).bit_length()
    even = [1 << i for i in range(bits)]
    return list(zip(even, even[::-1]))


def turn_swap(x, turn):
    even, odd = turn
    return swap(x, lambda w, b: (w ^ (odd if b % 2 else even), b))


def exchange_ids(wins, blks):
    rows = []
    for w in range(wins):
        for b in range(blks):
            core, chip = b % 2, b // 2
            tiles = [w ^ (i if core else flip(i, wins)) for i in range(wins)]
            rows.append(tiles + [tiles.index(t) for t in range(wins)] + [core, chip, w, b])
    me = lax.axis_index("win") * blks + lax.axis_index("blk")
    return lax.dynamic_index_in_dim(jnp.asarray(np.array(rows, np.int32)), me, 0, keepdims=False)


def stacked(rows, width):
    parts = []
    for row in rows:
        parts += [row[i : i + width] for i in range(0, row.shape[0], width)]
    count = -(-len(parts) // 8) * 8
    index = lax.broadcasted_iota(jnp.int32, (count, width), 0)
    out = jnp.zeros((count, width), F32)
    for r, part in enumerate(parts):
        out = jnp.where(index == r, part[None, :], out)
    return out


def turns(wins, chips):
    def chip_turn(s):
        return lambda x: chip_swap(x, s)

    out = [functools.partial(turn_swap, turn=turn) for turn in win_turns(wins)]
    bits = (chips - 1).bit_length()
    return out + [chip_turn(1 << i) for i in range(bits)]


class Sum:
    def __init__(self, run, keep, sends, swaps, chip_turns):
        self.run, self.keep, self.swaps, self.chip_turns = run, keep, swaps, chip_turns
        self.turn, self.x, self.unpacked = 0, None, 0
        self.got = [core_swap(send) for send in sends]

    def fold(self):
        return fold(self.run, self.keep, self.got)

    def total(self):
        return total(self.run, self.keep, self.got[0])

    def step(self):
        if self.x is None and self.turn < len(self.swaps):
            away, self.keep = self.fold()
            self.got = [self.swaps[self.turn](away)]
            self.turn += 1
            return
        if self.x is None:
            self.x, self.owns, self.gots = self.total(), [], []
        else:
            [arrived] = self.got
            if self.turn == 0:
                arrived = copied(self.run, arrived)
            if self.turn == 0:
                self.own(arrived)
            else:
                self.x = gather_parts(self.run, [self.x, arrived])
        self.turn -= 1
        if self.turn >= 0:
            self.got = [self.swaps[self.turn](self.x)]
        if self.turn == 0:
            self.own(self.x)

    def own(self, part):
        self.owns.append(part)
        self.gots.append(core_swap(part))


class TokenSum(Sum):
    def fold(self):
        return fold_windows(self.run, self.keep, self.got) if self.turn == 0 else fold(self.run, self.keep, self.got)


class VecSum(Sum):
    def fold(self):
        return fold_vecs(self.run, self.keep, self.got, False)

    def total(self):
        x, sums = fold_vecs(self.run, self.keep, self.got, True)
        self.sums = jnp.where(lax.axis_index("blk") % 2 == 0, sums, core_swap(sums))
        return x[None]


ORDER = (
    "b0", "0", "1", "bb", "t0", "tt", "0", "weight", "pack", "1", "0", "T", "Q", "0", "Q", "r", "0",
    "1", "Q", "T", "1", "1", "0", "uT", "Q", "place", "1", "0", "Q", "1", "0", "Q", "v", "Q", "0", "u0",
    "1", "Q", "u0", "u1", "uQ", "Q", "1", "uQ", "u1",
)


def schedule(more):
    steps = list(ORDER)
    for name in ("0", "1", "Q", "T") if more else ():
        places = [i for i, step in enumerate(steps) if step == name]
        if name in "01Q":
            steps[places[5] : places[5]] = [name] * more
            steps[places[3] : places[3]] = [name] * more
        else:
            steps[places[1] : places[1]] = [name] * more
    return steps


def per_device(
    inputs,
    species,
    random_blocks,
    qkv_weight,
    q_bias,
    v_bias,
    out_weight,
    out_bias,
    norm1_gain,
    norm1_bias,
    norm2_gain,
    norm2_bias,
    ffn_in_weight,
    ffn_in_bias,
    ffn_out_weight,
    ffn_out_bias,
    cotangent,
):
    count, tok, d = inputs.shape
    rows = count * tok
    wins, blks = lax.axis_size("win"), lax.axis_size("blk")
    chips = blks // 2
    ids = exchange_ids(wins, blks)
    run = Order()
    vecs = stacked(
        [norm1_gain, norm1_bias, q_bias, v_bias, out_bias, norm2_gain, norm2_bias, ffn_out_bias, ffn_in_bias], d
    )
    swaps = turns(wins, chips)
    chip_bits = [1 << i for i in range((chips - 1).bit_length())]

    first, *later = chip_bits[::-1]
    parts = [[row, chip_swap(row, first)] for row in (inputs[w : w + 1] for w in range(count))]
    x = inputs.reshape(rows, d)
    a_own, q, bias, *cots = query_rows(
        run, ids, species, random_blocks.transpose(2, 0, 1), x, vecs, qkv_weight, cotangent, count, wins, blks
    )
    cots = [cots[0]] + [win_swap(cots[s], s) for s in range(1, wins)]
    for s in later:
        parts = [window + [chip_swap(part, s) for part in window] for window in parts]
    mine = [gather_parts(run, parts[w]) for w in range(count)]
    theirs = [core_swap(part) for part in mine]
    keys, before, a = [], (), ()
    for w in range(count):
        a, k, v = kv_rows(run, mine[w], theirs[w], vecs, qkv_weight, w, count, a)
        a = (a,)
        keys.append((k, v))
        before = attend(run, q, k, v, bias, w, count, before)
    [a] = a
    o, lse = before
    y, dx1, do, keep0, keep1, *sends, g_out, sums2 = ffn(
        run, ids, x, o, cots, out_weight, vecs, ffn_in_weight, ffn_out_weight, wins, chips
    )
    slotted = lambda part: part.reshape(wins * chips, part.shape[2], part.shape[3])
    bits = len(chip_bits)
    f0 = Sum(run, slotted(keep0), sends[:wins], swaps, bits)
    f1 = Sum(run, slotted(keep1), sends[wins:], swaps[-bits:] + swaps[:-bits], bits)
    got = {"back": [], "t": []}

    def back(w):
        got["back"].append(attend_back(run, q, o, do, *keys[w], bias, lse, w, count))

    def token(w):
        dq, dk, dv = got["back"][w]
        got["t"].append(token_back(run, a, dk, dv, a_own, dq, qkv_weight, tok, w))
        if w == 0:
            got["T"] = TokenSum(run, [], [], swaps[-bits:], bits)
        part = got["T"]
        part.keep.append(got["t"][w][0])
        part.got.append(core_swap(got["t"][w][1]))

    def weight():
        dqs, dks, dvs = zip(*got["back"])
        got["g"] = qkv_grad(run, a, dks, dvs, a_own, dqs)

    def packed():
        keep, *sends = pack(run, ids, got["g"], g_out, [part[3] for part in got["t"]], sums2, wins, chips)
        got["Q"] = VecSum(run, keep, sends, swaps, bits)

    def send_result():
        own = copied(run, y.reshape(count, tok, d))
        got["y"] = [own] + [win_swap(own, s) for s in range(1, wins)]

    def place():
        got["result"] = place_rows(run, ids, species, got["y"], cotangent.shape[0], wins)

    def tokens_end():
        part, owns = got["T"], [part[2] for part in got["t"]]
        got["input"] = input_back(run, x, dx1, vecs, part.keep, part.got[0], owns).reshape(count, tok, d)

    def halves(piece):
        at = piece.unpacked
        piece.unpacked += 1
        return piece.owns[at], piece.gots[at], at * piece.owns[0].shape[0]

    def unpack(part, piece):
        own, arrived, start = halves(piece)
        got["ffn"] = unpack_ffn(run, ids, own, arrived, chips, wins, part, 2, start, got.get("ffn", ()))

    def vectors():
        sums = got["Q"].sums
        gain = (sums[0] - norm1_bias * sums[1]) / norm1_gain
        got["vectors"] = [gain] + [sums[i] for i in range(1, 8)] + [sums[8 : 8 + wins].reshape(-1)]
        run.touch(*got["vectors"])

    def unpack_last():
        own, arrived, start = halves(got["Q"])
        got["qkvo"] = unpack_qkvo(run, ids, own, arrived, chips, wins, start, got.get("qkvo", ()))

    todo = {
        "b0": lambda: back(0),
        "bb": lambda: [back(w) for w in range(1, count)],
        "t0": lambda: token(0),
        "tt": lambda: [token(w) for w in range(1, count)],
        "T": lambda: got["T"].step(),
        "r": send_result,
        "place": place,
        "weight": weight,
        "pack": packed,
        "0": f0.step,
        "1": f1.step,
        "Q": lambda: got["Q"].step(),
        "v": vectors,
        "u0": lambda: unpack(0, f0),
        "u1": lambda: unpack(1, f1),
        "uQ": unpack_last,
        "uT": tokens_end,
    }
    for name in schedule(len(swaps) - 4):
        todo[name]()
    ffn_out_grad, ffn_in_grad = got["ffn"]
    qkv_grad_all, out_grad = got["qkvo"]
    result, input_grad = got["result"], got["input"]
    gain1, shift1, q_grad, v_grad, down, gain2, shift2, out_bias_grad, hidden = got["vectors"]
    return (
        result,
        input_grad,
        qkv_grad_all,
        q_grad,
        v_grad,
        out_grad,
        out_bias_grad,
        gain1,
        shift1,
        gain2,
        shift2,
        ffn_in_grad,
        hidden,
        ffn_out_grad,
        down,
    )


def solution(mesh):
    split = P("win", "blk", None)
    return jax.shard_map(
        per_device,
        mesh=mesh,
        in_specs=(split,) + (P(),) * 15 + (split,),
        out_specs=(split, split) + (P(),) * 13,
        check_vma=False,
    )
```
